128 devices in a mesh: img: 32 (over x, z, core), blk: 4 (over y).
Axes of the slice: x: 4, y: 4, z: 4, core: 2. Of those that a mesh axis runs over, the one named last changes fastest.
Arguments:
- params: float32 [59, 524288], P(None, ('img', 'blk')), may hold values from -7 to 5.3, as said below
- adam_first: float32 [59, 524288], P(None, ('img', 'blk')), may hold values from -2 to 2
- adam_second: float32 [59, 524288], P(None, ('img', 'blk')), may hold values from 0.001 to 1
- view_yaw: float32 [32], replicated, may hold values from -3.1416 to 3.1416
- tile_plan: int32 [2048], P(('img', 'blk')), may hold values from 0 to 261119, as said below
- tile_lists: int32 [2048, 256], P(('img', 'blk')), may hold values from 0 to 8191, as said below
- requests: int32 [128, 8192], P(('img', 'blk')), may hold values from 0 to 4095, as said below
- targets: float32 [3, 2048, 256], P(None, ('img', 'blk')), may hold values from 0 to 1
Outputs:
- new_params: float32 [59, 524288], P(None, ('img', 'blk'))
- new_first: float32 [59, 524288], P(None, ('img', 'blk'))
- new_second: float32 [59, 524288], P(None, ('img', 'blk'))
The draws below stay inside these ranges and needn't reach their ends.
Inputs may be any that keep to these rules, and one draw needn't show every extreme that they name: `requests`: row d holds, owner by owner, the 64 row numbers of that owner's Gaussians that device d receives, in the order of its slots; the rows one device asks of one owner are distinct; different devices may ask for the same rows. `tile_lists`: each entry names a slot s * 64 + j of the rendering device; a tile's 256 entries are in the order in which they are composited; on one device no slot is named twice, and on every device some owner has all 64 of its slots named. `tile_plan`: entry = v * 8160 + r * 120 + c for view v and the tile in tile row r and tile column c; no device renders one tile twice. `params`: row 0 and row 2 lie within [-5.3, 5.3], row 1 within [-2.8, 2.8], rows 3 to 5 within [-4.6, -3.4], row 6 within [0.6, 1.4], rows 7 to 9 within [-1, 1], row 10 within [-7, -2.5], rows 11 to 58 within [-2, 2].
All inputs are finite; a program needn't handle non-finite values.
Results may differ from the reference program's by a relative error of at most 0.0003.
Values sent between devices are 32-bit elements; how exact they have to be, the bound alone decides.
No kernel may reach another device: no remote copies, remote signals or barrier semaphores. Data moves between devices by JAX's collectives and lax.ppermute only.
A program may use at most 64 MiB of HBM per device.

```python
import math
from functools import partial
import jax
import jax.numpy as jnp
from jax import lax

PARAM = 59
GAUSS_DEV = 4096
TILES_DEV = 16
LIST = 256
VIEWS = 32
TILE_EDGE = 16
IMG_W = 1920
IMG_H = 1088
STEP = 1000
PIX = 256
TILES_ACROSS = 120
TILES_VIEW = 8160
CAP = 64
GAUSSIANS = 524288
TILES = 2048
DEVICES = 128


focal_px = 2400.0


camera_distance = 10.0


def permute_each(base, count_rows, length):
    subkeys = jax.random.split(base, count_rows)

    def one_perm(sub_key):
        return jax.random.permutation(sub_key, length).astype(jnp.int32)
    return jax.vmap(one_perm)(subkeys)


def layout(key):
    base = jax.random.fold_in(key, 71)
    keys_all = jax.random.split(base, 7)
    pool = TILES_DEV * LIST
    device_ids = jnp.arange(DEVICES, dtype=jnp.int32)
    hot_owner = jax.random.randint(keys_all[0], (DEVICES, 1), 0, DEVICES)
    hot_owner = hot_owner.at[0, 0].set(DEVICES - 1).at[1, 0].set(0)
    order = permute_each(keys_all[1], DEVICES, pool)
    spill = jnp.maximum(order - CAP, 0)
    spill_pick = permute_each(keys_all[5], DEVICES, (DEVICES - 1) * CAP)
    picked = jnp.take_along_axis(spill_pick, spill, axis=1)
    owner = jnp.where(order < CAP, hot_owner, (hot_owner + 1 + jnp.floor_divide(picked, CAP)) % DEVICES)
    slot_index = jnp.where(order < CAP, order, jnp.mod(picked, CAP))
    row_order = permute_each(keys_all[2], DEVICES, GAUSS_DEV)
    window_start = jax.random.randint(keys_all[6], (DEVICES, DEVICES), 0, GAUSS_DEV)
    places = (window_start[:, :, None] + jnp.arange(CAP, dtype=jnp.int32)[None, None, :]) % GAUSS_DEV
    wanted = row_order[device_ids[None, :, None], places]
    gaussian_row = wanted[device_ids[:, None], owner, slot_index]
    gauss_ids = owner * GAUSS_DEV + gaussian_row
    slot_ids = owner * CAP + slot_index
    device_view = device_ids % VIEWS
    rank_view = device_ids // VIEWS
    strides = jnp.array([7, 11, 13, 19, 23, 29, 31, 37, 41, 43], jnp.int32)
    stride_view = strides[jax.random.randint(keys_all[3], (VIEWS,), 0, 10)]
    offset_view = jax.random.randint(keys_all[4], (VIEWS,), 0, TILES_VIEW)
    offset_view = offset_view.at[VIEWS - 1].set(TILES_VIEW - 1).at[0].set(0)
    tile_ids = jnp.arange(TILES_DEV, dtype=jnp.int32)
    tiles = ((rank_view[:, None] * TILES_DEV + tile_ids[None, :]) * stride_view[device_view][:, None] + offset_view[device_view][:, None]) % TILES_VIEW
    return (wanted, slot_ids, gauss_ids, device_view, tiles)


def cameras(key):
    base = jax.random.fold_in(key, 83)
    first_key, second_key = jax.random.split(base)
    stratum = jax.random.permutation(first_key, VIEWS).astype(jnp.float32)
    jitter = jax.random.uniform(second_key, (VIEWS,), jnp.float32, 0.2, 0.8)
    return -3.1 + (stratum + jitter) * (6.2 / VIEWS)


def draw_view_yaw(key, part):
    view_yaw = cameras(key)
    key = jax.random.fold_in(key, 2)
    return view_yaw


def draw_requests(key, part):
    wanted, slot_ids, gauss_ids, device_view, tiles = layout(key)
    key = jax.random.fold_in(key, 3)
    return wanted.reshape(DEVICES, DEVICES * CAP)


def draw_tile_plan(key, part):
    wanted, slot_ids, gauss_ids, device_view, tiles = layout(key)
    key = jax.random.fold_in(key, 4)
    return (device_view[:, None] * TILES_VIEW + tiles).reshape(-1)


def draw_tile_lists(key, part):
    wanted, slot_ids, gauss_ids, device_view, tiles = layout(key)
    key = jax.random.fold_in(key, 6)
    return slot_ids.reshape(DEVICES * TILES_DEV, LIST)


def draw_params(key, part):
    wanted, slot_ids, gauss_ids, device_view, tiles = layout(key)
    view_yaw = cameras(key)
    key = jax.random.fold_in(key, 5)
    keys_all = jax.random.split(key, 10)
    pool = TILES_DEV * LIST
    total = GAUSS_DEV * DEVICES
    entry = jnp.arange(pool, dtype=jnp.int32)
    home_tile = tiles[:, entry // LIST]
    depth_rank = (entry % LIST).astype(jnp.float32)[None, :]
    pixel_x = (home_tile % TILES_ACROSS * TILE_EDGE).astype(jnp.float32) + TILE_EDGE * jax.random.uniform(keys_all[0], (DEVICES, pool), jnp.float32)
    pixel_y = (home_tile // TILES_ACROSS * TILE_EDGE).astype(jnp.float32) + TILE_EDGE * jax.random.uniform(keys_all[1], (DEVICES, pool), jnp.float32)
    depth = 8.0 + 4.0 * (depth_rank + jax.random.uniform(keys_all[2], (DEVICES, pool), jnp.float32)) / LIST
    yaw_home = view_yaw[device_view][:, None]
    cos_home = jnp.cos(yaw_home)
    sin_home = jnp.sin(yaw_home)
    ahead_x = depth * (pixel_x - 0.5 * IMG_W) / focal_px
    ahead_y = depth * (pixel_y - 0.5 * IMG_H) / focal_px
    ahead_z = depth - camera_distance
    home = jnp.stack([cos_home * ahead_x - sin_home * ahead_z, ahead_y, sin_home * ahead_x + cos_home * ahead_z]).reshape(3, -1)
    flat_ids = gauss_ids.reshape(-1)
    entry_all = jnp.arange(DEVICES * pool, dtype=jnp.int32)
    winner = jnp.full((total,), -1, jnp.int32).at[flat_ids].max(entry_all)
    has_home = winner >= 0
    home_at = jnp.take(home, jnp.maximum(winner, 0), axis=1)
    spread = jnp.array([3.6, 2.7, 3.6], jnp.float32)[:, None]
    position = spread * jax.random.uniform(keys_all[3], (3, total), jnp.float32, -1.0, 1.0)
    position = jnp.where(has_home[None, :], home_at, position)
    log_scale = jax.random.uniform(keys_all[4], (3, total), jnp.float32, -4.6, -3.4)
    quat_real = jax.random.uniform(keys_all[5], (1, total), jnp.float32, 0.6, 1.4)
    quat_imag = jax.random.uniform(keys_all[6], (3, total), jnp.float32, -1.0, 1.0)
    opacity_logit = jax.random.uniform(keys_all[7], (1, total), jnp.float32, -6.0, -2.5)
    color_zero = jnp.clip(0.6 * jax.random.normal(keys_all[8], (3, total), jnp.float32), -2.0, 2.0)
    color_rest = jnp.clip(0.4 * jax.random.normal(keys_all[9], (45, total), jnp.float32), -1.2, 1.2)
    return jnp.concatenate([position, log_scale, quat_real, quat_imag, opacity_logit, color_zero, color_rest], axis=0)


def shard_levels(stream_key, dims, shards, low, largest):
    def one(dim, blocks):
        heights = jax.random.uniform(jax.random.fold_in(jax.random.fold_in(stream_key, 6), dim), (blocks,), jnp.float32, low / len(shards), largest / len(shards))
        return jnp.repeat(jnp.exp(heights), dims[dim] // blocks).reshape((-1,) + (1,) * (len(dims) - dim - 1))

    gain = one(*shards[0])
    for cut in shards[1:]:
        gain = gain * one(*cut)
    return gain


def bell_draw(key, shape, deviation, most, cuts=(), kind=jnp.bfloat16):
    entries = jax.random.normal(key, shape, jnp.float32) * deviation
    if len(cuts) > 0:
        entries = shard_levels(key, shape, cuts, -0.22, 0.18) * entries
    return jnp.clip(entries, min=-most, max=most).astype(kind)


def setup_inputs(seed: int = 0) -> dict:
    arg_keys = jax.random.split(jax.random.key(seed), 9)
    params = draw_params(jax.random.fold_in(arg_keys[8], 71), 0)
    adam_first = bell_draw(arg_keys[1], (PARAM, GAUSSIANS), 0.3, 2.0, ((1, 128),), jnp.float32)
    adam_second = jnp.clip(jnp.exp(math.log(1.0) - 6.9077552 * jax.random.uniform(arg_keys[2], (PARAM, GAUSSIANS), jnp.float32) ** shard_levels(arg_keys[2], (PARAM, GAUSSIANS), ((1, 128),), -0.2, 0.2)), 0.001, 1.0)
    view_yaw = draw_view_yaw(jax.random.fold_in(arg_keys[8], 71), 0)
    tile_plan = draw_tile_plan(jax.random.fold_in(arg_keys[8], 71), 0)
    tile_lists = draw_tile_lists(jax.random.fold_in(arg_keys[8], 71), 0)
    requests = draw_requests(jax.random.fold_in(arg_keys[8], 71), 0)
    targets = jnp.clip(1.0 * jax.random.uniform(arg_keys[7], (3, TILES, PIX), jnp.float32) ** shard_levels(arg_keys[7], (3, TILES, PIX), ((1, 128),), -0.2, 0.2), 0.0, 1.0)
    return {"params": params, "adam_first": adam_first, "adam_second": adam_second, "view_yaw": view_yaw, "tile_plan": tile_plan, "tile_lists": tile_lists, "requests": requests, "targets": targets}


focal_px = 2400.0
camera_distance = 10.0
low_pass = 0.3
loss_scale = 16.0
beta_one = 0.9
beta_two = 0.999
adam_eps = 1e-08
band_zero = 0.28209479177387814
band_one = 0.4886025119029199
band_two = (1.0925484305920792, -1.0925484305920792, 0.31539156525252005, -1.0925484305920792, 0.5462742152960396)
band_three = (-0.5900435899266435, 2.890611442640554, -0.4570457994644658, 0.3731763325901154, -0.4570457994644658, 1.445305721320277, -0.5900435899266435)

def harmonics(looking_x, look_y, look_z):
    square_x = looking_x * looking_x
    square_y = look_y * look_y
    square_z = look_z * look_z
    return [jnp.full_like(looking_x, band_zero), -band_one * look_y, band_one * look_z, -band_one * looking_x, band_two[0] * looking_x * look_y, band_two[1] * look_y * look_z, band_two[2] * (2.0 * square_z - square_x - square_y), band_two[3] * looking_x * look_z, band_two[4] * (square_x - square_y), band_three[0] * look_y * (3.0 * square_x - square_y), band_three[1] * looking_x * look_y * look_z, band_three[2] * look_y * (4.0 * square_z - square_x - square_y), band_three[3] * look_z * (2.0 * square_z - 3.0 * square_x - 3.0 * square_y), band_three[4] * looking_x * (4.0 * square_z - square_x - square_y), band_three[5] * look_z * (square_x - square_y), band_three[6] * looking_x * (square_x - 3.0 * square_y)]

def running_sum(log_keep):
    return jnp.cumsum(log_keep, axis=1) - log_keep

def tile_loss(gauss_rows, tile_code, view_yaw, targets, exclusive):
    view_ids = tile_code // TILES_VIEW
    tile_num = tile_code % TILES_VIEW
    anchor_x = (tile_num % TILES_ACROSS * TILE_EDGE).astype(jnp.float32)
    anchor_y = (tile_num // TILES_ACROSS * TILE_EDGE).astype(jnp.float32)
    matches = view_ids[:, None] == jnp.arange(view_yaw.shape[0], dtype=jnp.int32)[None, :]
    yaw_angle = lax.optimization_barrier(jnp.sum(jnp.where(matches, view_yaw[None, :], jnp.zeros_like(view_yaw)[None, :]), axis=1))
    cos_yaw = jnp.cos(yaw_angle)[:, None]
    sin_yaw = jnp.sin(yaw_angle)[:, None]
    world_x = gauss_rows[0]
    world_y = gauss_rows[1]
    world_z = gauss_rows[2]
    view_x = cos_yaw * world_x + sin_yaw * world_z
    view_y = world_y
    view_z = cos_yaw * world_z - sin_yaw * world_x + camera_distance
    inverse_z = 1.0 / view_z
    mean_x = focal_px * view_x * inverse_z + 0.5 * IMG_W
    mean_y = focal_px * view_y * inverse_z + 0.5 * IMG_H
    scales = jnp.exp(gauss_rows[3:6])
    quaternion = gauss_rows[6:10]
    quaternion = quaternion / jnp.sqrt(lax.optimization_barrier(jnp.sum(quaternion * quaternion, axis=0)))
    quat_w = quaternion[0]
    quat_x = quaternion[1]
    quat_y = quaternion[2]
    quat_z = quaternion[3]
    rotation = [[1.0 - 2.0 * (quat_y * quat_y + quat_z * quat_z), 2.0 * (quat_x * quat_y - quat_w * quat_z), 2.0 * (quat_x * quat_z + quat_w * quat_y)], [2.0 * (quat_x * quat_y + quat_w * quat_z), 1.0 - 2.0 * (quat_x * quat_x + quat_z * quat_z), 2.0 * (quat_y * quat_z - quat_w * quat_x)], [2.0 * (quat_x * quat_z - quat_w * quat_y), 2.0 * (quat_y * quat_z + quat_w * quat_x), 1.0 - 2.0 * (quat_x * quat_x + quat_y * quat_y)]]
    factor = [[rotation[row_idx][col_idx] * scales[col_idx] for col_idx in range(3)] for row_idx in range(3)]
    world_cov = [[sum((factor[row_idx][inner_k] * factor[col_idx][inner_k] for inner_k in range(3))) for col_idx in range(3)] for row_idx in range(3)]
    focal_z = focal_px * inverse_z
    shear_x = focal_z * view_x * inverse_z
    shear_y = focal_z * view_y * inverse_z
    zero_row = jnp.zeros_like(view_x)
    jacob_a = [focal_z * cos_yaw + shear_x * sin_yaw, zero_row, focal_z * sin_yaw - shear_x * cos_yaw]
    jacob_b = [shear_y * sin_yaw, focal_z, -shear_y * cos_yaw]

    def project(first_vec, second_vec):
        return sum((first_vec[row_idx] * world_cov[row_idx][col_idx] * second_vec[col_idx] for row_idx in range(3) for col_idx in range(3)))
    covar_xx = project(jacob_a, jacob_a) + low_pass
    covar_yy = project(jacob_b, jacob_b) + low_pass
    covar_xy = project(jacob_a, jacob_b)
    determinant = covar_xx * covar_yy - covar_xy * covar_xy
    conic_a = covar_yy / determinant
    conic_b = -covar_xy / determinant
    conic_c = covar_xx / determinant
    opacity = jax.nn.sigmoid(gauss_rows[10])
    view_len = jnp.sqrt(view_x * view_x + view_y * view_y + view_z * view_z)
    looking_x = (cos_yaw * view_x - sin_yaw * view_z) / view_len
    look_y = view_y / view_len
    look_z = (sin_yaw * view_x + cos_yaw * view_z) / view_len
    basis = harmonics(looking_x, look_y, look_z)
    color_values = jnp.stack([jnp.maximum(0.5 + sum((basis[degree] * gauss_rows[11 + 3 * degree + channel] for degree in range(16))), 0.0) for channel in range(3)])
    pixels = jnp.arange(TILE_EDGE * TILE_EDGE, dtype=jnp.int32)
    pixel_x = anchor_x[:, None] + (pixels % TILE_EDGE).astype(jnp.float32)[None, :] + 0.5
    pixel_y = anchor_y[:, None] + (pixels // TILE_EDGE).astype(jnp.float32)[None, :] + 0.5
    delta_x = pixel_x[:, None, :] - mean_x[:, :, None]
    delta_y = pixel_y[:, None, :] - mean_y[:, :, None]
    exponent = -0.5 * (conic_a[:, :, None] * delta_x * delta_x + conic_c[:, :, None] * delta_y * delta_y) - conic_b[:, :, None] * delta_x * delta_y
    alpha_values = opacity[:, :, None] * jnp.exp(exponent)
    log_keep = jnp.log(1.0 - alpha_values)
    blend_weights = alpha_values * jnp.exp(exclusive(log_keep))
    rendered_image = jnp.einsum('ing,oin->oig', blend_weights, color_values, precision=lax.Precision.HIGHEST)
    residual = rendered_image - targets
    return 0.5 * jnp.sum(residual * residual) / loss_scale

def slot_loss(slot_rows, tile_lists, tile_plan, targets, view_yaw):
    gauss_rows = jnp.take(slot_rows, tile_lists.reshape(-1), axis=1).reshape(slot_rows.shape[0], tile_lists.shape[0], tile_lists.shape[1])
    return tile_loss(gauss_rows, tile_plan, view_yaw, targets, running_sum)

def rate_column(count_rows):
    pieces = [jnp.full((3,), 0.0008, jnp.float32), jnp.full((3,), 0.005, jnp.float32), jnp.full((4,), 0.001, jnp.float32), jnp.full((1,), 0.05, jnp.float32), jnp.full((3,), 0.0025, jnp.float32), jnp.full((count_rows - 14,), 0.000125, jnp.float32)]
    return jnp.concatenate(pieces)[:, None]

def adam_update(params, adam_first, adam_second, gradient):
    first_new = beta_one * adam_first + (1.0 - beta_one) * gradient
    second_new = beta_two * adam_second + (1.0 - beta_two) * gradient * gradient
    bias_one = 1.0 - beta_one ** STEP
    bias_two = 1.0 - beta_two ** STEP
    params_new = params - rate_column(params.shape[0]) * (first_new / bias_one) / (jnp.sqrt(second_new / bias_two) + adam_eps)
    return (params_new, first_new, second_new)

def reference(params, adam_first, adam_second, view_yaw, tile_plan, tile_lists, requests, targets):
    wants_all = requests.reshape(DEVICES, DEVICES, CAP)
    owner_base = (jnp.arange(DEVICES, dtype=jnp.int32) * GAUSS_DEV).astype(jnp.int32)
    global_all = (wants_all + owner_base[None, :, None]).astype(jnp.int32)
    lists_all = tile_lists.reshape(DEVICES, TILES_DEV, LIST)
    codes_all = tile_plan.reshape(DEVICES, TILES_DEV)
    target_all = jnp.transpose(targets.reshape(3, DEVICES, TILES_DEV, PIX), (1, 0, 2, 3))

    def one_device(packed):
        global_ids, list_block, code_block, target_block = packed
        slot_rows = jnp.take(params, global_ids.reshape(-1), axis=1)
        loss_fn = partial(slot_loss, tile_lists=list_block, tile_plan=code_block, targets=target_block, view_yaw=view_yaw)
        return jax.grad(loss_fn)(slot_rows)
    slot_grads = lax.map(one_device, (global_all, lists_all, codes_all, target_all))
    flat_grads = jnp.transpose(slot_grads, (1, 0, 2)).reshape(PARAM, -1)
    gradient = jnp.zeros((PARAM, GAUSSIANS), jnp.float32).at[:, global_all.reshape(-1)].add(flat_grads)
    return adam_update(params, adam_first, adam_second, gradient)
```

```python
from functools import partial

import jax
import jax.numpy as jnp
from jax import lax
from jax.experimental import pallas as pl
from jax.experimental.pallas import tpu as pltpu
from jax.sharding import PartitionSpec as P

AXES = ("img", "blk")
STEP = 1000
TILES_ACROSS = 120
TILES_VIEW = 8160
TILE_EDGE = 16
PARAM = 59
OWN = 4096
SLOTS = 8192
TILES = 16
LIST = 256
PIX = 256
SENT = 9
LINES = 5

focal_px = 2400.0
camera_distance = 10.0
low_pass = 0.3
loss_scale = 16.0
beta_one = 0.9
beta_two = 0.999
adam_eps = 1e-08
band_zero = 0.28209479177387814
band_one = 0.4886025119029199
band_two = (
    1.0925484305920792,
    -1.0925484305920792,
    0.31539156525252005,
    -1.0925484305920792,
    0.5462742152960396,
)
band_three = (
    -0.5900435899266435,
    2.890611442640554,
    -0.4570457994644658,
    0.3731763325901154,
    -0.4570457994644658,
    1.445305721320277,
    -0.5900435899266435,
)
f32 = jnp.float32
bf16 = jnp.bfloat16
i32 = jnp.int32
VM = pl.BlockSpec(memory_space=pltpu.VMEM)
SM = pl.BlockSpec(memory_space=pltpu.SMEM)


def iota(shape, dim):
    return lax.broadcasted_iota(i32, shape, dim)


def dot(a, b):
    return lax.dot_general(a, b, (((1,), (0,)), ((), ())), preferred_element_type=f32)


def dot_t(a, b):
    return lax.dot_general(a, b, (((1,), (1,)), ((), ())), preferred_element_type=f32)


def pieces(x, count):
    out = []
    for k in range(count):
        part = x.astype(bf16)
        out.append(part)
        if k + 1 < count:
            x = x - part.astype(f32)
    return out


def call(kernel, out_shape, name, scratch=(), in_specs=None, flops=0):
    return partial(
        pl.pallas_call,
        kernel,
        out_shape=out_shape,
        in_specs=in_specs,
        out_specs=jax.tree.map(lambda _: VM, out_shape),
        scratch_shapes=list(scratch),
        name=name,
        cost_estimate=pl.CostEstimate(flops=flops, bytes_accessed=4 << 20, transcendentals=0),
        compiler_params=pltpu.CompilerParams(vmem_limit_bytes=40 << 20),
    )()


def harmonics(looking_x, look_y, look_z):
    square_x = looking_x * looking_x
    square_y = look_y * look_y
    square_z = look_z * look_z
    return [
        jnp.full_like(looking_x, band_zero),
        -band_one * look_y,
        band_one * look_z,
        -band_one * looking_x,
        band_two[0] * looking_x * look_y,
        band_two[1] * look_y * look_z,
        band_two[2] * (2.0 * square_z - square_x - square_y),
        band_two[3] * looking_x * look_z,
        band_two[4] * (square_x - square_y),
        band_three[0] * look_y * (3.0 * square_x - square_y),
        band_three[1] * looking_x * look_y * look_z,
        band_three[2] * look_y * (4.0 * square_z - square_x - square_y),
        band_three[3] * look_z * (2.0 * square_z - 3.0 * square_x - 3.0 * square_y),
        band_three[4] * looking_x * (4.0 * square_z - square_x - square_y),
        band_three[5] * look_z * (square_x - square_y),
        band_three[6] * looking_x * (square_x - 3.0 * square_y),
    ]


def project_slots(rows, cos_yaw, sin_yaw, centre_x, centre_y):
    world_x, world_y, world_z = rows[0], rows[1], rows[2]
    view_x = cos_yaw * world_x + sin_yaw * world_z
    view_z = cos_yaw * world_z - sin_yaw * world_x + camera_distance
    inverse_z = 1.0 / view_z
    mean_x = focal_px * view_x * inverse_z - centre_x
    mean_y = focal_px * world_y * inverse_z - centre_y
    scales = [jnp.exp(rows[3 + k]) for k in range(3)]
    norm = jnp.sqrt(
        rows[6] * rows[6] + rows[7] * rows[7] + rows[8] * rows[8] + rows[9] * rows[9]
    )
    inverse_norm = 1.0 / norm
    quat_w, quat_x, quat_y, quat_z = [rows[6 + k] * inverse_norm for k in range(4)]
    rotation = [
        [
            1.0 - 2.0 * (quat_y * quat_y + quat_z * quat_z),
            2.0 * (quat_x * quat_y - quat_w * quat_z),
            2.0 * (quat_x * quat_z + quat_w * quat_y),
        ],
        [
            2.0 * (quat_x * quat_y + quat_w * quat_z),
            1.0 - 2.0 * (quat_x * quat_x + quat_z * quat_z),
            2.0 * (quat_y * quat_z - quat_w * quat_x),
        ],
        [
            2.0 * (quat_x * quat_z - quat_w * quat_y),
            2.0 * (quat_y * quat_z + quat_w * quat_x),
            1.0 - 2.0 * (quat_x * quat_x + quat_y * quat_y),
        ],
    ]
    focal_z = focal_px * inverse_z
    shear_x = focal_z * view_x * inverse_z
    shear_y = focal_z * world_y * inverse_z
    jacob_ax = focal_z * cos_yaw + shear_x * sin_yaw
    jacob_az = focal_z * sin_yaw - shear_x * cos_yaw
    jacob_bx = shear_y * sin_yaw
    jacob_bz = -shear_y * cos_yaw
    row_a = [
        (jacob_ax * rotation[0][k] + jacob_az * rotation[2][k]) * scales[k] for k in range(3)
    ]
    row_b = [
        (jacob_bx * rotation[0][k] + focal_z * rotation[1][k] + jacob_bz * rotation[2][k])
        * scales[k]
        for k in range(3)
    ]
    covar_xx = row_a[0] * row_a[0] + row_a[1] * row_a[1] + row_a[2] * row_a[2] + low_pass
    covar_yy = row_b[0] * row_b[0] + row_b[1] * row_b[1] + row_b[2] * row_b[2] + low_pass
    covar_xy = row_a[0] * row_b[0] + row_a[1] * row_b[1] + row_a[2] * row_b[2]
    inverse_det = 1.0 / (covar_xx * covar_yy - covar_xy * covar_xy)
    conic_a = covar_yy * inverse_det
    conic_b = -covar_xy * inverse_det
    conic_c = covar_xx * inverse_det
    log_opacity = rows[10] - jnp.log(1.0 + jnp.exp(rows[10]))
    slope_x = conic_a * mean_x + conic_b * mean_y
    slope_y = conic_c * mean_y + conic_b * mean_x
    constant = log_opacity - 0.5 * (slope_x * mean_x + slope_y * mean_y)
    inverse_len = 1.0 / jnp.sqrt(view_x * view_x + world_y * world_y + view_z * view_z)
    basis = harmonics(
        (cos_yaw * view_x - sin_yaw * view_z) * inverse_len,
        world_y * inverse_len,
        (sin_yaw * view_x + cos_yaw * view_z) * inverse_len,
    )
    colors = []
    for channel in range(3):
        total = basis[0] * rows[11 + channel]
        for degree in range(1, 16):
            total = total + basis[degree] * rows[11 + 3 * degree + channel]
        colors.append(jnp.maximum(0.5 + total, 0.0))
    return [
        constant,
        slope_x,
        slope_y,
        -0.5 * conic_a,
        -conic_b,
        -0.5 * conic_c,
    ] + colors


def camera_of(codes, cos_ref, sin_ref):
    code = codes.astype(f32)
    view = jnp.floor((code + 0.5) * (1.0 / TILES_VIEW))
    number = code - view * float(TILES_VIEW)
    across = jnp.floor((number + 0.5) * (1.0 / TILES_ACROSS))
    column = number - across * float(TILES_ACROSS)
    view = view.astype(i32)
    cos_yaw = jnp.take_along_axis(cos_ref[...], view, axis=1, mode="promise_in_bounds")
    sin_yaw = jnp.take_along_axis(sin_ref[...], view, axis=1, mode="promise_in_bounds")
    centre_x = column * 16.0 + (8.0 - 960.0)
    centre_y = across * 16.0 + (8.0 - 544.0)
    return cos_yaw, sin_yaw, centre_x, centre_y


def slot_parts(slot):
    line = jnp.right_shift(slot, 7)
    high = jnp.bitwise_and(line, 31)
    low = jnp.right_shift(line, 5) * 128 + jnp.bitwise_and(slot, 127)
    return high, low


def ask_kernel(plan_ref, lists_ref, req_ref, out_ref):
    total = jnp.zeros((32, 256), f32)
    for t in range(TILES):
        high, low = slot_parts(lists_ref[t : t + 1, :])
        hot = (iota((256, LIST), 0) == low).astype(f32).astype(bf16)
        left = jnp.where(iota((32, LIST), 0) == high, float(t + 1), 0.0).astype(bf16)
        total = total + dot_t(left, hot)
    codes = jnp.zeros((32, 256), i32)
    for t in range(TILES):
        codes = jnp.where(total == float(t + 1), plan_ref[t], codes)
    codes = jnp.concatenate([codes[:, :128], codes[:, 128:]], axis=0)
    asked = req_ref[...]
    first = iota((64, 128), 1) < 64
    out_ref[pl.ds(0, 64, stride=2), :] = jnp.where(first, asked, pltpu.roll(codes, 64, 1))
    out_ref[pl.ds(1, 64, stride=2), :] = jnp.where(first, pltpu.roll(asked, 64, 1), codes)


def table_kernel(params_ref, out_ref):
    for h in range(16):
        cols = pl.ds(h * 256, 256)
        top, mid, rest = pieces(params_ref[:, cols], 3)
        shifted = pltpu.roll(rest[0:16].astype(f32)[0:8], 3, 0)
        last = top.astype(f32)[56:64]
        last = jnp.where(iota((8, 256), 0) < 3, last, shifted)
        top = jnp.concatenate([top.astype(f32)[:56], last], axis=0).astype(bf16)
        out_ref[pl.ds(h * 128, 64), :] = top
        out_ref[pl.ds(h * 128 + 64, 64), :] = mid


def answer_kernel(came_ref, table_ref, cos_ref, sin_ref, out_ref, slots_ref, rows_ref, codes_ref, wide):
    even = came_ref[pl.ds(0, 64, stride=2), :]
    odd = came_ref[pl.ds(1, 64, stride=2), :]
    first = iota((64, 128), 1) < 64
    rows_ref[...] = jnp.where(first, even, pltpu.roll(odd, 64, 1))
    codes_ref[...] = jnp.where(first, pltpu.roll(even, 64, 1), odd)

    def fetch(b, _):
        for k in range(2):
            line = 2 * b + k
            row = rows_ref[pl.ds(line, 1), :]
            high = jnp.right_shift(row, 8)
            low = jnp.bitwise_and(row, 255)
            hot = (iota((256, 128), 0) == low).astype(f32).astype(bf16)
            wide[:, k * 128 : (k + 1) * 128] = hot
        found = dot(table_ref[...], wide[...])
        for k in range(2):
            line = 2 * b + k
            row = rows_ref[pl.ds(line, 1), :]
            high = jnp.broadcast_to(jnp.right_shift(row, 8), (8, 128))
            half = found[:, k * 128 : (k + 1) * 128]
            masks = [high == h for h in range(16)]
            for g in range(8):
                parts = []
                for base in (g * 8, 64 + g * 8):
                    acc = half[base : base + 8]
                    for h in range(1, 16):
                        acc = jnp.where(masks[h], half[h * 128 + base : h * 128 + base + 8], acc)
                    parts.append(acc)
                if g == 7:
                    extra = parts[0]
                if g == 0:
                    head = parts
                else:
                    slots_ref[pl.ds(g * 512 + line, 8, stride=64), :] = parts[0] + parts[1]
            third = jnp.where(iota((8, 128), 0) < 3, pltpu.roll(extra, 5, 0), 0.0)
            slots_ref[pl.ds(line, 8, stride=64), :] = head[0] + (head[1] + third)
        return 0

    lax.fori_loop(0, 32, fetch, 0)

    def work(g, _):
        at = pl.multiple_of(g * 8, 8)
        rows = [slots_ref[pl.ds(pl.multiple_of(r * 64 + at, 8), 8), :] for r in range(PARAM)]
        camera = camera_of(codes_ref[pl.ds(at, 8), :], cos_ref, sin_ref)
        values = project_slots(rows, *camera)
        values.append(jnp.zeros((8, 128), f32))
        left = iota((8, 128), 1) < 64
        for line in range(LINES):
            a, b = values[2 * line], values[2 * line + 1]
            out_ref[pl.ds(g * 80 + line, 8, stride=10), :] = jnp.where(left, a, pltpu.roll(b, 64, 1))
            out_ref[pl.ds(g * 80 + 5 + line, 8, stride=10), :] = jnp.where(
                left, pltpu.roll(a, 64, 1), b
            )
        return 0

    lax.fori_loop(0, 8, work, 0)


def monomials(x, y, which):
    out = jnp.zeros(x.shape, f32)
    for k, value in enumerate((jnp.ones_like(x), x, y, x * x, x * y, y * y)):
        out = jnp.where(which == k, value, out)
    return out


def render_kernel(came_ref, lists_ref, targets_ref, out_ref, table, back):
    first = iota((64, 128), 1) < 64
    for q in range(SENT):
        line = q // 2
        even = came_ref[pl.ds(line, 64, stride=10), :]
        odd = came_ref[pl.ds(5 + line, 64, stride=10), :]
        if q % 2 == 0:
            dense = jnp.where(first, even, pltpu.roll(odd, 64, 1))
        else:
            dense = jnp.where(first, pltpu.roll(even, 64, 1), odd)
        square = jnp.concatenate([dense[:32], dense[32:]], axis=1)
        for s, part in enumerate(pieces(square, 3)):
            table[pl.ds(s * 288 + q * 32, 32), :] = part
    back[...] = jnp.zeros_like(back)
    col = iota((PIX, 32), 1)
    pix = iota((PIX, 32), 0)
    basis = monomials(
        jnp.bitwise_and(pix, 15).astype(f32) - 7.5,
        jnp.right_shift(pix, 4).astype(f32) - 7.5,
        jnp.where(col < 24, jnp.bitwise_and(col, 7), 7),
    ).astype(bf16)
    row = iota((16, PIX), 0)
    pix = iota((16, PIX), 1)
    basis_t = monomials(
        jnp.bitwise_and(pix, 15).astype(f32) - 7.5,
        jnp.right_shift(pix, 4).astype(f32) - 7.5,
        row,
    ).astype(bf16)
    before = (iota((LIST, LIST), 0) < iota((LIST, LIST), 1)).astype(f32).astype(bf16)
    after = (iota((LIST, LIST), 0) > iota((LIST, LIST), 1)).astype(f32).astype(bf16)
    eight = iota((8, LIST), 0)

    def stack(parts):
        wide = [p.astype(f32) for p in parts]
        while len(wide) < 4:
            wide.append(jnp.zeros_like(wide[0]))
        return jnp.concatenate(wide, axis=0)

    def tile(t, _):
        high, low = slot_parts(lists_ref[pl.ds(t, 1), :])
        hot = (iota((256, LIST), 0) == low).astype(f32).astype(bf16)
        here = iota((32, LIST), 0) == high
        found = dot(table[...], hot)
        found = found[0:288] + (found[288:576] + found[576:864])
        coefs = jnp.zeros((8, LIST), f32)
        color = jnp.zeros((8, LIST), f32)
        for q in range(SENT):
            value = jnp.sum(
                jnp.where(here, found[q * 32 : (q + 1) * 32], 0.0), axis=0, keepdims=True
            )
            if q < 6:
                coefs = jnp.where(eight == q, value, coefs)
            else:
                color = jnp.where(eight == q - 6, value, color)
        exponent = dot(basis, stack(pieces(coefs, 3)).astype(bf16))
        alpha = jnp.exp(exponent)
        keep = 1.0 - alpha
        log_keep = jnp.log(keep)
        log_top, log_low = pieces(log_keep, 2)
        through = jnp.exp(dot(log_top, before) + dot(log_low, before))
        weight = alpha * through
        w_top, w_low = pieces(weight, 2)
        colors = pieces(color, 3)
        color_rows = stack(colors).astype(bf16)
        seen = dot_t(color_rows, w_top) + dot_t(color_rows, w_low)
        seen = seen[0:8] + (seen[8:16] + seen[16:24])
        pull = (seen - targets_ref[t]) * (1.0 / loss_scale)
        pulls = pieces(pull, 3)
        cross = jnp.transpose(stack([pulls[0], pulls[0], pulls[1], pulls[1]])).astype(bf16)
        other = stack([colors[0], colors[1], colors[0], colors[1]]).astype(bf16)
        gain = weight * dot(cross, other)
        g_top, g_low = pieces(gain, 2)
        behind = dot(g_top, after) + dot(g_low, after)
        slope = gain - behind * (alpha / keep)
        moment = sum(dot(basis_t, part) for part in pieces(slope, 3))
        pull_rows = stack(pulls).astype(bf16)
        tint = dot(pull_rows, w_top) + dot(pull_rows, w_low)
        tint = tint[0:8] + (tint[8:16] + tint[16:24])
        spread = []
        for q in range(SENT):
            value = moment[q : q + 1] if q < 6 else tint[q - 6 : q - 5]
            spread.append(jnp.where(here, jnp.broadcast_to(value, (32, LIST)), 0.0))
        for part in pieces(jnp.concatenate(spread, axis=0), 3):
            back[...] += dot_t(part, hot)
        return 0

    lax.fori_loop(0, TILES, tile, 0)

    zero = jnp.zeros((64, 128), f32)

    def dense_of(q):
        if q >= SENT:
            return zero
        square = back[pl.ds(q * 32, 32), :]
        return jnp.concatenate([square[:, :128], square[:, 128:]], axis=0)

    for line in range(LINES):
        a, b = dense_of(2 * line), dense_of(2 * line + 1)
        out_ref[pl.ds(line, 64, stride=10), :] = jnp.where(first, a, pltpu.roll(b, 64, 1))
        out_ref[pl.ds(5 + line, 64, stride=10), :] = jnp.where(first, pltpu.roll(a, 64, 1), b)


def rates(shape):
    row = iota(shape, 0)
    out = jnp.full(shape, 0.000125, f32)
    for end, rate in ((14, 0.0025), (11, 0.05), (10, 0.001), (6, 0.005), (3, 0.0008)):
        out = jnp.where(row < end, rate, out)
    return out


DEPTH = 1024


def update_kernel(
    came_ref, slots_ref, rows_ref, codes_ref, cos_ref, sin_ref, params_ref, first_ref, second_ref,
    new_params_ref, new_first_ref, new_second_ref, grads, left_ref, right_ref, total,
):
    def work(g, _):
        at = pl.multiple_of(g * 8, 8)
        rows = [slots_ref[pl.ds(pl.multiple_of(r * 64 + at, 8), 8), :] for r in range(PARAM)]
        cos_yaw, sin_yaw, centre_x, centre_y = camera_of(
            codes_ref[pl.ds(at, 8), :], cos_ref, sin_ref
        )
        left = iota((8, 128), 1) < 64
        cots = []
        for line in range(LINES):
            even = came_ref[pl.ds(g * 80 + line, 8, stride=10), :]
            odd = came_ref[pl.ds(g * 80 + 5 + line, 8, stride=10), :]
            cots.append(jnp.where(left, even, pltpu.roll(odd, 64, 1)))
            cots.append(jnp.where(left, pltpu.roll(even, 64, 1), odd))
        _, pullback = jax.vjp(
            lambda r: project_slots(r, cos_yaw, sin_yaw, centre_x, centre_y), rows
        )
        (out,) = pullback(cots[:SENT])
        for r in range(PARAM):
            grads[pl.ds(pl.multiple_of(r * 64 + at, 8), 8), :] = out[r]
        return 0

    for r in range(PARAM, 64):
        grads[pl.ds(r * 64, 64), :] = jnp.zeros((64, 128), f32)
    lax.fori_loop(0, 8, work, 0)
    total[...] = jnp.zeros_like(total)

    def gather(step, _):
        for k in range(DEPTH // 128):
            line = step * (DEPTH // 128) + k
            row = rows_ref[pl.ds(line, 1), :]
            high = jnp.right_shift(row, 8)
            low = jnp.bitwise_and(row, 255)
            cols = slice(k * 128, (k + 1) * 128)
            right_ref[:, cols] = (iota((256, 128), 0) == low).astype(f32).astype(bf16)
            value = jnp.concatenate(
                [grads[pl.ds(g * 512 + line, 8, stride=64), :] for g in range(8)], axis=0
            )
            top = value.astype(bf16).astype(f32)
            both = jnp.concatenate([top, value - top], axis=0)
            for h in range(16):
                left_ref[pl.ds(h * 128, 128), cols] = jnp.where(high == h, both, 0.0).astype(bf16)
        total[...] += dot_t(left_ref[...], right_ref[...])
        return 0

    lax.fori_loop(0, SLOTS // DEPTH, gather, 0)
    bias_one = 1.0 - beta_one**STEP
    bias_two = 1.0 - beta_two**STEP
    rate = rates((PARAM, 256))
    for h in range(16):
        cols = slice(h * 256, (h + 1) * 256)
        gradient = total[h * 128 : h * 128 + PARAM] + total[h * 128 + 64 : h * 128 + 64 + PARAM]
        first_new = beta_one * first_ref[:, cols] + (1.0 - beta_one) * gradient
        second_new = beta_two * second_ref[:, cols] + (1.0 - beta_two) * gradient * gradient
        new_first_ref[:, cols] = first_new
        new_second_ref[:, cols] = second_new
        new_params_ref[:, cols] = params_ref[:, cols] - rate * (first_new / bias_one) / (
            jnp.sqrt(second_new / bias_two) + adam_eps
        )


def shape(rows, cols, dtype=f32):
    return jax.ShapeDtypeStruct((rows, cols), dtype)


def exchange(lines, count):
    sent = lines.reshape(128, 1, count * 128)
    came = lax.all_to_all(sent, AXES, split_axis=0, concat_axis=0, tiled=True)
    return came.reshape(128 * count, 128)


def shards(params, adam_first, adam_second, view_yaw, tile_plan, tile_lists, requests, targets):
    cos_yaw = jnp.broadcast_to(jnp.pad(jnp.cos(view_yaw), (0, 96))[None, :], (8, 128))
    sin_yaw = jnp.broadcast_to(jnp.pad(jnp.sin(view_yaw), (0, 96))[None, :], (8, 128))
    asked = call(ask_kernel, shape(128, 128, i32), "ask", in_specs=[SM, VM, VM])(
        tile_plan, tile_lists, requests.reshape(64, 128)
    )
    came = exchange(asked, 1)
    table = call(table_kernel, shape(2048, 256, bf16), "table", in_specs=[VM])(
        jnp.pad(params, ((0, 64 - PARAM), (0, 0)))
    )
    aims = jnp.pad(jnp.transpose(targets, (1, 0, 2)), ((0, 0), (0, 5), (0, 0)))
    answers, slots, rows, codes = call(
        answer_kernel,
        (shape(128 * LINES, 128), shape(64 * 64, 128), shape(64, 128, i32), shape(64, 128, i32)),
        "answer",
        scratch=[pltpu.VMEM((256, 256), bf16)],
        in_specs=[VM] * 4,
        flops=9_000_000_000,
    )(came, table, cos_yaw, sin_yaw)
    arrived = exchange(answers, LINES)
    returned = call(
        render_kernel,
        shape(128 * LINES, 128),
        "render",
        scratch=[pltpu.VMEM((864, 256), bf16), pltpu.VMEM((288, 256), f32)],
        in_specs=[VM] * 3,
        flops=5_000_000_000,
    )(arrived, tile_lists, aims)
    back = exchange(returned, LINES)
    return call(
        update_kernel,
        (shape(PARAM, OWN), shape(PARAM, OWN), shape(PARAM, OWN)),
        "update",
        scratch=[
            pltpu.VMEM((64 * 64, 128), f32),
            pltpu.VMEM((2048, DEPTH), bf16),
            pltpu.VMEM((256, DEPTH), bf16),
            pltpu.VMEM((2048, 256), f32),
        ],
        in_specs=[VM] * 9,
        flops=9_000_000_000,
    )(back, slots, rows, codes, cos_yaw, sin_yaw, params, adam_first, adam_second)


def solution(mesh):
    placed = (
        P(None, AXES),
        P(None, AXES),
        P(None, AXES),
        P(),
        P(AXES),
        P(AXES, None),
        P(AXES, None),
        P(None, AXES, None),
    )
    return jax.shard_map(
        shards,
        mesh=mesh,
        in_specs=placed,
        out_specs=(P(None, AXES), P(None, AXES), P(None, AXES)),
        check_vma=False,
    )
```

```python
from functools import partial

import jax
import jax.numpy as jnp
from jax import lax
from jax.experimental import pallas as pl
from jax.experimental.pallas import tpu as pltpu
from jax.sharding import PartitionSpec as P

AXES = ("img", "blk")
STEP = 1000
TILES_ACROSS = 120
TILES_VIEW = 8160
TILE_EDGE = 16
PARAM = 59
OWN = 4096
SLOTS = 8192
TILES = 16
LIST = 256
PIX = 256
SENT = 9
LINES = 5

focal_px = 2400.0
camera_distance = 10.0
low_pass = 0.3
loss_scale = 16.0
beta_one = 0.9
beta_two = 0.999
adam_eps = 1e-08
band_zero = 0.28209479177387814
band_one = 0.4886025119029199
band_two = (
    1.0925484305920792,
    -1.0925484305920792,
    0.31539156525252005,
    -1.0925484305920792,
    0.5462742152960396,
)
band_three = (
    -0.5900435899266435,
    2.890611442640554,
    -0.4570457994644658,
    0.3731763325901154,
    -0.4570457994644658,
    1.445305721320277,
    -0.5900435899266435,
)
f32 = jnp.float32
bf16 = jnp.bfloat16
i32 = jnp.int32
VM = pl.BlockSpec(memory_space=pltpu.VMEM)
SM = pl.BlockSpec(memory_space=pltpu.SMEM)


def iota(shape, dim):
    return lax.broadcasted_iota(i32, shape, dim)


def dot(a, b):
    return lax.dot_general(a, b, (((1,), (0,)), ((), ())), preferred_element_type=f32)


def dot_t(a, b):
    return lax.dot_general(a, b, (((1,), (1,)), ((), ())), preferred_element_type=f32)


def pieces(x, count):
    out = []
    for k in range(count):
        part = x.astype(bf16)
        out.append(part)
        if k + 1 < count:
            x = x - part.astype(f32)
    return out


def call(kernel, out_shape, name, scratch=(), in_specs=None, flops=0):
    return partial(
        pl.pallas_call,
        kernel,
        out_shape=out_shape,
        in_specs=in_specs,
        out_specs=jax.tree.map(lambda _: VM, out_shape),
        scratch_shapes=list(scratch),
        name=name,
        cost_estimate=pl.CostEstimate(flops=flops, bytes_accessed=4 << 20, transcendentals=0),
        compiler_params=pltpu.CompilerParams(vmem_limit_bytes=40 << 20),
    )()


def harmonics(looking_x, look_y, look_z):
    square_x = looking_x * looking_x
    square_y = look_y * look_y
    square_z = look_z * look_z
    return [
        jnp.full_like(looking_x, band_zero),
        -band_one * look_y,
        band_one * look_z,
        -band_one * looking_x,
        band_two[0] * looking_x * look_y,
        band_two[1] * look_y * look_z,
        band_two[2] * (2.0 * square_z - square_x - square_y),
        band_two[3] * looking_x * look_z,
        band_two[4] * (square_x - square_y),
        band_three[0] * look_y * (3.0 * square_x - square_y),
        band_three[1] * looking_x * look_y * look_z,
        band_three[2] * look_y * (4.0 * square_z - square_x - square_y),
        band_three[3] * look_z * (2.0 * square_z - 3.0 * square_x - 3.0 * square_y),
        band_three[4] * looking_x * (4.0 * square_z - square_x - square_y),
        band_three[5] * look_z * (square_x - square_y),
        band_three[6] * looking_x * (square_x - 3.0 * square_y),
    ]


def project_slots(rows, cos_yaw, sin_yaw, centre_x, centre_y):
    world_x, world_y, world_z = rows[0], rows[1], rows[2]
    view_x = cos_yaw * world_x + sin_yaw * world_z
    view_z = cos_yaw * world_z - sin_yaw * world_x + camera_distance
    inverse_z = 1.0 / view_z
    mean_x = focal_px * view_x * inverse_z - centre_x
    mean_y = focal_px * world_y * inverse_z - centre_y
    scales = [jnp.exp(rows[3 + k]) for k in range(3)]
    norm = jnp.sqrt(
        rows[6] * rows[6] + rows[7] * rows[7] + rows[8] * rows[8] + rows[9] * rows[9]
    )
    inverse_norm = 1.0 / norm
    quat_w, quat_x, quat_y, quat_z = [rows[6 + k] * inverse_norm for k in range(4)]
    rotation = [
        [
            1.0 - 2.0 * (quat_y * quat_y + quat_z * quat_z),
            2.0 * (quat_x * quat_y - quat_w * quat_z),
            2.0 * (quat_x * quat_z + quat_w * quat_y),
        ],
        [
            2.0 * (quat_x * quat_y + quat_w * quat_z),
            1.0 - 2.0 * (quat_x * quat_x + quat_z * quat_z),
            2.0 * (quat_y * quat_z - quat_w * quat_x),
        ],
        [
            2.0 * (quat_x * quat_z - quat_w * quat_y),
            2.0 * (quat_y * quat_z + quat_w * quat_x),
            1.0 - 2.0 * (quat_x * quat_x + quat_y * quat_y),
        ],
    ]
    focal_z = focal_px * inverse_z
    shear_x = focal_z * view_x * inverse_z
    shear_y = focal_z * world_y * inverse_z
    jacob_ax = focal_z * cos_yaw + shear_x * sin_yaw
    jacob_az = focal_z * sin_yaw - shear_x * cos_yaw
    jacob_bx = shear_y * sin_yaw
    jacob_bz = -shear_y * cos_yaw
    row_a = [
        (jacob_ax * rotation[0][k] + jacob_az * rotation[2][k]) * scales[k] for k in range(3)
    ]
    row_b = [
        (jacob_bx * rotation[0][k] + focal_z * rotation[1][k] + jacob_bz * rotation[2][k])
        * scales[k]
        for k in range(3)
    ]
    covar_xx = row_a[0] * row_a[0] + row_a[1] * row_a[1] + row_a[2] * row_a[2] + low_pass
    covar_yy = row_b[0] * row_b[0] + row_b[1] * row_b[1] + row_b[2] * row_b[2] + low_pass
    covar_xy = row_a[0] * row_b[0] + row_a[1] * row_b[1] + row_a[2] * row_b[2]
    inverse_det = 1.0 / (covar_xx * covar_yy - covar_xy * covar_xy)
    conic_a = covar_yy * inverse_det
    conic_b = -covar_xy * inverse_det
    conic_c = covar_xx * inverse_det
    log_opacity = rows[10] - jnp.log(1.0 + jnp.exp(rows[10]))
    slope_x = conic_a * mean_x + conic_b * mean_y
    slope_y = conic_c * mean_y + conic_b * mean_x
    constant = log_opacity - 0.5 * (slope_x * mean_x + slope_y * mean_y)
    inverse_len = 1.0 / jnp.sqrt(view_x * view_x + world_y * world_y + view_z * view_z)
    basis = harmonics(
        (cos_yaw * view_x - sin_yaw * view_z) * inverse_len,
        world_y * inverse_len,
        (sin_yaw * view_x + cos_yaw * view_z) * inverse_len,
    )
    colors = []
    for channel in range(3):
        total = basis[0] * rows[11 + channel]
        for degree in range(1, 16):
            total = total + basis[degree] * rows[11 + 3 * degree + channel]
        colors.append(jnp.maximum(0.5 + total, 0.0))
    return [
        constant,
        slope_x,
        slope_y,
        -0.5 * conic_a,
        -conic_b,
        -0.5 * conic_c,
    ] + colors


def camera_of(codes, cos_ref, sin_ref):
    code = codes.astype(f32)
    view = jnp.floor((code + 0.5) * (1.0 / TILES_VIEW))
    number = code - view * float(TILES_VIEW)
    across = jnp.floor((number + 0.5) * (1.0 / TILES_ACROSS))
    column = number - across * float(TILES_ACROSS)
    view = view.astype(i32)
    cos_yaw = jnp.take_along_axis(cos_ref[...], view, axis=1, mode="promise_in_bounds")
    sin_yaw = jnp.take_along_axis(sin_ref[...], view, axis=1, mode="promise_in_bounds")
    centre_x = column * 16.0 + (8.0 - 960.0)
    centre_y = across * 16.0 + (8.0 - 544.0)
    return cos_yaw, sin_yaw, centre_x, centre_y


def slot_parts(slot):
    line = jnp.right_shift(slot, 7)
    high = jnp.bitwise_and(line, 31)
    low = jnp.right_shift(line, 5) * 128 + jnp.bitwise_and(slot, 127)
    return high, low


def ask_kernel(plan_ref, lists_ref, req_ref, out_ref):
    total = jnp.zeros((32, 256), f32)
    for t in range(TILES):
        high, low = slot_parts(lists_ref[t : t + 1, :])
        hot = (iota((256, LIST), 0) == low).astype(f32).astype(bf16)
        left = jnp.where(iota((32, LIST), 0) == high, float(t + 1), 0.0).astype(bf16)
        total = total + dot_t(left, hot)
    codes = jnp.zeros((32, 256), i32)
    for t in range(TILES):
        codes = jnp.where(total == float(t + 1), plan_ref[t], codes)
    codes = jnp.concatenate([codes[:, :128], codes[:, 128:]], axis=0)
    asked = req_ref[...]
    first = iota((64, 128), 1) < 64
    out_ref[pl.ds(0, 64, stride=2), :] = jnp.where(first, asked, pltpu.roll(codes, 64, 1))
    out_ref[pl.ds(1, 64, stride=2), :] = jnp.where(first, pltpu.roll(asked, 64, 1), codes)


def table_kernel(params_ref, out_ref, turned_ref):
    for h in range(16):
        cols = pl.ds(h * 256, 256)
        block = params_ref[:, cols]
        turned_ref[h * 256 : (h + 1) * 256, :] = jnp.transpose(
            jnp.concatenate([block, jnp.zeros((64, 256), f32)], axis=0)
        )
        top, mid, rest = pieces(block, 3)
        shifted = pltpu.roll(rest[0:16].astype(f32)[0:8], 3, 0)
        last = top.astype(f32)[56:64]
        last = jnp.where(iota((8, 256), 0) < 3, last, shifted)
        top = jnp.concatenate([top.astype(f32)[:56], last], axis=0).astype(bf16)
        out_ref[pl.ds(h * 128, 64), :] = top
        out_ref[pl.ds(h * 128 + 64, 64), :] = mid


def answer_kernel(
    came_ref, index_ref, table_ref, turned_ref, cos_ref, sin_ref,
    out_ref, slots_ref, rows_ref, codes_ref, wide, fetched0, fetched1,
):
    even = came_ref[pl.ds(0, 64, stride=2), :]
    odd = came_ref[pl.ds(1, 64, stride=2), :]
    first = iota((64, 128), 1) < 64
    rows_ref[...] = jnp.where(first, even, pltpu.roll(odd, 64, 1))
    codes_ref[...] = jnp.where(first, pltpu.roll(even, 64, 1), odd)

    def fetch(b, _):
        for k in range(2):
            line = 2 * b + k
            row = rows_ref[pl.ds(line, 1), :]
            high = jnp.right_shift(row, 8)
            low = jnp.bitwise_and(row, 255)
            hot = (iota((256, 128), 0) == low).astype(f32).astype(bf16)
            wide[:, k * 128 : (k + 1) * 128] = hot
        found = dot(table_ref[...], wide[...])
        for k in range(2):
            line = 2 * b + k
            row = rows_ref[pl.ds(line, 1), :]
            high = jnp.broadcast_to(jnp.right_shift(row, 8), (8, 128))
            half = found[:, k * 128 : (k + 1) * 128]
            masks = [high == h for h in range(16)]
            for g in range(8):
                parts = []
                for base in (g * 8, 64 + g * 8):
                    acc = half[base : base + 8]
                    for h in range(1, 16):
                        acc = jnp.where(masks[h], half[h * 128 + base : h * 128 + base + 8], acc)
                    parts.append(acc)
                if g == 7:
                    extra = parts[0]
                if g == 0:
                    head = parts
                else:
                    slots_ref[pl.ds(g * 512 + line, 8, stride=64), :] = parts[0] + parts[1]
            third = jnp.where(iota((8, 128), 0) < 3, pltpu.roll(extra, 5, 0), 0.0)
            slots_ref[pl.ds(line, 8, stride=64), :] = head[0] + (head[1] + third)
        for k, fetched in enumerate((fetched0, fetched1)):
            line = 32 + 2 * b + k
            for h in range(2):
                for j in range(64):
                    at = index_ref[2 * line + h, j]
                    fetched[h * 64 + j : h * 64 + j + 1, :] = turned_ref[pl.ds(at, 1), :]
            turned = jnp.transpose(fetched[...])
            for g in range(8):
                slots_ref[pl.ds(g * 512 + line, 8, stride=64), :] = turned[g * 8 : g * 8 + 8]
        return 0

    lax.fori_loop(0, 16, fetch, 0)

    def work(g, _):
        at = pl.multiple_of(g * 8, 8)
        rows = [slots_ref[pl.ds(pl.multiple_of(r * 64 + at, 8), 8), :] for r in range(PARAM)]
        camera = camera_of(codes_ref[pl.ds(at, 8), :], cos_ref, sin_ref)
        values = project_slots(rows, *camera)
        values.append(jnp.zeros((8, 128), f32))
        left = iota((8, 128), 1) < 64
        for line in range(LINES):
            a, b = values[2 * line], values[2 * line + 1]
            out_ref[pl.ds(g * 80 + line, 8, stride=10), :] = jnp.where(left, a, pltpu.roll(b, 64, 1))
            out_ref[pl.ds(g * 80 + 5 + line, 8, stride=10), :] = jnp.where(
                left, pltpu.roll(a, 64, 1), b
            )
        return 0

    lax.fori_loop(0, 8, work, 0)


def monomials(x, y, which):
    out = jnp.zeros(x.shape, f32)
    for k, value in enumerate((jnp.ones_like(x), x, y, x * x, x * y, y * y)):
        out = jnp.where(which == k, value, out)
    return out


def render_kernel(
    came_ref, lists_ref, targets_ref, out_ref,
    table, hots, back, coefs0, coefs1, spread0, spread1, alphas, before, weights, gains, behind, sums,
):
    coefs, spreads = (coefs0, coefs1), (spread0, spread1)
    first = iota((64, 128), 1) < 64
    for q in range(SENT):
        line = q // 2
        even = came_ref[pl.ds(line, 64, stride=10), :]
        odd = came_ref[pl.ds(5 + line, 64, stride=10), :]
        if q % 2 == 0:
            dense = jnp.where(first, even, pltpu.roll(odd, 64, 1))
        else:
            dense = jnp.where(first, pltpu.roll(even, 64, 1), odd)
        square = jnp.concatenate([dense[:32], dense[32:]], axis=1)
        for s, part in enumerate(pieces(square, 3 if q < 6 else 2)):
            table[pl.ds(s * 288 + q * 32, 32), :] = part
    back[...] = jnp.zeros_like(back)
    spread1[...] = jnp.zeros_like(spread1)
    sums[...] = jnp.zeros_like(sums)
    row = iota((32, PIX), 0)
    pix = iota((32, PIX), 1)
    basis = monomials(
        jnp.bitwise_and(pix, 15).astype(f32) - 7.5,
        jnp.right_shift(pix, 4).astype(f32) - 7.5,
        jnp.where(row < 24, jnp.bitwise_and(row, 7), 7),
    ).astype(bf16)
    sub = iota((8, PIX), 0)
    lane = iota((8, 128), 1)
    offset_x = jnp.bitwise_and(lane, 15).astype(f32) - 7.5
    offset_y = jnp.right_shift(lane, 4).astype(f32) - 3.5
    square_y = offset_y * offset_y + 16.0
    eight_y = offset_y * 8.0

    def make_hot(t, _):
        low = slot_parts(lists_ref[pl.ds(t, 1), :])[1]
        hots[t] = (iota((256, LIST), 0) == low).astype(f32).astype(bf16)
        return 0

    lax.fori_loop(0, TILES, make_hot, 0)

    def here_of(t):
        return iota((32, LIST), 0) == slot_parts(lists_ref[pl.ds(t, 1), :])[0]

    def gather(t, to):
        found = dot(table[...], hots[t])
        here = here_of(t)
        values = []
        for q in range(SENT):
            at = q * 32
            value = found[at : at + 32] + (
                found[288 + at : 320 + at] + found[576 + at : 608 + at]
                if q < 6
                else found[288 + at : 320 + at]
            )
            values.append(jnp.sum(jnp.where(here, value, 0.0), axis=0, keepdims=True))
        shape_rows = jnp.zeros((8, LIST), f32)
        color_rows = jnp.zeros((8, LIST), f32)
        for q in range(6):
            shape_rows = jnp.where(sub == q, values[q], shape_rows)
        for q in range(3):
            color_rows = jnp.where(sub == q, values[6 + q], color_rows)
        parts = [p.astype(f32) for p in pieces(shape_rows, 3)]
        stack = jnp.concatenate(parts + [color_rows] + [jnp.zeros((96, LIST), f32)], axis=0)
        to[...] = jnp.transpose(stack)

    def scatter(t, source):
        here = here_of(t)
        parts = [p.astype(f32) for p in pieces(source[...], 3)]
        left = []
        for s in range(3):
            for q in range(SENT if s < 2 else 6):
                value = jnp.broadcast_to(parts[s][q : q + 1], (32, LIST))
                left.append(jnp.where(here, value, 0.0).astype(bf16))
        moved = dot_t(jnp.concatenate(left, axis=0), hots[t])
        back[0:192] += moved[0:192] + (moved[288:480] + moved[576:768])
        back[192:288] += moved[192:288] + moved[480:576]

    def scan8(x, neutral, op, down):
        def shift(y, n):
            if down:
                return jnp.where(sub >= n, pltpu.roll(y, n, 0), neutral)
            return jnp.where(sub < 8 - n, pltpu.roll(y, 8 - n, 0), neutral)

        x = shift(x, 1)
        for n in (1, 2, 4):
            x = op(x, shift(x, n))
        return x

    def compose(t, source, to):
        exponent = dot(source[:, 0:32].astype(bf16), basis)
        product = jnp.ones((8, PIX), f32)
        for v in range(32):
            rows = slice(v * 8, v * 8 + 8)
            alpha = jnp.exp(exponent[rows])
            alphas[rows] = alpha
            before[rows] = product
            product = product * (1.0 - alpha)
        ahead = scan8(product, 1.0, jnp.multiply, True)
        seen = [jnp.zeros((8, PIX), f32) for _ in range(3)]
        for v in range(32):
            rows = slice(v * 8, v * 8 + 8)
            weight = alphas[rows] * (before[rows] * ahead)
            weights[rows] = weight
            for c in range(3):
                seen[c] = seen[c] + weight * source[rows, 24 + c : 25 + c]
        pulls = []
        for c in range(3):
            total = jnp.sum(seen[c], axis=0, keepdims=True)
            pull = (total - targets_ref[t, c : c + 1, :]) * (1.0 / loss_scale)
            pulls.append(jnp.broadcast_to(pull, (8, PIX)))
        rest = jnp.zeros((8, PIX), f32)
        for v in reversed(range(32)):
            rows = slice(v * 8, v * 8 + 8)
            weight = weights[rows]
            gain = pulls[0] * source[rows, 24:25]
            gain = gain + pulls[1] * source[rows, 25:26]
            gain = gain + pulls[2] * source[rows, 26:27]
            gain = gain * weight
            gains[rows] = gain
            behind[rows] = rest
            rest = rest + gain
            line = jnp.zeros((8, 128), f32)
            for c in range(3):
                tint = weight * pulls[c]
                tint = jnp.sum(tint[:, :128] + tint[:, 128:], axis=1, keepdims=True)
                line = jnp.where(lane == 6 + c, tint, line)
            sums[rows, :] = line
        after = scan8(rest, 0.0, jnp.add, False)
        for v in range(32):
            rows = slice(v * 8, v * 8 + 8)
            alpha = alphas[rows]
            slope = gains[rows] - (behind[rows] + after) * (alpha / (1.0 - alpha))
            upper, lower = slope[:, :128], slope[:, 128:]
            both, apart = upper + lower, lower - upper
            along = both * offset_x
            down = both * offset_y + apart * 4.0
            line = sums[rows, :]
            for k, value in enumerate(
                (both, along, down, along * offset_x, down * offset_x,
                 both * square_y + apart * eight_y)
            ):
                line = jnp.where(lane == k, jnp.sum(value, axis=1, keepdims=True), line)
            sums[rows, :] = line
        to[...] = jnp.transpose(sums[...])[0:16]

    gather(0, coefs[0])

    def pair(step, _):
        for k in range(2):
            t = 2 * step + k
            gather(jnp.minimum(t + 1, TILES - 1), coefs[1 - k])
            compose(t, coefs[k], spreads[k])
            scatter(jnp.maximum(t - 1, 0), spreads[1 - k])
        return 0

    lax.fori_loop(0, TILES // 2, pair, 0)
    scatter(TILES - 1, spreads[1])

    zero = jnp.zeros((64, 128), f32)

    def dense_of(q):
        if q >= SENT:
            return zero
        square = back[pl.ds(q * 32, 32), :]
        return jnp.concatenate([square[:, :128], square[:, 128:]], axis=0)

    for line in range(LINES):
        a, b = dense_of(2 * line), dense_of(2 * line + 1)
        out_ref[pl.ds(line, 64, stride=10), :] = jnp.where(first, a, pltpu.roll(b, 64, 1))
        out_ref[pl.ds(5 + line, 64, stride=10), :] = jnp.where(first, pltpu.roll(a, 64, 1), b)


def rates(shape):
    row = iota(shape, 0)
    out = jnp.full(shape, 0.000125, f32)
    for end, rate in ((14, 0.0025), (11, 0.05), (10, 0.001), (6, 0.005), (3, 0.0008)):
        out = jnp.where(row < end, rate, out)
    return out


DEPTH = 512


def update_kernel(
    came_ref, index_ref, slots_ref, rows_ref, codes_ref, cos_ref, sin_ref, params_ref, first_ref, second_ref,
    new_params_ref, new_first_ref, new_second_ref,
    grads, left_ref, right_ref, total, sums0, sums1, *turned_refs,
):
    def work(g, _):
        at = pl.multiple_of(g * 8, 8)
        rows = [slots_ref[pl.ds(pl.multiple_of(r * 64 + at, 8), 8), :] for r in range(PARAM)]
        cos_yaw, sin_yaw, centre_x, centre_y = camera_of(
            codes_ref[pl.ds(at, 8), :], cos_ref, sin_ref
        )
        left = iota((8, 128), 1) < 64
        cots = []
        for line in range(LINES):
            even = came_ref[pl.ds(g * 80 + line, 8, stride=10), :]
            odd = came_ref[pl.ds(g * 80 + 5 + line, 8, stride=10), :]
            cots.append(jnp.where(left, even, pltpu.roll(odd, 64, 1)))
            cots.append(jnp.where(left, pltpu.roll(even, 64, 1), odd))
        _, pullback = jax.vjp(
            lambda r: project_slots(r, cos_yaw, sin_yaw, centre_x, centre_y), rows
        )
        (out,) = pullback(cots[:SENT])
        for r in range(PARAM):
            grads[pl.ds(pl.multiple_of(r * 64 + at, 8), 8), :] = out[r]
        return 0

    for r in range(PARAM, 64):
        grads[pl.ds(r * 64, 64), :] = jnp.zeros((64, 128), f32)
    lax.fori_loop(0, 8, work, 0)
    total[...] = jnp.zeros_like(total)
    sums0[...] = jnp.zeros_like(sums0)
    sums1[...] = jnp.zeros_like(sums1)

    def value_of(line):
        return jnp.concatenate(
            [grads[pl.ds(g * 512 + line, 8, stride=64), :] for g in range(8)], axis=0
        )

    def gather(step, _):
        for k in range(DEPTH // 128):
            line = 32 + step * (DEPTH // 128) + k
            turned = turned_refs[k]
            turned[...] = jnp.transpose(
                jnp.concatenate([value_of(line), jnp.zeros((64, 128), f32)], axis=0)
            )
            for j in range(0, 64, 8):
                for h, sums in enumerate((sums0, sums1)):
                    at = [index_ref[2 * line + h, j + n] for n in range(8)]
                    old = [sums[pl.ds(at[n], 1), :] for n in range(8)]
                    for n in range(8):
                        row = h * 64 + j + n
                        sums[pl.ds(at[n], 1), :] = old[n] + turned[row : row + 1, :]
        for k in range(DEPTH // 128):
            line = step * (DEPTH // 128) + k
            row = rows_ref[pl.ds(line, 1), :]
            high = jnp.right_shift(row, 8)
            low = jnp.bitwise_and(row, 255)
            cols = slice(k * 128, (k + 1) * 128)
            right_ref[:, cols] = (iota((256, 128), 0) == low).astype(f32).astype(bf16)
            value = value_of(line)
            top = value.astype(bf16).astype(f32)
            both = jnp.concatenate([top, value - top], axis=0)
            for h in range(16):
                left_ref[pl.ds(h * 128, 128), cols] = jnp.where(high == h, both, 0.0).astype(bf16)
        total[...] += dot_t(left_ref[...], right_ref[...])
        return 0

    lax.fori_loop(0, SLOTS // (2 * DEPTH), gather, 0)
    bias_one = 1.0 - beta_one**STEP
    bias_two = 1.0 - beta_two**STEP
    rate = rates((PARAM, 256)) * (1.0 / bias_one)
    for h in range(16):
        cols = slice(h * 256, (h + 1) * 256)
        gradient = total[h * 128 : h * 128 + PARAM] + total[h * 128 + 64 : h * 128 + 64 + PARAM]
        gradient = gradient + jnp.transpose(sums0[cols, :] + sums1[cols, :])[:PARAM]
        first_new = beta_one * first_ref[:, cols] + (1.0 - beta_one) * gradient
        second_new = beta_two * second_ref[:, cols] + (1.0 - beta_two) * gradient * gradient
        new_first_ref[:, cols] = first_new
        new_second_ref[:, cols] = second_new
        new_params_ref[:, cols] = params_ref[:, cols] - rate * first_new / (
            jnp.sqrt(second_new * (1.0 / bias_two)) + adam_eps
        )


def shape(rows, cols, dtype=f32):
    return jax.ShapeDtypeStruct((rows, cols), dtype)


def exchange(lines, count):
    sent = lines.reshape(128, 1, count * 128)
    came = lax.all_to_all(sent, AXES, split_axis=0, concat_axis=0, tiled=True)
    return came.reshape(128 * count, 128)


def shards(params, adam_first, adam_second, view_yaw, tile_plan, tile_lists, requests, targets):
    cos_yaw = jnp.broadcast_to(jnp.pad(jnp.cos(view_yaw), (0, 96))[None, :], (8, 128))
    sin_yaw = jnp.broadcast_to(jnp.pad(jnp.sin(view_yaw), (0, 96))[None, :], (8, 128))
    asked = call(ask_kernel, shape(128, 128, i32), "ask", in_specs=[SM, VM, VM])(
        tile_plan, tile_lists, requests.reshape(64, 128)
    )
    came = exchange(asked, 1)
    table, turned = call(
        table_kernel, (shape(2048, 256, bf16), shape(OWN, 128)), "table", in_specs=[VM]
    )(
        jnp.pad(params, ((0, 64 - PARAM), (0, 0)))
    )
    woven = jnp.transpose(tile_lists.reshape(TILES, 8, 32), (0, 2, 1)).reshape(TILES, LIST)
    aims = jnp.pad(jnp.transpose(targets, (1, 0, 2)), ((0, 0), (0, 5), (0, 0)))
    answers, slots, rows, codes = call(
        answer_kernel,
        (shape(128 * LINES, 128), shape(64 * 64, 128), shape(64, 128, i32), shape(64, 128, i32)),
        "answer",
        scratch=[
            pltpu.VMEM((256, 256), bf16),
            pltpu.VMEM((128, 128), f32),
            pltpu.VMEM((128, 128), f32),
        ],
        in_specs=[VM, SM] + [VM] * 4,
        flops=9_000_000_000,
    )(came, came, table, turned, cos_yaw, sin_yaw)
    arrived = exchange(answers, LINES)
    returned = call(
        render_kernel,
        shape(128 * LINES, 128),
        "render",
        scratch=[
            pltpu.VMEM((768, 256), bf16),
            pltpu.VMEM((TILES, 256, LIST), bf16),
            pltpu.VMEM((288, 256), f32),
            pltpu.VMEM((LIST, 128), f32),
            pltpu.VMEM((LIST, 128), f32),
            pltpu.VMEM((16, LIST), f32),
            pltpu.VMEM((16, LIST), f32),
            pltpu.VMEM((LIST, PIX), f32),
            pltpu.VMEM((LIST, PIX), f32),
            pltpu.VMEM((LIST, PIX), f32),
            pltpu.VMEM((LIST, PIX), f32),
            pltpu.VMEM((LIST, PIX), f32),
            pltpu.VMEM((LIST, 128), f32),
        ],
        in_specs=[VM] * 3,
        flops=5_000_000_000,
    )(arrived, woven, aims)
    back = exchange(returned, LINES)
    return call(
        update_kernel,
        (shape(PARAM, OWN), shape(PARAM, OWN), shape(PARAM, OWN)),
        "update",
        scratch=[
            pltpu.VMEM((64 * 64, 128), f32),
            pltpu.VMEM((2048, DEPTH), bf16),
            pltpu.VMEM((256, DEPTH), bf16),
            pltpu.VMEM((2048, 256), f32),
            pltpu.VMEM((OWN, 128), f32),
            pltpu.VMEM((OWN, 128), f32),
        ]
        + [pltpu.VMEM((128, 128), f32)] * (DEPTH // 128),
        in_specs=[VM, SM] + [VM] * 8,
        flops=9_000_000_000,
    )(back, came, slots, rows, codes, cos_yaw, sin_yaw, params, adam_first, adam_second)


def solution(mesh):
    placed = (
        P(None, AXES),
        P(None, AXES),
        P(None, AXES),
        P(),
        P(AXES),
        P(AXES, None),
        P(AXES, None),
        P(None, AXES, None),
    )
    return jax.shard_map(
        shards,
        mesh=mesh,
        in_specs=placed,
        out_specs=(P(None, AXES), P(None, AXES), P(None, AXES)),
        check_vma=False,
    )
```

```python
from functools import partial

import jax
import jax.numpy as jnp
from jax import lax
from jax.experimental import pallas as pl
from jax.experimental.pallas import tpu as pltpu
from jax.sharding import PartitionSpec as P

AXES = ("img", "blk")
STEP = 1000
TILES_ACROSS = 120
TILES_VIEW = 8160
TILE_EDGE = 16
PARAM = 59
OWN = 4096
SLOTS = 8192
TILES = 16
LIST = 256
PIX = 256
SENT = 9
LINES = 5

focal_px = 2400.0
camera_distance = 10.0
low_pass = 0.3
loss_scale = 16.0
beta_one = 0.9
beta_two = 0.999
adam_eps = 1e-08
band_zero = 0.28209479177387814
band_one = 0.4886025119029199
band_two = (
    1.0925484305920792,
    -1.0925484305920792,
    0.31539156525252005,
    -1.0925484305920792,
    0.5462742152960396,
)
band_three = (
    -0.5900435899266435,
    2.890611442640554,
    -0.4570457994644658,
    0.3731763325901154,
    -0.4570457994644658,
    1.445305721320277,
    -0.5900435899266435,
)
f32 = jnp.float32
bf16 = jnp.bfloat16
i32 = jnp.int32
VM = pl.BlockSpec(memory_space=pltpu.VMEM)
SM = pl.BlockSpec(memory_space=pltpu.SMEM)


def iota(shape, dim):
    return lax.broadcasted_iota(i32, shape, dim)


def dot(a, b):
    return lax.dot_general(a, b, (((1,), (0,)), ((), ())), preferred_element_type=f32)


def dot_t(a, b):
    return lax.dot_general(a, b, (((1,), (1,)), ((), ())), preferred_element_type=f32)


def pieces(x, count):
    out = []
    for k in range(count):
        part = x.astype(bf16)
        out.append(part)
        if k + 1 < count:
            x = x - part.astype(f32)
    return out


def call(kernel, out_shape, name, scratch=(), in_specs=None, flops=0, mib=16):
    return partial(
        pl.pallas_call,
        kernel,
        out_shape=out_shape,
        in_specs=in_specs,
        out_specs=jax.tree.map(lambda _: VM, out_shape),
        scratch_shapes=list(scratch),
        name=name,
        cost_estimate=pl.CostEstimate(flops=flops, bytes_accessed=4 << 20, transcendentals=0),
        compiler_params=pltpu.CompilerParams(vmem_limit_bytes=mib << 20),
    )()


def harmonics(looking_x, look_y, look_z):
    square_x = looking_x * looking_x
    square_y = look_y * look_y
    square_z = look_z * look_z
    return [
        jnp.full_like(looking_x, band_zero),
        -band_one * look_y,
        band_one * look_z,
        -band_one * looking_x,
        band_two[0] * looking_x * look_y,
        band_two[1] * look_y * look_z,
        band_two[2] * (2.0 * square_z - square_x - square_y),
        band_two[3] * looking_x * look_z,
        band_two[4] * (square_x - square_y),
        band_three[0] * look_y * (3.0 * square_x - square_y),
        band_three[1] * looking_x * look_y * look_z,
        band_three[2] * look_y * (4.0 * square_z - square_x - square_y),
        band_three[3] * look_z * (2.0 * square_z - 3.0 * square_x - 3.0 * square_y),
        band_three[4] * looking_x * (4.0 * square_z - square_x - square_y),
        band_three[5] * look_z * (square_x - square_y),
        band_three[6] * looking_x * (square_x - 3.0 * square_y),
    ]


def project_slots(rows, cos_yaw, sin_yaw, centre_x, centre_y):
    world_x, world_y, world_z = rows[0], rows[1], rows[2]
    view_x = cos_yaw * world_x + sin_yaw * world_z
    view_z = cos_yaw * world_z - sin_yaw * world_x + camera_distance
    inverse_z = 1.0 / view_z
    mean_x = focal_px * view_x * inverse_z - centre_x
    mean_y = focal_px * world_y * inverse_z - centre_y
    scales = [jnp.exp(rows[3 + k]) for k in range(3)]
    norm = jnp.sqrt(
        rows[6] * rows[6] + rows[7] * rows[7] + rows[8] * rows[8] + rows[9] * rows[9]
    )
    inverse_norm = 1.0 / norm
    quat_w, quat_x, quat_y, quat_z = [rows[6 + k] * inverse_norm for k in range(4)]
    rotation = [
        [
            1.0 - 2.0 * (quat_y * quat_y + quat_z * quat_z),
            2.0 * (quat_x * quat_y - quat_w * quat_z),
            2.0 * (quat_x * quat_z + quat_w * quat_y),
        ],
        [
            2.0 * (quat_x * quat_y + quat_w * quat_z),
            1.0 - 2.0 * (quat_x * quat_x + quat_z * quat_z),
            2.0 * (quat_y * quat_z - quat_w * quat_x),
        ],
        [
            2.0 * (quat_x * quat_z - quat_w * quat_y),
            2.0 * (quat_y * quat_z + quat_w * quat_x),
            1.0 - 2.0 * (quat_x * quat_x + quat_y * quat_y),
        ],
    ]
    focal_z = focal_px * inverse_z
    shear_x = focal_z * view_x * inverse_z
    shear_y = focal_z * world_y * inverse_z
    jacob_ax = focal_z * cos_yaw + shear_x * sin_yaw
    jacob_az = focal_z * sin_yaw - shear_x * cos_yaw
    jacob_bx = shear_y * sin_yaw
    jacob_bz = -shear_y * cos_yaw
    row_a = [
        (jacob_ax * rotation[0][k] + jacob_az * rotation[2][k]) * scales[k] for k in range(3)
    ]
    row_b = [
        (jacob_bx * rotation[0][k] + focal_z * rotation[1][k] + jacob_bz * rotation[2][k])
        * scales[k]
        for k in range(3)
    ]
    covar_xx = row_a[0] * row_a[0] + row_a[1] * row_a[1] + row_a[2] * row_a[2] + low_pass
    covar_yy = row_b[0] * row_b[0] + row_b[1] * row_b[1] + row_b[2] * row_b[2] + low_pass
    covar_xy = row_a[0] * row_b[0] + row_a[1] * row_b[1] + row_a[2] * row_b[2]
    inverse_det = 1.0 / (covar_xx * covar_yy - covar_xy * covar_xy)
    conic_a = covar_yy * inverse_det
    conic_b = -covar_xy * inverse_det
    conic_c = covar_xx * inverse_det
    log_opacity = rows[10] - jnp.log(1.0 + jnp.exp(rows[10]))
    slope_x = conic_a * mean_x + conic_b * mean_y
    slope_y = conic_c * mean_y + conic_b * mean_x
    constant = log_opacity - 0.5 * (slope_x * mean_x + slope_y * mean_y)
    inverse_len = 1.0 / jnp.sqrt(view_x * view_x + world_y * world_y + view_z * view_z)
    basis = harmonics(
        (cos_yaw * view_x - sin_yaw * view_z) * inverse_len,
        world_y * inverse_len,
        (sin_yaw * view_x + cos_yaw * view_z) * inverse_len,
    )
    colors = []
    for channel in range(3):
        total = basis[0] * rows[11 + channel]
        for degree in range(1, 16):
            total = total + basis[degree] * rows[11 + 3 * degree + channel]
        colors.append(jnp.maximum(0.5 + total, 0.0))
    return [
        constant,
        slope_x,
        slope_y,
        -0.5 * conic_a,
        -conic_b,
        -0.5 * conic_c,
    ] + colors


def camera_of(codes, cos_ref, sin_ref):
    code = jnp.maximum(codes, 0).astype(f32)
    view = jnp.floor((code + 0.5) * (1.0 / TILES_VIEW))
    number = code - view * float(TILES_VIEW)
    across = jnp.floor((number + 0.5) * (1.0 / TILES_ACROSS))
    column = number - across * float(TILES_ACROSS)
    view = view.astype(i32)
    cos_yaw = jnp.take_along_axis(cos_ref[...], view, axis=1, mode="promise_in_bounds")
    sin_yaw = jnp.take_along_axis(sin_ref[...], view, axis=1, mode="promise_in_bounds")
    centre_x = column * 16.0 + (8.0 - 960.0)
    centre_y = across * 16.0 + (8.0 - 544.0)
    return cos_yaw, sin_yaw, centre_x, centre_y


def slot_parts(slot):
    line = jnp.right_shift(slot, 7)
    high = jnp.bitwise_and(line, 31)
    low = jnp.right_shift(line, 5) * 128 + jnp.bitwise_and(slot, 127)
    return high, low


def hot_rows(low, count=256):
    return (iota((count, low.shape[1]), 0) == low).astype(f32).astype(bf16)


def ask_kernel(plan_ref, lists_ref, req_ref, out_ref, rank_ref):
    total = jnp.zeros((32, 256), f32)
    for t in range(TILES):
        high, low = slot_parts(lists_ref[t : t + 1, :])
        left = jnp.where(iota((32, LIST), 0) == high, float(t + 1), 0.0).astype(bf16)
        total = total + dot_t(left, hot_rows(low))
    tiles = jnp.concatenate([total[:, :128], total[:, 128:]], axis=0)
    named = tiles > 0.0
    a, b = iota((128, 128), 0), iota((128, 128), 1)
    earlier = jnp.logical_and(a < b, jnp.right_shift(a, 6) == jnp.right_shift(b, 6))
    rank = dot(named.astype(f32).astype(bf16), earlier.astype(f32).astype(bf16))
    rank_ref[...] = rank
    gap = jnp.bitwise_and(iota((64, 128), 1), 63) - rank.astype(i32)
    held = req_ref[...] + tiles.astype(i32) * 4096 + gap * 131072
    held = jnp.where(named, held, 0)
    for k in range(6):
        ahead = pltpu.roll(held, 128 - (1 << k), 1)
        comes = jnp.bitwise_and(jnp.right_shift(ahead, 17 + k), 1) == 1
        stays = jnp.bitwise_and(jnp.right_shift(held, 17 + k), 1) == 0
        held = jnp.where(comes, ahead, jnp.where(stays, held, 0))
    asked = jnp.bitwise_and(held, 4095)
    tile = jnp.bitwise_and(jnp.right_shift(held, 12), 31)
    codes = jnp.full((64, 128), -1, i32)
    for t in range(TILES):
        codes = jnp.where(tile == t + 1, plan_ref[t], codes)
    first = iota((64, 128), 1) < 64
    out_ref[pl.ds(0, 64, stride=2), :] = jnp.where(first, asked, pltpu.roll(codes, 64, 1))
    out_ref[pl.ds(1, 64, stride=2), :] = jnp.where(first, pltpu.roll(asked, 64, 1), codes)


def relist_kernel(lists_ref, rank_ref, out_ref, hots_ref):
    rank = rank_ref[...]
    table = jnp.concatenate([rank[:32], rank[32:]], axis=1).astype(bf16)

    def tile(t, _):
        slot = lists_ref[pl.ds(t, 1), :]
        high, low = slot_parts(slot)
        found = jnp.where(iota((32, LIST), 0) == high, dot(table, hot_rows(low)), 0.0)
        place = jnp.sum(found, axis=0, keepdims=True).astype(i32)
        slot = slot - jnp.bitwise_and(slot, 63) + place
        out_ref[pl.ds(t, 1), :] = slot
        hots_ref[t] = hot_rows(slot_parts(slot)[1])
        return 0

    lax.fori_loop(0, TILES, tile, 0, unroll=4)


def turn_kernel(params_ref, out_ref):
    for h in range(16):
        block = params_ref[:, h * 256 : (h + 1) * 256]
        out_ref[h * 256 : (h + 1) * 256, :] = jnp.transpose(jnp.concatenate([block, block], axis=0))


FRONT = 32


def list_beyond(came, out_ref):
    lane = iota((128, 128), 1)
    used = jnp.where(jnp.logical_and(lane >= 64, came >= 0), 1.0, 0.0)
    count = jnp.broadcast_to(jnp.sum(used, axis=1, keepdims=True), (128, 128)).astype(i32)
    eights = jnp.right_shift(jnp.maximum(count - FRONT, 0) + 7, 3).astype(f32)
    upto = (lane <= iota((128, 128), 0)).astype(f32).astype(bf16)
    ends = dot(upto, eights.astype(bf16))
    for c in range(4):
        place = (iota((128, 128), 1) + c * 128).astype(f32)
        past = ends <= place
        asker = jnp.sum(jnp.where(past, 1.0, 0.0), axis=0, keepdims=True)
        begun = jnp.sum(jnp.where(past, eights, 0.0), axis=0, keepdims=True)
        slot = FRONT + 8.0 * (place[0:1] - begun)
        row = iota((8, 128), 0)
        lines = jnp.where(row == 0, asker, jnp.where(row == 1, slot, ends[127:128]))
        out_ref[:, c * 128 : (c + 1) * 128] = lines.astype(i32)


def answer_kernel(
    came_ref, turned_ref, cos_ref, sin_ref, out_ref, slots_ref, codes_ref, places_ref, beyond_ref,
    over, values, index_s, beyond_s, index_sem, beyond_sem,
):
    index_copy = pltpu.make_async_copy(came_ref, index_s, index_sem)
    index_copy.start()
    came = came_ref[...]
    list_beyond(came, beyond_ref)
    beyond_copy = pltpu.make_async_copy(beyond_ref, beyond_s, beyond_sem)
    beyond_copy.start()
    codes_ref[...] = jnp.transpose(came.astype(f32))[64:128].astype(i32)
    spare = OWN + jnp.bitwise_and(iota((128, 128), 1), 7)
    places_ref[...] = jnp.where(pltpu.roll(came, 64, 1) < 0, spare, came)
    index_copy.wait()

    def fetch(step, _):
        for k in range(2):
            p = 2 * step + k
            for j in range(FRONT):
                over[pl.ds(p * FRONT + j, 1), :] = turned_ref[pl.ds(index_s[p, j], 1), :]
        return 0

    lax.fori_loop(0, 64, fetch, 0)
    beyond_copy.wait()
    first = iota((1, 128), 1) < 64

    def fetch_beyond(k, _):
        p, slot = beyond_s[0, k], beyond_s[1, k]
        for j in range(8):
            at = p * FRONT + slot - FRONT + j
            row = turned_ref[pl.ds(index_s[p, slot + j], 1), :]
            over[pl.ds(at, 1), :] = jnp.where(first, over[pl.ds(at, 1), :], row)
        return 0

    lax.fori_loop(0, beyond_s[2, 0], fetch_beyond, 0)

    def spread(step, _):
        for k in range(4):
            j = step * 4 + k
            turned = jnp.transpose(over[pl.ds(j, 128, stride=FRONT), :])
            for g in range(8):
                slots_ref[pl.ds(g * 512 + j, 8, stride=64), :] = turned[g * 8 : g * 8 + 8]
                slots_ref[pl.ds(g * 512 + j + 32, 8, stride=64), :] = turned[
                    64 + g * 8 : 72 + g * 8
                ]
        return 0

    lax.fori_loop(0, 8, spread, 0)

    def work(g, _):
        at = pl.multiple_of(g * 8, 8)
        rows = [slots_ref[pl.ds(pl.multiple_of(r * 64 + at, 8), 8), :] for r in range(PARAM)]
        camera = camera_of(codes_ref[pl.ds(at, 8), :], cos_ref, sin_ref)
        for q, value in enumerate(project_slots(rows, *camera)):
            values[pl.ds(pl.multiple_of(q * 64 + at, 8), 8), :] = value
        return 0

    values[SENT * 64 :, :] = jnp.zeros((64, 128), f32)
    lax.fori_loop(0, 8, work, 0)
    for line in range(LINES):
        block = values[line * 128 : (line + 1) * 128, :]
        out_ref[pl.ds(line, 128, stride=LINES), :] = jnp.transpose(block)


def monomials(x, y, which):
    out = jnp.zeros(x.shape, f32)
    for k, value in enumerate((jnp.ones_like(x), x, y, x * x, x * y, y * y)):
        out = jnp.where(which == k, value, out)
    return out


def render_kernel(
    came_ref, lists_ref, hots, targets_ref, out_ref,
    table, back, coefs0, coefs1, spread0, spread1, *work_refs,
):
    coefs, spreads = (coefs0, coefs1), (spread0, spread1)
    first = iota((64, 128), 1) < 64
    for q in range(SENT):
        line = q // 2
        even = came_ref[pl.ds(line, 64, stride=10), :]
        odd = came_ref[pl.ds(5 + line, 64, stride=10), :]
        if q % 2 == 0:
            dense = jnp.where(first, even, pltpu.roll(odd, 64, 1))
        else:
            dense = jnp.where(first, pltpu.roll(even, 64, 1), odd)
        square = jnp.concatenate([dense[:32], dense[32:]], axis=1)
        for s, part in enumerate(pieces(square, 3 if q < 6 else 2)):
            table[pl.ds(s * 288 + q * 32, 32), :] = part
    back[...] = jnp.zeros_like(back)
    spread1[...] = jnp.zeros_like(spread1)
    works = (work_refs[:6], work_refs[6:])
    for refs in works:
        refs[5][...] = jnp.zeros((LIST, 128), f32)
    row = iota((32, PIX), 0)
    pix = iota((32, PIX), 1)
    basis = monomials(
        jnp.bitwise_and(pix, 15).astype(f32) - 7.5,
        jnp.right_shift(pix, 4).astype(f32) - 7.5,
        jnp.where(row < 24, jnp.bitwise_and(row, 7), 7),
    ).astype(bf16)
    sub = iota((8, PIX), 0)
    lane = iota((8, 128), 1)
    offset_x = jnp.bitwise_and(lane, 15).astype(f32) - 7.5
    offset_y = jnp.right_shift(lane, 4).astype(f32) - 3.5
    square_y = offset_y * offset_y + 16.0
    eight_y = offset_y * 8.0

    def here_of(t):
        return iota((32, LIST), 0) == slot_parts(lists_ref[pl.ds(t, 1), :])[0]

    def gather(t, to):
        found = dot(table[...], hots[t])
        here = here_of(t)
        values = []
        for q in range(SENT):
            at = q * 32
            value = found[at : at + 32] + (
                found[288 + at : 320 + at] + found[576 + at : 608 + at]
                if q < 6
                else found[288 + at : 320 + at]
            )
            values.append(jnp.sum(jnp.where(here, value, 0.0), axis=0, keepdims=True))
        shape_rows = jnp.zeros((8, LIST), f32)
        color_rows = jnp.zeros((8, LIST), f32)
        for q in range(6):
            shape_rows = jnp.where(sub == q, values[q], shape_rows)
        for q in range(3):
            color_rows = jnp.where(sub == q, values[6 + q], color_rows)
        parts = [p.astype(f32) for p in pieces(shape_rows, 3)]
        stack = jnp.concatenate(parts + [color_rows] + [jnp.zeros((96, LIST), f32)], axis=0)
        to[...] = jnp.transpose(stack)

    def scatter(t, source):
        here = here_of(t)
        parts = [p.astype(f32) for p in pieces(source[...], 3)]
        left = []
        for s in range(3):
            for q in range(SENT if s < 2 else 6):
                value = jnp.broadcast_to(parts[s][q : q + 1], (32, LIST))
                left.append(jnp.where(here, value, 0.0).astype(bf16))
        moved = dot_t(jnp.concatenate(left, axis=0), hots[t])
        back[0:192] += moved[0:192] + (moved[288:480] + moved[576:768])
        back[192:288] += moved[192:288] + moved[480:576]

    def scan8(x, neutral, op, down):
        def shift(y, n):
            if down:
                return jnp.where(sub >= n, pltpu.roll(y, n, 0), neutral)
            return jnp.where(sub < 8 - n, pltpu.roll(y, 8 - n, 0), neutral)

        x = shift(x, 1)
        for n in (1, 2, 4):
            x = op(x, shift(x, n))
        return x

    def compose(t, source, to, refs):
        alphas, before, weights, gains, behind, sums = refs
        exponent = dot(source[:, 0:32].astype(bf16), basis)
        product = jnp.ones((8, PIX), f32)
        for v in range(32):
            rows = slice(v * 8, v * 8 + 8)
            alpha = jnp.exp(exponent[rows])
            alphas[rows] = alpha
            before[rows] = product
            product = product * (1.0 - alpha)
        ahead = scan8(product, 1.0, jnp.multiply, True)
        seen = [jnp.zeros((8, PIX), f32) for _ in range(3)]
        for v in range(32):
            rows = slice(v * 8, v * 8 + 8)
            weight = alphas[rows] * (before[rows] * ahead)
            weights[rows] = weight
            for c in range(3):
                seen[c] = seen[c] + weight * source[rows, 24 + c : 25 + c]
        pulls = []
        for c in range(3):
            total = jnp.sum(seen[c], axis=0, keepdims=True)
            pull = (total - targets_ref[t, c : c + 1, :]) * (1.0 / loss_scale)
            pulls.append(jnp.broadcast_to(pull, (8, PIX)))
        rest = jnp.zeros((8, PIX), f32)
        for v in reversed(range(32)):
            rows = slice(v * 8, v * 8 + 8)
            weight = weights[rows]
            gain = pulls[0] * source[rows, 24:25]
            gain = gain + pulls[1] * source[rows, 25:26]
            gain = gain + pulls[2] * source[rows, 26:27]
            gain = gain * weight
            gains[rows] = gain
            behind[rows] = rest
            rest = rest + gain
            line = jnp.zeros((8, 128), f32)
            for c in range(3):
                tint = weight * pulls[c]
                tint = jnp.sum(tint[:, :128] + tint[:, 128:], axis=1, keepdims=True)
                line = jnp.where(lane == 6 + c, tint, line)
            sums[rows, :] = line
        after = scan8(rest, 0.0, jnp.add, False)
        for v in range(32):
            rows = slice(v * 8, v * 8 + 8)
            alpha = alphas[rows]
            slope = gains[rows] - (behind[rows] + after) * (alpha / (1.0 - alpha))
            upper, lower = slope[:, :128], slope[:, 128:]
            both, apart = upper + lower, lower - upper
            along = both * offset_x
            down = both * offset_y + apart * 4.0
            line = sums[rows, :]
            for k, value in enumerate(
                (both, along, down, along * offset_x, down * offset_x,
                 both * square_y + apart * eight_y)
            ):
                line = jnp.where(lane == k, jnp.sum(value, axis=1, keepdims=True), line)
            sums[rows, :] = line
        to[...] = jnp.transpose(sums[...])[0:16]

    gather(0, coefs[0])

    def pair(step, _):
        for k in range(2):
            t = 2 * step + k
            gather(jnp.minimum(t + 1, TILES - 1), coefs[1 - k])
            compose(t, coefs[k], spreads[k], works[k])
            scatter(jnp.maximum(t - 1, 0), spreads[1 - k])
        return 0

    lax.fori_loop(0, TILES // 2, pair, 0)
    scatter(TILES - 1, spreads[1])

    zero = jnp.zeros((64, 128), f32)

    def dense_of(q):
        if q >= SENT:
            return zero
        square = back[pl.ds(q * 32, 32), :]
        return jnp.concatenate([square[:, :128], square[:, 128:]], axis=0)

    for line in range(LINES):
        a, b = dense_of(2 * line), dense_of(2 * line + 1)
        out_ref[pl.ds(line, 64, stride=10), :] = jnp.where(first, a, pltpu.roll(b, 64, 1))
        out_ref[pl.ds(5 + line, 64, stride=10), :] = jnp.where(first, pltpu.roll(a, 64, 1), b)


def rates(shape):
    row = iota(shape, 0)
    out = jnp.full(shape, 0.000125, f32)
    for end, rate in ((14, 0.0025), (11, 0.05), (10, 0.001), (6, 0.005), (3, 0.0008)):
        out = jnp.where(row < end, rate, out)
    return out


def update_kernel(
    back_ref, places_ref, beyond_ref, slots_ref, codes_ref, cos_ref, sin_ref,
    params_ref, first_ref, second_ref, new_params_ref, new_first_ref, new_second_ref,
    cots, grads, over, even, odd, rest, index_s, beyond_s, index_sem, beyond_sem,
):
    index_copy = pltpu.make_async_copy(places_ref, index_s, index_sem)
    beyond_copy = pltpu.make_async_copy(beyond_ref, beyond_s, beyond_sem)
    index_copy.start()
    beyond_copy.start()
    for line in range(LINES):
        block = back_ref[pl.ds(line, 128, stride=LINES), :]
        cots[line * 128 : (line + 1) * 128, :] = jnp.transpose(block)
    for r in range(PARAM, 64):
        grads[pl.ds(r * 64, 64), :] = jnp.zeros((64, 128), f32)

    def work(g, _):
        at = pl.multiple_of(g * 8, 8)
        rows = [slots_ref[pl.ds(pl.multiple_of(r * 64 + at, 8), 8), :] for r in range(PARAM)]
        camera = camera_of(codes_ref[pl.ds(at, 8), :], cos_ref, sin_ref)
        _, pullback = jax.vjp(lambda r: project_slots(r, *camera), rows)
        (out,) = pullback(
            [cots[pl.ds(pl.multiple_of(q * 64 + at, 8), 8), :] for q in range(SENT)]
        )
        for r in range(PARAM):
            grads[pl.ds(pl.multiple_of(r * 64 + at, 8), 8), :] = out[r]
        return 0

    lax.fori_loop(0, 8, work, 0)
    for sums in (even, odd, rest):
        sums[...] = jnp.zeros_like(sums)

    def value_of(line):
        return [grads[pl.ds(g * 512 + line, 8, stride=64), :] for g in range(8)]

    def spread(step, _):
        for k in range(4):
            j = step * 4 + k
            block = jnp.concatenate(value_of(j) + value_of(j + 32), axis=0)
            over[pl.ds(j, 128, stride=FRONT), :] = jnp.transpose(block)
        return 0

    lax.fori_loop(0, 8, spread, 0)
    index_copy.wait()
    beyond_copy.wait()

    def add_eight(sums, p, slot, at):
        old = [sums[pl.ds(index_s[p, slot + n], 1), :] for n in range(8)]
        new = [old[n] + over[pl.ds(at + n, 1), :] for n in range(8)]
        for n in range(8):
            sums[pl.ds(index_s[p, slot + n], 1), :] = new[n]

    def gather(step, _):
        for j in range(0, FRONT, 8):
            add_eight(even, 2 * step, j, 2 * step * FRONT + j)
            add_eight(odd, 2 * step + 1, j, (2 * step + 1) * FRONT + j)
        return 0

    lax.fori_loop(0, 64, gather, 0)

    def gather_beyond(k, _):
        p, slot = beyond_s[0, k], beyond_s[1, k]
        add_eight(rest, p, slot, p * FRONT + slot - FRONT)
        return 0

    lax.fori_loop(0, beyond_s[2, 0], gather_beyond, 0)
    first = iota((256, 128), 1) < 64
    bias_one = 1.0 - beta_one**STEP
    bias_two = 1.0 - beta_two**STEP
    rate = rates((PARAM, 256)) * (1.0 / bias_one)
    for h in range(16):
        cols = slice(h * 256, (h + 1) * 256)
        both = jnp.transpose(jnp.where(first, even[cols, :] + odd[cols, :], rest[cols, :]))
        gradient = both[:PARAM] + both[64 : 64 + PARAM]
        first_new = beta_one * first_ref[:, cols] + (1.0 - beta_one) * gradient
        second_new = beta_two * second_ref[:, cols] + (1.0 - beta_two) * gradient * gradient
        new_first_ref[:, cols] = first_new
        new_second_ref[:, cols] = second_new
        new_params_ref[:, cols] = params_ref[:, cols] - rate * first_new / (
            jnp.sqrt(second_new * (1.0 / bias_two)) + adam_eps
        )


def shape(rows, cols, dtype=f32):
    return jax.ShapeDtypeStruct((rows, cols), dtype)


def exchange(lines, count):
    sent = lines.reshape(128, 1, count * 128)
    came = lax.all_to_all(sent, AXES, split_axis=0, concat_axis=0, tiled=True)
    return came.reshape(128 * count, 128)


def shards(params, adam_first, adam_second, view_yaw, tile_plan, tile_lists, requests, targets):
    cos_yaw = jnp.broadcast_to(jnp.pad(jnp.cos(view_yaw), (0, 96))[None, :], (8, 128))
    sin_yaw = jnp.broadcast_to(jnp.pad(jnp.sin(view_yaw), (0, 96))[None, :], (8, 128))
    woven = jnp.transpose(tile_lists.reshape(TILES, 8, 32), (0, 2, 1)).reshape(TILES, LIST)
    asked, rank = call(
        ask_kernel, (shape(128, 128, i32), shape(64, 128)), "ask", in_specs=[SM, VM, VM]
    )(tile_plan, tile_lists, requests.reshape(64, 128))
    came = exchange(asked, 1)
    turned = call(turn_kernel, shape(OWN, 128), "turn", in_specs=[VM])(
        jnp.pad(params, ((0, 64 - PARAM), (0, 0)))
    )
    lists, hots = call(
        relist_kernel,
        (shape(TILES, LIST, i32), jax.ShapeDtypeStruct((TILES, 256, LIST), bf16)),
        "relist",
        in_specs=[VM, VM],
    )(woven, rank)
    aims = jnp.pad(jnp.transpose(targets, (1, 0, 2)), ((0, 0), (0, 5), (0, 0)))
    indexes = [
        pltpu.SMEM((128, 128), i32),
        pltpu.SMEM((8, 512), i32),
        pltpu.SemaphoreType.DMA,
        pltpu.SemaphoreType.DMA,
    ]
    answers, slots, codes, places, beyond = call(
        answer_kernel,
        (
            shape(128 * LINES, 128),
            shape(64 * 64, 128),
            shape(64, 128, i32),
            shape(128, 128, i32),
            shape(8, 512, i32),
        ),
        "answer",
        scratch=[pltpu.VMEM((OWN, 128), f32), pltpu.VMEM((128 * LINES, 128), f32)] + indexes,
        in_specs=[VM] * 4,
        flops=4_500_000_000,
    )(came, turned, cos_yaw, sin_yaw)
    arrived = exchange(answers, LINES)
    wide = pltpu.VMEM((LIST, PIX), f32)
    narrow = pltpu.VMEM((LIST, 128), f32)
    returned = call(
        render_kernel,
        shape(128 * LINES, 128),
        "render",
        scratch=[pltpu.VMEM((768, 256), bf16), pltpu.VMEM((288, 256), f32), narrow, narrow]
        + [pltpu.VMEM((16, LIST), f32)] * 2
        + ([wide] * 5 + [narrow]) * 2,
        in_specs=[VM] * 4,
        flops=5_000_000_000,
    )(arrived, lists, hots, aims)
    back = exchange(returned, LINES)
    return call(
        update_kernel,
        (shape(PARAM, OWN), shape(PARAM, OWN), shape(PARAM, OWN)),
        "update",
        scratch=[
            pltpu.VMEM((128 * LINES, 128), f32),
            pltpu.VMEM((64 * 64, 128), f32),
            pltpu.VMEM((OWN, 128), f32),
        ]
        + [pltpu.VMEM((OWN + 8, 128), f32)] * 3
        + indexes,
        in_specs=[VM] * 10,
        flops=4_500_000_000,
        mib=24,
    )(back, places, beyond, slots, codes, cos_yaw, sin_yaw, params, adam_first, adam_second)


def solution(mesh):
    placed = (
        P(None, AXES),
        P(None, AXES),
        P(None, AXES),
        P(),
        P(AXES),
        P(AXES, None),
        P(AXES, None),
        P(None, AXES, None),
    )
    return jax.shard_map(
        shards,
        mesh=mesh,
        in_specs=placed,
        out_specs=(P(None, AXES), P(None, AXES), P(None, AXES)),
        check_vma=False,
    )
```

```python
from functools import partial

import jax
import jax.numpy as jnp
from jax import lax
from jax.experimental import pallas as pl
from jax.experimental.pallas import tpu as pltpu
from jax.sharding import PartitionSpec as P

AXES = ("img", "blk")
STEP = 1000
TILES_ACROSS = 120
TILES_VIEW = 8160
TILE_EDGE = 16
PARAM = 59
OWN = 4096
SLOTS = 8192
TILES = 16
LIST = 256
PIX = 256
SENT = 9
LINES = 5

focal_px = 2400.0
camera_distance = 10.0
low_pass = 0.3
loss_scale = 16.0
beta_one = 0.9
beta_two = 0.999
adam_eps = 1e-08
band_zero = 0.28209479177387814
band_one = 0.4886025119029199
band_two = (
    1.0925484305920792,
    -1.0925484305920792,
    0.31539156525252005,
    -1.0925484305920792,
    0.5462742152960396,
)
band_three = (
    -0.5900435899266435,
    2.890611442640554,
    -0.4570457994644658,
    0.3731763325901154,
    -0.4570457994644658,
    1.445305721320277,
    -0.5900435899266435,
)
f32 = jnp.float32
bf16 = jnp.bfloat16
i32 = jnp.int32
VM = pl.BlockSpec(memory_space=pltpu.VMEM)
SM = pl.BlockSpec(memory_space=pltpu.SMEM)
HB = pl.BlockSpec(memory_space=pltpu.HBM)


def iota(shape, dim):
    return lax.broadcasted_iota(i32, shape, dim)


def dot(a, b):
    return lax.dot_general(a, b, (((1,), (0,)), ((), ())), preferred_element_type=f32)


def dot_t(a, b):
    return lax.dot_general(a, b, (((1,), (1,)), ((), ())), preferred_element_type=f32)


def pieces(x, count):
    out = []
    for k in range(count):
        part = x.astype(bf16)
        out.append(part)
        if k + 1 < count:
            x = x - part.astype(f32)
    return out


def call(kernel, out_shape, name, scratch=(), in_specs=None, out_specs=None, flops=0, mib=16):
    return partial(
        pl.pallas_call,
        kernel,
        out_shape=out_shape,
        in_specs=in_specs,
        out_specs=out_specs or jax.tree.map(lambda _: VM, out_shape),
        scratch_shapes=list(scratch),
        name=name,
        cost_estimate=pl.CostEstimate(flops=flops, bytes_accessed=4 << 20, transcendentals=0),
        compiler_params=pltpu.CompilerParams(vmem_limit_bytes=mib << 20),
    )()


def harmonics(looking_x, look_y, look_z):
    square_x = looking_x * looking_x
    square_y = look_y * look_y
    square_z = look_z * look_z
    return [
        jnp.full_like(looking_x, band_zero),
        -band_one * look_y,
        band_one * look_z,
        -band_one * looking_x,
        band_two[0] * looking_x * look_y,
        band_two[1] * look_y * look_z,
        band_two[2] * (2.0 * square_z - square_x - square_y),
        band_two[3] * looking_x * look_z,
        band_two[4] * (square_x - square_y),
        band_three[0] * look_y * (3.0 * square_x - square_y),
        band_three[1] * looking_x * look_y * look_z,
        band_three[2] * look_y * (4.0 * square_z - square_x - square_y),
        band_three[3] * look_z * (2.0 * square_z - 3.0 * square_x - 3.0 * square_y),
        band_three[4] * looking_x * (4.0 * square_z - square_x - square_y),
        band_three[5] * look_z * (square_x - square_y),
        band_three[6] * looking_x * (square_x - 3.0 * square_y),
    ]


def project_slots(rows, cos_yaw, sin_yaw, centre_x, centre_y):
    world_x, world_y, world_z = rows[0], rows[1], rows[2]
    view_x = cos_yaw * world_x + sin_yaw * world_z
    view_z = cos_yaw * world_z - sin_yaw * world_x + camera_distance
    inverse_z = 1.0 / view_z
    mean_x = focal_px * view_x * inverse_z - centre_x
    mean_y = focal_px * world_y * inverse_z - centre_y
    scales = [jnp.exp(rows[3 + k]) for k in range(3)]
    norm = jnp.sqrt(
        rows[6] * rows[6] + rows[7] * rows[7] + rows[8] * rows[8] + rows[9] * rows[9]
    )
    inverse_norm = 1.0 / norm
    quat_w, quat_x, quat_y, quat_z = [rows[6 + k] * inverse_norm for k in range(4)]
    rotation = [
        [
            1.0 - 2.0 * (quat_y * quat_y + quat_z * quat_z),
            2.0 * (quat_x * quat_y - quat_w * quat_z),
            2.0 * (quat_x * quat_z + quat_w * quat_y),
        ],
        [
            2.0 * (quat_x * quat_y + quat_w * quat_z),
            1.0 - 2.0 * (quat_x * quat_x + quat_z * quat_z),
            2.0 * (quat_y * quat_z - quat_w * quat_x),
        ],
        [
            2.0 * (quat_x * quat_z - quat_w * quat_y),
            2.0 * (quat_y * quat_z + quat_w * quat_x),
            1.0 - 2.0 * (quat_x * quat_x + quat_y * quat_y),
        ],
    ]
    focal_z = focal_px * inverse_z
    shear_x = focal_z * view_x * inverse_z
    shear_y = focal_z * world_y * inverse_z
    jacob_ax = focal_z * cos_yaw + shear_x * sin_yaw
    jacob_az = focal_z * sin_yaw - shear_x * cos_yaw
    jacob_bx = shear_y * sin_yaw
    jacob_bz = -shear_y * cos_yaw
    row_a = [
        (jacob_ax * rotation[0][k] + jacob_az * rotation[2][k]) * scales[k] for k in range(3)
    ]
    row_b = [
        (jacob_bx * rotation[0][k] + focal_z * rotation[1][k] + jacob_bz * rotation[2][k])
        * scales[k]
        for k in range(3)
    ]
    covar_xx = row_a[0] * row_a[0] + row_a[1] * row_a[1] + row_a[2] * row_a[2] + low_pass
    covar_yy = row_b[0] * row_b[0] + row_b[1] * row_b[1] + row_b[2] * row_b[2] + low_pass
    covar_xy = row_a[0] * row_b[0] + row_a[1] * row_b[1] + row_a[2] * row_b[2]
    inverse_det = 1.0 / (covar_xx * covar_yy - covar_xy * covar_xy)
    conic_a = covar_yy * inverse_det
    conic_b = -covar_xy * inverse_det
    conic_c = covar_xx * inverse_det
    log_opacity = rows[10] - jnp.log(1.0 + jnp.exp(rows[10]))
    slope_x = conic_a * mean_x + conic_b * mean_y
    slope_y = conic_c * mean_y + conic_b * mean_x
    constant = log_opacity - 0.5 * (slope_x * mean_x + slope_y * mean_y)
    inverse_len = 1.0 / jnp.sqrt(view_x * view_x + world_y * world_y + view_z * view_z)
    basis = harmonics(
        (cos_yaw * view_x - sin_yaw * view_z) * inverse_len,
        world_y * inverse_len,
        (sin_yaw * view_x + cos_yaw * view_z) * inverse_len,
    )
    colors = []
    for channel in range(3):
        total = basis[0] * rows[11 + channel]
        for degree in range(1, 16):
            total = total + basis[degree] * rows[11 + 3 * degree + channel]
        colors.append(jnp.maximum(0.5 + total, 0.0))
    return [
        constant,
        slope_x,
        slope_y,
        -0.5 * conic_a,
        -conic_b,
        -0.5 * conic_c,
    ] + colors


def camera_of(codes, cos_ref, sin_ref):
    code = jnp.maximum(codes, 0).astype(f32)
    view = jnp.floor((code + 0.5) * (1.0 / TILES_VIEW))
    number = code - view * float(TILES_VIEW)
    across = jnp.floor((number + 0.5) * (1.0 / TILES_ACROSS))
    column = number - across * float(TILES_ACROSS)
    view = view.astype(i32)
    cos_yaw = jnp.take_along_axis(cos_ref[...], view, axis=1, mode="promise_in_bounds")
    sin_yaw = jnp.take_along_axis(sin_ref[...], view, axis=1, mode="promise_in_bounds")
    centre_x = column * 16.0 + (8.0 - 960.0)
    centre_y = across * 16.0 + (8.0 - 544.0)
    return cos_yaw, sin_yaw, centre_x, centre_y


def slot_parts(slot):
    line = jnp.right_shift(slot, 7)
    high = jnp.bitwise_and(line, 31)
    low = jnp.right_shift(line, 5) * 128 + jnp.bitwise_and(slot, 127)
    return high, low


def hot_rows(low, count=256):
    return (iota((count, low.shape[1]), 0) == low).astype(f32).astype(bf16)


def ask_kernel(plan_any, lists_any, req_any, out_ref, rank_ref, plan_ref, lists_ref, req_ref, sems):
    copies = [
        pltpu.make_async_copy(source, to, sems.at[k])
        for k, (source, to) in enumerate(
            ((lists_any, lists_ref), (plan_any, plan_ref), (req_any, req_ref))
        )
    ]
    for copy in copies:
        copy.start()
    copies[0].wait()
    total = jnp.zeros((32, 256), f32)
    for t in range(TILES):
        high, low = slot_parts(lists_ref[t : t + 1, :])
        left = jnp.where(iota((32, LIST), 0) == high, float(t + 1), 0.0).astype(bf16)
        total = total + dot_t(left, hot_rows(low))
    tiles = jnp.concatenate([total[:, :128], total[:, 128:]], axis=0)
    named = tiles > 0.0
    a, b = iota((128, 128), 0), iota((128, 128), 1)
    earlier = jnp.logical_and(a < b, jnp.right_shift(a, 6) == jnp.right_shift(b, 6))
    rank = dot(named.astype(f32).astype(bf16), earlier.astype(f32).astype(bf16))
    rank_ref[...] = rank
    gap = jnp.bitwise_and(iota((64, 128), 1), 63) - rank.astype(i32)
    copies[1].wait()
    copies[2].wait()
    held = req_ref[...] + tiles.astype(i32) * 4096 + gap * 131072
    held = jnp.where(named, held, 0)
    for k in range(6):
        ahead = pltpu.roll(held, 128 - (1 << k), 1)
        comes = jnp.bitwise_and(jnp.right_shift(ahead, 17 + k), 1) == 1
        stays = jnp.bitwise_and(jnp.right_shift(held, 17 + k), 1) == 0
        held = jnp.where(comes, ahead, jnp.where(stays, held, 0))
    asked = jnp.bitwise_and(held, 4095)
    tile = jnp.bitwise_and(jnp.right_shift(held, 12), 31)
    codes = jnp.full((64, 128), -1, i32)
    for t in range(TILES):
        codes = jnp.where(tile == t + 1, plan_ref[t], codes)
    first = iota((64, 128), 1) < 64
    out_ref[pl.ds(0, 64, stride=2), :] = jnp.where(first, asked, pltpu.roll(codes, 64, 1))
    out_ref[pl.ds(1, 64, stride=2), :] = jnp.where(first, pltpu.roll(asked, 64, 1), codes)


def relist_kernel(lists_ref, rank_ref, out_ref):
    rank = rank_ref[...]
    table = jnp.concatenate([rank[:32], rank[32:]], axis=1).astype(bf16)

    def tile(t, _):
        slot = lists_ref[pl.ds(t, 1), :]
        high, low = slot_parts(slot)
        found = jnp.where(iota((32, LIST), 0) == high, dot(table, hot_rows(low)), 0.0)
        place = jnp.sum(found, axis=0, keepdims=True).astype(i32)
        out_ref[pl.ds(t, 1), :] = slot - jnp.bitwise_and(slot, 63) + place
        return 0

    lax.fori_loop(0, TILES, tile, 0, unroll=4)


def turn_kernel(params_ref, out_ref):
    for h in range(16):
        block = params_ref[:, h * 256 : (h + 1) * 256]
        out_ref[h * 256 : (h + 1) * 256, :] = jnp.transpose(jnp.concatenate([block, block], axis=0))


FRONT = 32


def list_beyond(came, out_ref):
    lane = iota((128, 128), 1)
    used = jnp.where(jnp.logical_and(lane >= 64, came >= 0), 1.0, 0.0)
    count = jnp.broadcast_to(jnp.sum(used, axis=1, keepdims=True), (128, 128)).astype(i32)
    eights = jnp.right_shift(jnp.maximum(count - FRONT, 0) + 7, 3).astype(f32)
    upto = (lane <= iota((128, 128), 0)).astype(f32).astype(bf16)
    ends = dot(upto, eights.astype(bf16))
    for c in range(4):
        place = (iota((128, 128), 1) + c * 128).astype(f32)
        past = ends <= place
        asker = jnp.sum(jnp.where(past, 1.0, 0.0), axis=0, keepdims=True)
        begun = jnp.sum(jnp.where(past, eights, 0.0), axis=0, keepdims=True)
        slot = FRONT + 8.0 * (place[0:1] - begun)
        row = iota((8, 128), 0)
        lines = jnp.where(row == 0, asker, jnp.where(row == 1, slot, ends[127:128]))
        out_ref[:, c * 128 : (c + 1) * 128] = lines.astype(i32)


def answer_kernel(
    came_ref, turned_ref, cos_ref, sin_ref, out_ref, slots_any, codes_ref, places_ref, beyond_ref,
    over, slots, values, slot_sems, index_s, beyond_s, index_sem, beyond_sem,
):
    index_copy = pltpu.make_async_copy(came_ref, index_s, index_sem)
    index_copy.start()
    came = came_ref[...]
    list_beyond(came, beyond_ref)
    beyond_copy = pltpu.make_async_copy(beyond_ref, beyond_s, beyond_sem)
    beyond_copy.start()
    codes_ref[...] = jnp.transpose(came.astype(f32))[64:128].astype(i32)
    spare = OWN + jnp.bitwise_and(iota((128, 128), 1), 7)
    places_ref[...] = jnp.where(pltpu.roll(came, 64, 1) < 0, spare, came)
    index_copy.wait()

    def fetch(step, _):
        for k in range(2):
            p = 2 * step + k
            for j in range(FRONT):
                over[pl.ds(j * 128 + p, 1), :] = turned_ref[pl.ds(index_s[p, j], 1), :]
        return 0

    lax.fori_loop(0, 64, fetch, 0)
    beyond_copy.wait()
    first = iota((1, 128), 1) < 64

    def fetch_beyond(k, _):
        p, slot = beyond_s[0, k], beyond_s[1, k]
        for j in range(8):
            at = (slot - FRONT + j) * 128 + p
            row = turned_ref[pl.ds(index_s[p, slot + j], 1), :]
            over[pl.ds(at, 1), :] = jnp.where(first, over[pl.ds(at, 1), :], row)
        return 0

    lax.fori_loop(0, beyond_s[2, 0], fetch_beyond, 0)

    def spread(step, _):
        for k in range(8):
            at = pl.multiple_of((step * 8 + k) * 128, 128)
            over[pl.ds(at, 128), :] = jnp.transpose(over[pl.ds(at, 128), :])
        return 0

    lax.fori_loop(0, FRONT // 8, spread, 0)

    def slot_copy(g):
        part = pl.ds(pl.multiple_of(g * 512, 512), 512)
        return pltpu.make_async_copy(slots.at[part], slots_any.at[part], slot_sems.at[g])

    for r in range(PARAM, 64):
        for g in range(8):
            slots[g * 512 + r * 8 : g * 512 + r * 8 + 8, :] = jnp.zeros((8, 128), f32)

    def work(g, _):
        at = pl.multiple_of(g * 8, 8)
        base = jnp.bitwise_and(g, 3) * 1024 + jnp.right_shift(g, 2) * 64
        rows = [over[pl.ds(base + r, 8, stride=128), :] for r in range(PARAM)]
        for r in range(PARAM):
            slots[pl.ds(pl.multiple_of(g * 512 + r * 8, 8), 8), :] = rows[r]
        slot_copy(g).start()
        camera = camera_of(codes_ref[pl.ds(at, 8), :], cos_ref, sin_ref)
        for q, value in enumerate(project_slots(rows, *camera)):
            values[pl.ds(pl.multiple_of(q * 64 + at, 8), 8), :] = value
        return 0

    values[SENT * 64 :, :] = jnp.zeros((64, 128), f32)
    lax.fori_loop(0, 8, work, 0)
    for line in range(LINES):
        block = values[line * 128 : (line + 1) * 128, :]
        out_ref[pl.ds(line, 128, stride=LINES), :] = jnp.transpose(block)
    for g in range(8):
        slot_copy(g).wait()


def monomials(x, y, which):
    out = jnp.zeros(x.shape, f32)
    for k, value in enumerate((jnp.ones_like(x), x, y, x * x, x * y, y * y)):
        out = jnp.where(which == k, value, out)
    return out


def render_kernel(
    came_ref, lists_ref, targets_ref, out_ref,
    table, hots, back, coefs0, coefs1, spread0, spread1, *work_refs,
):
    coefs, spreads = (coefs0, coefs1), (spread0, spread1)
    first = iota((64, 128), 1) < 64
    for q in range(SENT):
        line = q // 2
        even = came_ref[pl.ds(line, 64, stride=10), :]
        odd = came_ref[pl.ds(5 + line, 64, stride=10), :]
        if q % 2 == 0:
            dense = jnp.where(first, even, pltpu.roll(odd, 64, 1))
        else:
            dense = jnp.where(first, pltpu.roll(even, 64, 1), odd)
        square = jnp.concatenate([dense[:32], dense[32:]], axis=1)
        for s, part in enumerate(pieces(square, 3 if q < 6 else 2)):
            table[pl.ds(s * 288 + q * 32, 32), :] = part
    back[...] = jnp.zeros_like(back)
    spread1[...] = jnp.zeros_like(spread1)
    works = (work_refs[:7], work_refs[7:])
    row = iota((32, PIX), 0)
    pix = iota((32, PIX), 1)
    basis = monomials(
        jnp.bitwise_and(pix, 15).astype(f32) - 7.5,
        jnp.right_shift(pix, 4).astype(f32) - 7.5,
        jnp.where(row < 24, jnp.bitwise_and(row, 7), 7),
    ).astype(bf16)
    sub = iota((8, PIX), 0)
    lane = iota((8, 128), 1)
    offset_x = jnp.bitwise_and(lane, 15).astype(f32) - 7.5
    offset_y = jnp.right_shift(lane, 4).astype(f32) - 3.5
    square_y = offset_y * offset_y + 16.0
    eight_y = offset_y * 8.0

    def make_hot(t, _):
        hots[t] = hot_rows(slot_parts(lists_ref[pl.ds(t, 1), :])[1])
        return 0

    lax.fori_loop(0, TILES, make_hot, 0, unroll=2)

    def here_of(t):
        return iota((32, LIST), 0) == slot_parts(lists_ref[pl.ds(t, 1), :])[0]

    def gather(t, to):
        found = dot(table[...], hots[t])
        here = here_of(t)
        values = []
        for q in range(SENT):
            at = q * 32
            value = found[at : at + 32] + (
                found[288 + at : 320 + at] + found[576 + at : 608 + at]
                if q < 6
                else found[288 + at : 320 + at]
            )
            values.append(jnp.sum(jnp.where(here, value, 0.0), axis=0, keepdims=True))
        shape_rows = jnp.zeros((8, LIST), f32)
        color_rows = jnp.zeros((8, LIST), f32)
        for q in range(6):
            shape_rows = jnp.where(sub == q, values[q], shape_rows)
        for q in range(3):
            color_rows = jnp.where(sub == q, values[6 + q], color_rows)
        parts = [p.astype(f32) for p in pieces(shape_rows, 3)]
        stack = jnp.concatenate(parts + [color_rows] + [jnp.zeros((96, LIST), f32)], axis=0)
        to[...] = jnp.transpose(stack)

    def scatter(t, source):
        here = here_of(t)
        parts = [p.astype(f32) for p in pieces(source[...], 3)]
        left = []
        for s in range(3):
            for q in range(SENT if s < 2 else 6):
                value = jnp.broadcast_to(parts[s][q : q + 1], (32, LIST))
                left.append(jnp.where(here, value, 0.0).astype(bf16))
        moved = dot_t(jnp.concatenate(left, axis=0), hots[t])
        back[0:192] += moved[0:192] + (moved[288:480] + moved[576:768])
        back[192:288] += moved[192:288] + moved[480:576]

    def scan8(x, neutral, op, down):
        def shift(y, n):
            if down:
                return jnp.where(sub >= n, pltpu.roll(y, n, 0), neutral)
            return jnp.where(sub < 8 - n, pltpu.roll(y, 8 - n, 0), neutral)

        x = shift(x, 1)
        for n in (1, 2, 4):
            x = op(x, shift(x, n))
        return x

    def rows_of(v):
        return slice(v * 8, v * 8 + 8)

    def twice(x):
        return jnp.concatenate([x, x], axis=1)

    def expose(source, refs):
        refs[0][...] = dot(source[:, 0:32].astype(bf16), basis)

    def pass_light(v, refs, product):
        alphas, before = refs[0], refs[1]
        alpha = jnp.exp(alphas[rows_of(v)])
        alphas[rows_of(v)] = alpha
        before[rows_of(v)] = product
        return product * (1.0 - alpha)

    def weigh(v, source, refs, ahead, seen):
        alphas, weights, tones = refs[0], refs[1], refs[5]
        weight = alphas[rows_of(v)] * (weights[rows_of(v)] * ahead)
        weights[rows_of(v)] = weight
        out = []
        for c in range(3):
            tone = jnp.broadcast_to(source[rows_of(v), 24 + c : 25 + c], (8, 128))
            tones[c * 256 + v * 8 : c * 256 + v * 8 + 8] = tone
            out.append(seen[c] + weight * twice(tone))
        return out

    def compare(t, seen, refs):
        for c in range(3):
            total = jnp.sum(seen[c], axis=0, keepdims=True)
            pull = (total - targets_ref[t, c : c + 1, :]) * (1.0 / loss_scale)
            refs[6][c * 8 : c * 8 + 8] = jnp.broadcast_to(pull, (8, PIX))

    def pull_back(v, refs, pulls, rest):
        weights, gains, behind, sums, tones = refs[1:6]
        weight = weights[rows_of(v)]
        gain = jnp.zeros((8, PIX), f32)
        line = jnp.zeros((8, 128), f32)
        for c in range(3):
            gain = gain + pulls[c] * twice(tones[c * 256 + v * 8 : c * 256 + v * 8 + 8])
            tint = weight * pulls[c]
            tint = jnp.sum(tint[:, :128] + tint[:, 128:], axis=1, keepdims=True)
            line = jnp.where(lane == 6 + c, tint, line)
        gain = gain * weight
        gains[rows_of(v)] = gain
        behind[rows_of(v)] = rest
        sums[rows_of(v)] = line
        return rest + gain

    def moments(v, refs, after):
        alphas, gains, behind, sums = refs[0], refs[2], refs[3], refs[4]
        alpha = alphas[rows_of(v)]
        slope = behind[rows_of(v)] + after
        slope = gains[rows_of(v)] - slope * (alpha / (1.0 - alpha))
        upper, lower = slope[:, :128], slope[:, 128:]
        both, apart = upper + lower, lower - upper
        along = both * offset_x
        down = both * offset_y + apart * 4.0
        line = sums[rows_of(v)]
        for k, value in enumerate(
            (both, along, down, along * offset_x, down * offset_x,
             both * square_y + apart * eight_y)
        ):
            line = jnp.where(lane == k, jnp.sum(value, axis=1, keepdims=True), line)
        sums[rows_of(v)] = line

    one = jnp.ones((8, PIX), f32)
    nothing = jnp.zeros((8, PIX), f32)
    gather(0, coefs[0])
    gather(1, coefs[1])
    expose(coefs[0], works[0])
    product = one
    for v in range(32):
        product = pass_light(v, works[0], product)
    ahead = scan8(product, 1.0, jnp.multiply, True)
    seen = [nothing] * 3
    for v in range(32):
        seen = weigh(v, coefs[0], works[0], ahead, seen)
    compare(0, seen, works[0])

    def pair(step, _):
        for k in range(2):
            t = 2 * step + k
            coming = jnp.minimum(t + 1, TILES - 1)
            here, there = works[k], works[1 - k]
            expose(coefs[1 - k], there)
            scatter(jnp.maximum(t - 1, 0), spreads[1 - k])
            pulls = [here[6][c * 8 : c * 8 + 8] for c in range(3)]
            product, rest = one, nothing
            for v in range(32):
                product = pass_light(v, there, product)
                rest = pull_back(31 - v, here, pulls, rest)
            ahead = scan8(product, 1.0, jnp.multiply, True)
            after = scan8(rest, 0.0, jnp.add, False)
            gather(jnp.minimum(t + 2, TILES - 1), coefs[k])
            seen = [nothing] * 3
            for v in range(32):
                seen = weigh(v, coefs[1 - k], there, ahead, seen)
                moments(v, here, after)
            compare(coming, seen, there)
            spreads[k][...] = jnp.transpose(here[4][...])[0:16]
        return 0

    lax.fori_loop(0, TILES // 2, pair, 0)
    scatter(TILES - 1, spreads[1])

    zero = jnp.zeros((64, 128), f32)

    def dense_of(q):
        if q >= SENT:
            return zero
        square = back[pl.ds(q * 32, 32), :]
        return jnp.concatenate([square[:, :128], square[:, 128:]], axis=0)

    for line in range(LINES):
        a, b = dense_of(2 * line), dense_of(2 * line + 1)
        out_ref[pl.ds(line, 64, stride=10), :] = jnp.where(first, a, pltpu.roll(b, 64, 1))
        out_ref[pl.ds(5 + line, 64, stride=10), :] = jnp.where(first, pltpu.roll(a, 64, 1), b)


def rates(shape):
    row = iota(shape, 0)
    out = jnp.full(shape, 0.000125, f32)
    for end, rate in ((14, 0.0025), (11, 0.05), (10, 0.001), (6, 0.005), (3, 0.0008)):
        out = jnp.where(row < end, rate, out)
    return out


def update_kernel(
    back_ref, places_ref, beyond_ref, slots_ref, codes_ref, cos_ref, sin_ref,
    params_ref, first_ref, second_ref, new_params_any, new_first_any, new_second_any,
    new_params_ref, new_first_ref, new_second_ref, out_sems,
    cots, grads, over, even, odd, rest, index_s, beyond_s, index_sem, beyond_sem,
):
    index_copy = pltpu.make_async_copy(places_ref, index_s, index_sem)
    beyond_copy = pltpu.make_async_copy(beyond_ref, beyond_s, beyond_sem)
    index_copy.start()
    beyond_copy.start()
    for line in range(LINES):
        block = back_ref[pl.ds(line, 128, stride=LINES), :]
        cots[line * 128 : (line + 1) * 128, :] = jnp.transpose(block)
    for r in range(PARAM, 64):
        for g in range(8):
            grads[g * 512 + r * 8 : g * 512 + r * 8 + 8, :] = jnp.zeros((8, 128), f32)

    def work(g, _):
        at = pl.multiple_of(g * 8, 8)
        lines = [pl.ds(pl.multiple_of(g * 512 + r * 8, 8), 8) for r in range(PARAM)]
        camera = camera_of(codes_ref[pl.ds(at, 8), :], cos_ref, sin_ref)
        _, pullback = jax.vjp(
            lambda r: project_slots(r, *camera), [slots_ref[line, :] for line in lines]
        )
        (out,) = pullback(
            [cots[pl.ds(pl.multiple_of(q * 64 + at, 8), 8), :] for q in range(SENT)]
        )
        for r in range(PARAM):
            grads[lines[r], :] = out[r]
        return 0

    lax.fori_loop(0, 8, work, 0)
    for sums in (even, odd, rest):
        sums[...] = jnp.zeros_like(sums)

    def spread(g, _):
        for k in range(8):
            block = [
                grads[pl.ds((g + half) * 512 + k + m * 64, 8, stride=8), :]
                for half in (0, 4)
                for m in range(8)
            ]
            at = pl.multiple_of((g * 8 + k) * 128, 128)
            over[pl.ds(at, 128), :] = jnp.transpose(jnp.concatenate(block, axis=0))
        return 0

    lax.fori_loop(0, FRONT // 8, spread, 0)
    index_copy.wait()
    beyond_copy.wait()

    def add_eight(sums, p, slot, line):
        at = [pl.ds(index_s[p, slot + n], 1) for n in range(8)]
        new = [sums[at[n], :] + over[pl.ds((line + n) * 128 + p, 1), :] for n in range(8)]
        for n in range(8):
            sums[at[n], :] = new[n]

    def gather(step, _):
        for j in range(0, FRONT, 8):
            add_eight(even, 2 * step, j, j)
            add_eight(odd, 2 * step + 1, j, j)
        return 0

    lax.fori_loop(0, 64, gather, 0)

    def gather_beyond(k, _):
        p, slot = beyond_s[0, k], beyond_s[1, k]
        add_eight(rest, p, slot, slot - FRONT)
        return 0

    lax.fori_loop(0, beyond_s[2, 0], gather_beyond, 0)
    first = iota((256, 128), 1) < 64
    bias_one = 1.0 - beta_one**STEP
    bias_two = 1.0 - beta_two**STEP
    rate = rates((PARAM, 256)) * (1.0 / bias_one)
    pending = []
    for h in range(16):
        cols = slice(h * 256, (h + 1) * 256)
        both = jnp.transpose(jnp.where(first, even[cols, :] + odd[cols, :], rest[cols, :]))
        gradient = both[:PARAM] + both[64 : 64 + PARAM]
        first_new = beta_one * first_ref[:, cols] + (1.0 - beta_one) * gradient
        second_new = beta_two * second_ref[:, cols] + (1.0 - beta_two) * gradient * gradient
        new_first_ref[:, cols] = first_new
        new_second_ref[:, cols] = second_new
        new_params_ref[:, cols] = params_ref[:, cols] - rate * first_new / (
            jnp.sqrt(second_new * (1.0 / bias_two)) + adam_eps
        )
        if h % 4 == 3:
            done = pl.ds((h - 3) * 256, 1024)
            for k, (near, far) in enumerate(
                (
                    (new_params_ref, new_params_any),
                    (new_first_ref, new_first_any),
                    (new_second_ref, new_second_any),
                )
            ):
                sem = out_sems.at[k, h // 4]
                pending.append(pltpu.make_async_copy(near.at[:, done], far.at[:, done], sem))
                pending[-1].start()
    for copy in pending:
        copy.wait()


def shape(rows, cols, dtype=f32):
    return jax.ShapeDtypeStruct((rows, cols), dtype)


def exchange(lines, count):
    sent = lines.reshape(128, 1, count * 128)
    came = lax.all_to_all(sent, AXES, split_axis=0, concat_axis=0, tiled=True)
    return came.reshape(128 * count, 128)


def shards(params, adam_first, adam_second, view_yaw, tile_plan, tile_lists, requests, targets):
    cos_yaw = jnp.broadcast_to(jnp.pad(jnp.cos(view_yaw), (0, 96))[None, :], (8, 128))
    sin_yaw = jnp.broadcast_to(jnp.pad(jnp.sin(view_yaw), (0, 96))[None, :], (8, 128))
    woven = jnp.transpose(tile_lists.reshape(TILES, 8, 32), (0, 2, 1)).reshape(TILES, LIST)
    asked, rank = call(
        ask_kernel,
        (shape(128, 128, i32), shape(64, 128)),
        "ask",
        scratch=[
            pltpu.SMEM((TILES,), i32),
            pltpu.VMEM((TILES, LIST), i32),
            pltpu.VMEM((64, 128), i32),
            pltpu.SemaphoreType.DMA((3,)),
        ],
        in_specs=[HB] * 3,
    )(tile_plan, tile_lists, requests.reshape(64, 128))
    came = exchange(asked, 1)
    turned = call(turn_kernel, shape(OWN, 128), "turn", in_specs=[VM])(
        jnp.pad(params, ((0, 64 - PARAM), (0, 0)))
    )
    lists = call(relist_kernel, shape(TILES, LIST, i32), "relist", in_specs=[VM, VM])(woven, rank)
    aims = jnp.pad(jnp.transpose(targets, (1, 0, 2)), ((0, 0), (0, 5), (0, 0)))
    indexes = [
        pltpu.SMEM((128, 128), i32),
        pltpu.SMEM((8, 512), i32),
        pltpu.SemaphoreType.DMA,
        pltpu.SemaphoreType.DMA,
    ]
    answers, slots, codes, places, beyond = call(
        answer_kernel,
        (
            shape(128 * LINES, 128),
            shape(64 * 64, 128),
            shape(64, 128, i32),
            shape(128, 128, i32),
            shape(8, 512, i32),
        ),
        "answer",
        scratch=[
            pltpu.VMEM((OWN, 128), f32),
            pltpu.VMEM((64 * 64, 128), f32),
            pltpu.VMEM((128 * LINES, 128), f32),
            pltpu.SemaphoreType.DMA((8,)),
        ]
        + indexes,
        in_specs=[VM] * 4,
        out_specs=(VM, HB, VM, VM, VM),
        flops=4_500_000_000,
    )(came, turned, cos_yaw, sin_yaw)
    arrived = exchange(answers, LINES)
    wide = pltpu.VMEM((LIST, PIX), f32)
    narrow = pltpu.VMEM((LIST, 128), f32)
    returned = call(
        render_kernel,
        shape(128 * LINES, 128),
        "render",
        scratch=[
            pltpu.VMEM((768, 256), bf16),
            pltpu.VMEM((TILES, 256, LIST), bf16),
            pltpu.VMEM((288, 256), f32),
            narrow,
            narrow,
        ]
        + [pltpu.VMEM((16, LIST), f32)] * 2
        + ([wide] * 4 + [narrow, pltpu.VMEM((3 * LIST, 128), f32), pltpu.VMEM((24, PIX), f32)]) * 2,
        in_specs=[VM] * 3,
        flops=5_000_000_000,
    )(arrived, lists, aims)
    back = exchange(returned, LINES)
    return call(
        update_kernel,
        (shape(PARAM, OWN), shape(PARAM, OWN), shape(PARAM, OWN)),
        "update",
        scratch=[pltpu.VMEM((PARAM, OWN), f32)] * 3
        + [
            pltpu.SemaphoreType.DMA((3, 4)),
            pltpu.VMEM((128 * LINES, 128), f32),
            pltpu.VMEM((64 * 64, 128), f32),
            pltpu.VMEM((OWN, 128), f32),
        ]
        + [pltpu.VMEM((OWN + 8, 128), f32)] * 3
        + indexes,
        in_specs=[VM] * 10,
        out_specs=(HB, HB, HB),
        flops=4_500_000_000,
        mib=24,
    )(back, places, beyond, slots, codes, cos_yaw, sin_yaw, params, adam_first, adam_second)


def solution(mesh):
    placed = (
        P(None, AXES),
        P(None, AXES),
        P(None, AXES),
        P(),
        P(AXES),
        P(AXES, None),
        P(AXES, None),
        P(None, AXES, None),
    )
    return jax.shard_map(
        shards,
        mesh=mesh,
        in_specs=placed,
        out_specs=(P(None, AXES), P(None, AXES), P(None, AXES)),
        check_vma=False,
    )
```

```python
from functools import partial

import jax
import jax.numpy as jnp
from jax import lax
from jax.experimental import pallas as pl
from jax.experimental.pallas import tpu as pltpu
from jax.sharding import PartitionSpec as P

AXES = ("img", "blk")
STEP = 1000
TILES_ACROSS = 120
TILES_VIEW = 8160
TILE_EDGE = 16
PARAM = 59
OWN = 4096
SLOTS = 8192
TILES = 16
LIST = 256
PIX = 256
SENT = 9
LINES = 5

focal_px = 2400.0
camera_distance = 10.0
low_pass = 0.3
loss_scale = 16.0
beta_one = 0.9
beta_two = 0.999
adam_eps = 1e-08
band_zero = 0.28209479177387814
band_one = 0.4886025119029199
band_two = (
    1.0925484305920792,
    -1.0925484305920792,
    0.31539156525252005,
    -1.0925484305920792,
    0.5462742152960396,
)
band_three = (
    -0.5900435899266435,
    2.890611442640554,
    -0.4570457994644658,
    0.3731763325901154,
    -0.4570457994644658,
    1.445305721320277,
    -0.5900435899266435,
)
f32 = jnp.float32
bf16 = jnp.bfloat16
i32 = jnp.int32
VM = pl.BlockSpec(memory_space=pltpu.VMEM)
SM = pl.BlockSpec(memory_space=pltpu.SMEM)
HB = pl.BlockSpec(memory_space=pltpu.HBM)


def iota(shape, dim):
    return lax.broadcasted_iota(i32, shape, dim)


def dot(a, b):
    return lax.dot_general(a, b, (((1,), (0,)), ((), ())), preferred_element_type=f32)


def dot_t(a, b):
    return lax.dot_general(a, b, (((1,), (1,)), ((), ())), preferred_element_type=f32)


def pieces(x, count):
    out = []
    for k in range(count):
        part = x.astype(bf16)
        out.append(part)
        if k + 1 < count:
            x = x - part.astype(f32)
    return out


def call(kernel, out_shape, name, scratch=(), in_specs=None, out_specs=None, flops=0, mib=16):
    return partial(
        pl.pallas_call,
        kernel,
        out_shape=out_shape,
        in_specs=in_specs,
        out_specs=out_specs or jax.tree.map(lambda _: VM, out_shape),
        scratch_shapes=list(scratch),
        name=name,
        cost_estimate=pl.CostEstimate(flops=flops, bytes_accessed=4 << 20, transcendentals=0),
        compiler_params=pltpu.CompilerParams(vmem_limit_bytes=mib << 20),
    )()


def harmonics(looking_x, look_y, look_z):
    square_x = looking_x * looking_x
    square_y = look_y * look_y
    square_z = look_z * look_z
    return [
        jnp.full_like(looking_x, band_zero),
        -band_one * look_y,
        band_one * look_z,
        -band_one * looking_x,
        band_two[0] * looking_x * look_y,
        band_two[1] * look_y * look_z,
        band_two[2] * (2.0 * square_z - square_x - square_y),
        band_two[3] * looking_x * look_z,
        band_two[4] * (square_x - square_y),
        band_three[0] * look_y * (3.0 * square_x - square_y),
        band_three[1] * looking_x * look_y * look_z,
        band_three[2] * look_y * (4.0 * square_z - square_x - square_y),
        band_three[3] * look_z * (2.0 * square_z - 3.0 * square_x - 3.0 * square_y),
        band_three[4] * looking_x * (4.0 * square_z - square_x - square_y),
        band_three[5] * look_z * (square_x - square_y),
        band_three[6] * looking_x * (square_x - 3.0 * square_y),
    ]


def project_slots(rows, cos_yaw, sin_yaw, centre_x, centre_y):
    world_x, world_y, world_z = rows[0], rows[1], rows[2]
    view_x = cos_yaw * world_x + sin_yaw * world_z
    view_z = cos_yaw * world_z - sin_yaw * world_x + camera_distance
    inverse_z = 1.0 / view_z
    mean_x = focal_px * view_x * inverse_z - centre_x
    mean_y = focal_px * world_y * inverse_z - centre_y
    scales = [jnp.exp(rows[3 + k]) for k in range(3)]
    norm = jnp.sqrt(
        rows[6] * rows[6] + rows[7] * rows[7] + rows[8] * rows[8] + rows[9] * rows[9]
    )
    inverse_norm = 1.0 / norm
    quat_w, quat_x, quat_y, quat_z = [rows[6 + k] * inverse_norm for k in range(4)]
    rotation = [
        [
            1.0 - 2.0 * (quat_y * quat_y + quat_z * quat_z),
            2.0 * (quat_x * quat_y - quat_w * quat_z),
            2.0 * (quat_x * quat_z + quat_w * quat_y),
        ],
        [
            2.0 * (quat_x * quat_y + quat_w * quat_z),
            1.0 - 2.0 * (quat_x * quat_x + quat_z * quat_z),
            2.0 * (quat_y * quat_z - quat_w * quat_x),
        ],
        [
            2.0 * (quat_x * quat_z - quat_w * quat_y),
            2.0 * (quat_y * quat_z + quat_w * quat_x),
            1.0 - 2.0 * (quat_x * quat_x + quat_y * quat_y),
        ],
    ]
    focal_z = focal_px * inverse_z
    shear_x = focal_z * view_x * inverse_z
    shear_y = focal_z * world_y * inverse_z
    jacob_ax = focal_z * cos_yaw + shear_x * sin_yaw
    jacob_az = focal_z * sin_yaw - shear_x * cos_yaw
    jacob_bx = shear_y * sin_yaw
    jacob_bz = -shear_y * cos_yaw
    row_a = [
        (jacob_ax * rotation[0][k] + jacob_az * rotation[2][k]) * scales[k] for k in range(3)
    ]
    row_b = [
        (jacob_bx * rotation[0][k] + focal_z * rotation[1][k] + jacob_bz * rotation[2][k])
        * scales[k]
        for k in range(3)
    ]
    covar_xx = row_a[0] * row_a[0] + row_a[1] * row_a[1] + row_a[2] * row_a[2] + low_pass
    covar_yy = row_b[0] * row_b[0] + row_b[1] * row_b[1] + row_b[2] * row_b[2] + low_pass
    covar_xy = row_a[0] * row_b[0] + row_a[1] * row_b[1] + row_a[2] * row_b[2]
    inverse_det = 1.0 / (covar_xx * covar_yy - covar_xy * covar_xy)
    conic_a = covar_yy * inverse_det
    conic_b = -covar_xy * inverse_det
    conic_c = covar_xx * inverse_det
    log_opacity = rows[10] - jnp.log(1.0 + jnp.exp(rows[10]))
    slope_x = conic_a * mean_x + conic_b * mean_y
    slope_y = conic_c * mean_y + conic_b * mean_x
    constant = log_opacity - 0.5 * (slope_x * mean_x + slope_y * mean_y)
    inverse_len = 1.0 / jnp.sqrt(view_x * view_x + world_y * world_y + view_z * view_z)
    basis = harmonics(
        (cos_yaw * view_x - sin_yaw * view_z) * inverse_len,
        world_y * inverse_len,
        (sin_yaw * view_x + cos_yaw * view_z) * inverse_len,
    )
    colors = []
    for channel in range(3):
        total = basis[0] * rows[11 + channel]
        for degree in range(1, 16):
            total = total + basis[degree] * rows[11 + 3 * degree + channel]
        colors.append(jnp.maximum(0.5 + total, 0.0))
    return [
        constant,
        slope_x,
        slope_y,
        -0.5 * conic_a,
        -conic_b,
        -0.5 * conic_c,
    ] + colors


def camera_of(codes, cos_ref, sin_ref):
    code = jnp.maximum(codes, 0).astype(f32)
    view = jnp.floor((code + 0.5) * (1.0 / TILES_VIEW))
    number = code - view * float(TILES_VIEW)
    across = jnp.floor((number + 0.5) * (1.0 / TILES_ACROSS))
    column = number - across * float(TILES_ACROSS)
    view = view.astype(i32)
    cos_yaw = jnp.take_along_axis(cos_ref[...], view, axis=1, mode="promise_in_bounds")
    sin_yaw = jnp.take_along_axis(sin_ref[...], view, axis=1, mode="promise_in_bounds")
    centre_x = column * 16.0 + (8.0 - 960.0)
    centre_y = across * 16.0 + (8.0 - 544.0)
    return cos_yaw, sin_yaw, centre_x, centre_y


def slot_parts(slot):
    line = jnp.right_shift(slot, 7)
    high = jnp.bitwise_and(line, 31)
    low = jnp.right_shift(line, 5) * 128 + jnp.bitwise_and(slot, 127)
    return high, low


def hot_rows(low, count=256):
    return (iota((count, low.shape[1]), 0) == low).astype(f32).astype(bf16)


def ask_kernel(plan_any, lists_any, req_any, out_ref, rank_ref, plan_ref, lists_ref, req_ref, sems):
    copies = [
        pltpu.make_async_copy(source, to, sems.at[k])
        for k, (source, to) in enumerate(
            ((lists_any, lists_ref), (plan_any, plan_ref), (req_any, req_ref))
        )
    ]
    for copy in copies:
        copy.start()
    copies[0].wait()
    tiles = jnp.zeros((64, 128), f32)
    for t in range(TILES):
        slot = lists_ref[t : t + 1, :]
        high, low = jnp.right_shift(slot, 7), jnp.bitwise_and(slot, 127)
        left = jnp.where(iota((64, LIST), 0) == high, float(t + 1), 0.0).astype(bf16)
        tiles = tiles + dot_t(left, hot_rows(low, 128))
    named = tiles > 0.0
    a, b = iota((128, 128), 0), iota((128, 128), 1)
    earlier = jnp.logical_and(a < b, jnp.right_shift(a, 6) == jnp.right_shift(b, 6))
    rank = dot(named.astype(f32).astype(bf16), earlier.astype(f32).astype(bf16))
    rank_ref[...] = rank
    gap = jnp.bitwise_and(iota((64, 128), 1), 63) - rank.astype(i32)
    copies[1].wait()
    copies[2].wait()
    held = req_ref[...] + tiles.astype(i32) * 4096 + gap * 131072
    held = jnp.where(named, held, 0)
    for k in range(6):
        ahead = pltpu.roll(held, 128 - (1 << k), 1)
        comes = jnp.bitwise_and(jnp.right_shift(ahead, 17 + k), 1) == 1
        stays = jnp.bitwise_and(jnp.right_shift(held, 17 + k), 1) == 0
        held = jnp.where(comes, ahead, jnp.where(stays, held, 0))
    asked = jnp.bitwise_and(held, 4095)
    tile = jnp.bitwise_and(jnp.right_shift(held, 12), 31)
    codes = jnp.full((64, 128), -1, i32)
    for t in range(TILES):
        codes = jnp.where(tile == t + 1, plan_ref[t], codes)
    first = iota((64, 128), 1) < 64
    out_ref[pl.ds(0, 64, stride=2), :] = jnp.where(first, asked, pltpu.roll(codes, 64, 1))
    out_ref[pl.ds(1, 64, stride=2), :] = jnp.where(first, pltpu.roll(asked, 64, 1), codes)


def relist_kernel(lists_ref, rank_ref, out_ref):
    rank = rank_ref[...]
    table = jnp.concatenate([rank[:32], rank[32:]], axis=1).astype(bf16)

    def tile(t, _):
        slot = lists_ref[pl.ds(t, 1), :]
        high, low = slot_parts(slot)
        found = jnp.where(iota((32, LIST), 0) == high, dot(table, hot_rows(low)), 0.0)
        place = jnp.sum(found, axis=0, keepdims=True).astype(i32)
        out_ref[pl.ds(t, 1), :] = slot - jnp.bitwise_and(slot, 63) + place
        return 0

    lax.fori_loop(0, TILES, tile, 0, unroll=4)


def turn_kernel(params_ref, out_ref):
    for h in range(16):
        block = params_ref[:, h * 256 : (h + 1) * 256]
        out_ref[h * 256 : (h + 1) * 256, :] = jnp.transpose(jnp.concatenate([block, block], axis=0))


FRONT = 32


def list_beyond(came, out_ref):
    lane = iota((128, 128), 1)
    used = jnp.where(jnp.logical_and(lane >= 64, came >= 0), 1.0, 0.0)
    count = jnp.broadcast_to(jnp.sum(used, axis=1, keepdims=True), (128, 128)).astype(i32)
    eights = jnp.right_shift(jnp.maximum(count - FRONT, 0) + 7, 3).astype(f32)
    upto = (lane <= iota((128, 128), 0)).astype(f32).astype(bf16)
    ends = dot(upto, eights.astype(bf16))
    for c in range(4):
        place = (iota((128, 128), 1) + c * 128).astype(f32)
        past = ends <= place
        asker = jnp.sum(jnp.where(past, 1.0, 0.0), axis=0, keepdims=True)
        begun = jnp.sum(jnp.where(past, eights, 0.0), axis=0, keepdims=True)
        slot = FRONT + 8.0 * (place[0:1] - begun)
        row = iota((8, 128), 0)
        lines = jnp.where(row == 0, asker, jnp.where(row == 1, slot, ends[127:128]))
        out_ref[:, c * 128 : (c + 1) * 128] = lines.astype(i32)


def by_groups(count, shift, body):
    size = 1 << shift
    groups = jnp.right_shift(count, shift)
    lax.fori_loop(0, groups, lambda k, _: body(k * size, size), None)
    lax.fori_loop(groups * size, count, lambda k, _: body(k, 1), None)


def answer_kernel(
    came_ref, turned_ref, cos_ref, sin_ref, out_ref, slots_ref, codes_ref, places_ref, beyond_ref,
    over, behind, values, index_s, beyond_s, index_sems, beyond_sem,
):
    index_copies = [
        pltpu.make_async_copy(came_ref.at[part], index_s.at[part], index_sems.at[k])
        for k, part in enumerate(pl.ds(32 * k, 32) for k in range(4))
    ]
    for copy in index_copies:
        copy.start()
    came = came_ref[...]
    list_beyond(came, beyond_ref)
    beyond_copy = pltpu.make_async_copy(beyond_ref, beyond_s, beyond_sem)
    beyond_copy.start()
    codes_ref[...] = jnp.transpose(came.astype(f32))[64:128].astype(i32)
    spare = OWN + jnp.bitwise_and(iota((128, 128), 1), 7)
    places_ref[...] = jnp.where(pltpu.roll(came, 64, 1) < 0, spare, came)

    def fetch(step, _):
        for k in range(2):
            p = 2 * step + k
            for j in range(FRONT):
                over[pl.ds(j * 128 + p, 1), :] = turned_ref[pl.ds(index_s[p, j], 1), :]
        return 0

    behind[...] = jnp.ones_like(behind)
    for k, copy in enumerate(index_copies):
        copy.wait()
        lax.fori_loop(16 * k, 16 * k + 16, fetch, 0)
    beyond_copy.wait()

    def fetch_beyond(first_k, count):
        for k in range(count):
            p, slot = beyond_s[0, first_k + k], beyond_s[1, first_k + k]
            for j in range(8):
                row = turned_ref[pl.ds(index_s[p, slot + j], 1), :]
                behind[pl.ds((slot - FRONT + j) * 128 + p, 1), :] = row

    by_groups(beyond_s[2, 0], 1, fetch_beyond)
    first = iota((128, 128), 1) < 64

    def spread(step, _):
        for k in range(8):
            part = pl.ds(pl.multiple_of((step * 8 + k) * 128, 128), 128)
            over[part, :] = jnp.transpose(jnp.where(first, over[part, :], behind[part, :]))
        return 0

    lax.fori_loop(0, FRONT // 8, spread, 0)

    for r in range(PARAM, 64):
        for g in range(8):
            slots_ref[g * 512 + r * 8 : g * 512 + r * 8 + 8, :] = jnp.zeros((8, 128), f32)

    def work(g, _):
        at = pl.multiple_of(g * 8, 8)
        base = jnp.bitwise_and(g, 3) * 1024 + jnp.right_shift(g, 2) * 64
        rows = [over[pl.ds(base + r, 8, stride=128), :] for r in range(PARAM)]
        for r in range(PARAM):
            slots_ref[pl.ds(pl.multiple_of(g * 512 + r * 8, 8), 8), :] = rows[r]
        camera = camera_of(codes_ref[pl.ds(at, 8), :], cos_ref, sin_ref)
        for q, value in enumerate(project_slots(rows, *camera)):
            values[pl.ds(pl.multiple_of(q * 64 + at, 8), 8), :] = value
        return 0

    values[SENT * 64 :, :] = jnp.zeros((64, 128), f32)
    lax.fori_loop(0, 8, work, 0)
    for line in range(LINES):
        block = values[line * 128 : (line + 1) * 128, :]
        out_ref[pl.ds(line, 128, stride=LINES), :] = jnp.transpose(block)


def monomials(x, y, which):
    out = jnp.zeros(x.shape, f32)
    for k, value in enumerate((jnp.ones_like(x), x, y, x * x, x * y, y * y)):
        out = jnp.where(which == k, value, out)
    return out


def render_kernel(
    came_ref, lists_ref, targets_ref, out_ref,
    table, hots, back, coefs0, coefs1, spread0, spread1, *work_refs,
):
    coefs, spreads = (coefs0, coefs1), (spread0, spread1)
    first = iota((64, 128), 1) < 64
    for q in range(SENT):
        line = q // 2
        even = came_ref[pl.ds(line, 64, stride=10), :]
        odd = came_ref[pl.ds(5 + line, 64, stride=10), :]
        if q % 2 == 0:
            dense = jnp.where(first, even, pltpu.roll(odd, 64, 1))
        else:
            dense = jnp.where(first, pltpu.roll(even, 64, 1), odd)
        square = jnp.concatenate([dense[:32], dense[32:]], axis=1)
        for s, part in enumerate(pieces(square, 3 if q < 6 else 2)):
            table[pl.ds(s * 288 + q * 32, 32), :] = part
    back[...] = jnp.zeros_like(back)
    spread1[...] = jnp.zeros_like(spread1)
    works = (work_refs[:7], work_refs[7:])
    row = iota((32, PIX), 0)
    pix = iota((32, PIX), 1)
    basis = monomials(
        jnp.bitwise_and(pix, 15).astype(f32) - 7.5,
        jnp.right_shift(pix, 4).astype(f32) - 7.5,
        jnp.where(row < 24, jnp.bitwise_and(row, 7), 7),
    ).astype(bf16)
    sub = iota((8, PIX), 0)
    lane = iota((8, 128), 1)
    offset_x = jnp.bitwise_and(lane, 15).astype(f32) - 7.5
    offset_y = jnp.right_shift(lane, 4).astype(f32) - 3.5
    square_y = offset_y * offset_y + 16.0
    eight_y = offset_y * 8.0

    def make_hot(t, _):
        hots[t] = hot_rows(slot_parts(lists_ref[pl.ds(t, 1), :])[1])
        return 0

    lax.fori_loop(0, TILES, make_hot, 0, unroll=2)

    def here_of(t):
        return iota((32, LIST), 0) == slot_parts(lists_ref[pl.ds(t, 1), :])[0]

    def gather(t, to):
        found = dot(table[...], hots[t])
        here = here_of(t)
        values = []
        for q in range(SENT):
            at = q * 32
            value = found[at : at + 32] + (
                found[288 + at : 320 + at] + found[576 + at : 608 + at]
                if q < 6
                else found[288 + at : 320 + at]
            )
            values.append(jnp.sum(jnp.where(here, value, 0.0), axis=0, keepdims=True))
        shape_rows = jnp.zeros((8, LIST), f32)
        color_rows = jnp.zeros((8, LIST), f32)
        for q in range(6):
            shape_rows = jnp.where(sub == q, values[q], shape_rows)
        for q in range(3):
            color_rows = jnp.where(sub == q, values[6 + q], color_rows)
        parts = [p.astype(f32) for p in pieces(shape_rows, 3)]
        stack = jnp.concatenate(parts + [color_rows] + [jnp.zeros((96, LIST), f32)], axis=0)
        to[...] = jnp.transpose(stack)

    def scatter(t, source):
        here = here_of(t)
        parts = [p.astype(f32) for p in pieces(source[...], 2)]
        left = []
        for s in range(2):
            for q in range(SENT):
                value = jnp.broadcast_to(parts[s][q : q + 1], (32, LIST))
                left.append(jnp.where(here, value, 0.0).astype(bf16))
        moved = dot_t(jnp.concatenate(left, axis=0), hots[t])
        back[...] += moved[0:288] + moved[288:576]

    def scan8(x, neutral, op, down):
        def shift(y, n):
            if down:
                return jnp.where(sub >= n, pltpu.roll(y, n, 0), neutral)
            return jnp.where(sub < 8 - n, pltpu.roll(y, 8 - n, 0), neutral)

        x = shift(x, 1)
        for n in (1, 2, 4):
            x = op(x, shift(x, n))
        return x

    def rows_of(v):
        return slice(v * 8, v * 8 + 8)

    def twice(x):
        return jnp.concatenate([x, x], axis=1)

    def expose(source, refs):
        refs[0][...] = dot(source[:, 0:32].astype(bf16), basis)

    def pass_light(v, refs, product):
        alphas, before = refs[0], refs[1]
        alpha = jnp.exp(alphas[rows_of(v)])
        alphas[rows_of(v)] = alpha
        before[rows_of(v)] = product
        return product * (1.0 - alpha)

    def weigh(v, source, refs, ahead, seen):
        alphas, weights, tones = refs[0], refs[1], refs[5]
        weight = alphas[rows_of(v)] * (weights[rows_of(v)] * ahead)
        weights[rows_of(v)] = weight
        out = []
        for c in range(3):
            tone = jnp.broadcast_to(source[rows_of(v), 24 + c : 25 + c], (8, 128))
            tones[c * 256 + v * 8 : c * 256 + v * 8 + 8] = tone
            out.append(seen[c] + weight * twice(tone))
        return out

    def compare(t, seen, refs):
        for c in range(3):
            total = jnp.sum(seen[c], axis=0, keepdims=True)
            pull = (total - targets_ref[t, c : c + 1, :]) * (1.0 / loss_scale)
            refs[6][c * 8 : c * 8 + 8] = jnp.broadcast_to(pull, (8, PIX))

    def pull_back(v, refs, pulls, rest):
        weights, gains, behind, sums, tones = refs[1:6]
        weight = weights[rows_of(v)]
        gain = jnp.zeros((8, PIX), f32)
        line = jnp.zeros((8, 128), f32)
        for c in range(3):
            gain = gain + pulls[c] * twice(tones[c * 256 + v * 8 : c * 256 + v * 8 + 8])
            tint = weight * pulls[c]
            tint = jnp.sum(tint[:, :128] + tint[:, 128:], axis=1, keepdims=True)
            line = jnp.where(lane == 6 + c, tint, line)
        gain = gain * weight
        gains[rows_of(v)] = gain
        behind[rows_of(v)] = rest
        sums[rows_of(v)] = line
        return rest + gain

    def moments(v, refs, after):
        alphas, gains, behind, sums = refs[0], refs[2], refs[3], refs[4]
        alpha = alphas[rows_of(v)]
        slope = behind[rows_of(v)] + after
        slope = gains[rows_of(v)] - slope * (alpha / (1.0 - alpha))
        upper, lower = slope[:, :128], slope[:, 128:]
        both, apart = upper + lower, lower - upper
        along = both * offset_x
        down = both * offset_y + apart * 4.0
        line = sums[rows_of(v)]
        for k, value in enumerate(
            (both, along, down, along * offset_x, down * offset_x,
             both * square_y + apart * eight_y)
        ):
            line = jnp.where(lane == k, jnp.sum(value, axis=1, keepdims=True), line)
        sums[rows_of(v)] = line

    one = jnp.ones((8, PIX), f32)
    nothing = jnp.zeros((8, PIX), f32)
    gather(0, coefs[0])
    gather(1, coefs[1])
    expose(coefs[0], works[0])
    product = one
    for v in range(32):
        product = pass_light(v, works[0], product)
    ahead = scan8(product, 1.0, jnp.multiply, True)
    seen = [nothing] * 3
    for v in range(32):
        seen = weigh(v, coefs[0], works[0], ahead, seen)
    compare(0, seen, works[0])

    def pair(step, _):
        for k in range(2):
            t = 2 * step + k
            coming = jnp.minimum(t + 1, TILES - 1)
            here, there = works[k], works[1 - k]
            expose(coefs[1 - k], there)
            scatter(jnp.maximum(t - 1, 0), spreads[1 - k])
            pulls = [here[6][c * 8 : c * 8 + 8] for c in range(3)]
            product, rest = one, nothing
            for v in range(32):
                product = pass_light(v, there, product)
                rest = pull_back(31 - v, here, pulls, rest)
            ahead = scan8(product, 1.0, jnp.multiply, True)
            after = scan8(rest, 0.0, jnp.add, False)
            gather(jnp.minimum(t + 2, TILES - 1), coefs[k])
            seen = [nothing] * 3
            for v in range(32):
                seen = weigh(v, coefs[1 - k], there, ahead, seen)
                moments(v, here, after)
            compare(coming, seen, there)
            spreads[k][...] = jnp.transpose(here[4][...])[0:16]
        return 0

    lax.fori_loop(0, TILES // 2, pair, 0)
    scatter(TILES - 1, spreads[1])

    zero = jnp.zeros((64, 128), f32)

    def dense_of(q):
        if q >= SENT:
            return zero
        square = back[pl.ds(q * 32, 32), :]
        return jnp.concatenate([square[:, :128], square[:, 128:]], axis=0)

    for line in range(LINES):
        a, b = dense_of(2 * line), dense_of(2 * line + 1)
        out_ref[pl.ds(line, 64, stride=10), :] = jnp.where(first, a, pltpu.roll(b, 64, 1))
        out_ref[pl.ds(5 + line, 64, stride=10), :] = jnp.where(first, pltpu.roll(a, 64, 1), b)


def rates(shape):
    row = iota(shape, 0)
    out = jnp.full(shape, 0.000125, f32)
    for end, rate in ((14, 0.0025), (11, 0.05), (10, 0.001), (6, 0.005), (3, 0.0008)):
        out = jnp.where(row < end, rate, out)
    return out


def update_kernel(
    back_ref, places_ref, beyond_ref, slots_ref, codes_ref, cos_ref, sin_ref,
    params_ref, first_ref, second_ref, new_params_any, new_first_any, new_second_any,
    new_params_ref, new_first_ref, new_second_ref, out_sems,
    cots, grads, over, even, odd, rest, index_s, beyond_s, index_sem, beyond_sem,
):
    index_copy = pltpu.make_async_copy(places_ref, index_s, index_sem)
    beyond_copy = pltpu.make_async_copy(beyond_ref, beyond_s, beyond_sem)
    index_copy.start()
    beyond_copy.start()
    for line in range(LINES):
        block = back_ref[pl.ds(line, 128, stride=LINES), :]
        cots[line * 128 : (line + 1) * 128, :] = jnp.transpose(block)
    for r in range(PARAM, 64):
        for g in range(8):
            grads[g * 512 + r * 8 : g * 512 + r * 8 + 8, :] = jnp.zeros((8, 128), f32)

    def work(g, _):
        at = pl.multiple_of(g * 8, 8)
        lines = [pl.ds(pl.multiple_of(g * 512 + r * 8, 8), 8) for r in range(PARAM)]
        camera = camera_of(codes_ref[pl.ds(at, 8), :], cos_ref, sin_ref)
        _, pullback = jax.vjp(
            lambda r: project_slots(r, *camera), [slots_ref[line, :] for line in lines]
        )
        (out,) = pullback(
            [cots[pl.ds(pl.multiple_of(q * 64 + at, 8), 8), :] for q in range(SENT)]
        )
        for r in range(PARAM):
            grads[lines[r], :] = out[r]
        clear = pl.ds(pl.multiple_of(g * 512, 512), 512)
        for sums in (even, odd, rest):
            sums[clear, :] = jnp.zeros((512, 128), f32)
        return 0

    lax.fori_loop(0, 8, work, 0)

    def spread(g, _):
        for k in range(8):
            block = [
                grads[pl.ds((g + half) * 512 + k + m * 64, 8, stride=8), :]
                for half in (0, 4)
                for m in range(8)
            ]
            at = pl.multiple_of((g * 8 + k) * 128, 128)
            over[pl.ds(at, 128), :] = jnp.transpose(jnp.concatenate(block, axis=0))
        return 0

    lax.fori_loop(0, FRONT // 8, spread, 0)
    index_copy.wait()
    beyond_copy.wait()

    def add_eight(sums, p, slot, line):
        at = [pl.ds(index_s[p, slot + n], 1) for n in range(8)]
        new = [sums[at[n], :] + over[pl.ds((line + n) * 128 + p, 1), :] for n in range(8)]
        for n in range(8):
            sums[at[n], :] = new[n]

    def gather(step, _):
        for j in range(0, FRONT, 8):
            add_eight(even, 2 * step, j, j)
            add_eight(odd, 2 * step + 1, j, j)
        return 0

    lax.fori_loop(0, 64, gather, 0)

    def gather_beyond(first_k, count):
        for k in range(count):
            p, slot = beyond_s[0, first_k + k], beyond_s[1, first_k + k]
            add_eight(rest, p, slot, slot - FRONT)

    by_groups(beyond_s[2, 0], 2, gather_beyond)
    first = iota((256, 128), 1) < 64
    bias_one = 1.0 - beta_one**STEP
    bias_two = 1.0 - beta_two**STEP
    rate = rates((PARAM, 256)) * (1.0 / bias_one)
    pending = []
    for h in range(16):
        cols = slice(h * 256, (h + 1) * 256)
        both = jnp.transpose(jnp.where(first, even[cols, :] + odd[cols, :], rest[cols, :]))
        gradient = both[:PARAM] + both[64 : 64 + PARAM]
        first_new = beta_one * first_ref[:, cols] + (1.0 - beta_one) * gradient
        second_new = beta_two * second_ref[:, cols] + (1.0 - beta_two) * gradient * gradient
        new_first_ref[:, cols] = first_new
        new_second_ref[:, cols] = second_new
        scaled = second_new * (1.0 / bias_two)
        new_params_ref[:, cols] = params_ref[:, cols] - rate * first_new / (
            scaled * lax.rsqrt(scaled) + adam_eps
        )
        if h % 4 == 3:
            done = pl.ds((h - 3) * 256, 1024)
            for k, (near, far) in enumerate(
                (
                    (new_params_ref, new_params_any),
                    (new_first_ref, new_first_any),
                    (new_second_ref, new_second_any),
                )
            ):
                sem = out_sems.at[k, h // 4]
                pending.append(pltpu.make_async_copy(near.at[:, done], far.at[:, done], sem))
                pending[-1].start()
    for copy in pending:
        copy.wait()


def shape(rows, cols, dtype=f32):
    return jax.ShapeDtypeStruct((rows, cols), dtype)


def exchange(lines, count):
    sent = lines.reshape(128, 1, count * 128)
    came = lax.all_to_all(sent, AXES, split_axis=0, concat_axis=0, tiled=True)
    return came.reshape(128 * count, 128)


def shards(params, adam_first, adam_second, view_yaw, tile_plan, tile_lists, requests, targets):
    cos_yaw = jnp.broadcast_to(jnp.pad(jnp.cos(view_yaw), (0, 96))[None, :], (8, 128))
    sin_yaw = jnp.broadcast_to(jnp.pad(jnp.sin(view_yaw), (0, 96))[None, :], (8, 128))
    woven = jnp.transpose(tile_lists.reshape(TILES, 8, 32), (0, 2, 1)).reshape(TILES, LIST)
    asked, rank = call(
        ask_kernel,
        (shape(128, 128, i32), shape(64, 128)),
        "ask",
        scratch=[
            pltpu.SMEM((TILES,), i32),
            pltpu.VMEM((TILES, LIST), i32),
            pltpu.VMEM((64, 128), i32),
            pltpu.SemaphoreType.DMA((3,)),
        ],
        in_specs=[HB] * 3,
        mib=60,
    )(tile_plan, tile_lists, requests.reshape(64, 128))
    came = exchange(asked, 1)
    turned = call(turn_kernel, shape(OWN, 128), "turn", in_specs=[VM])(
        jnp.pad(params, ((0, 64 - PARAM), (0, 0)))
    )
    lists = call(relist_kernel, shape(TILES, LIST, i32), "relist", in_specs=[VM, VM])(woven, rank)
    aims = jnp.pad(jnp.transpose(targets, (1, 0, 2)), ((0, 0), (0, 5), (0, 0)))
    indexes = [
        pltpu.SMEM((128, 128), i32),
        pltpu.SMEM((8, 512), i32),
        pltpu.SemaphoreType.DMA,
        pltpu.SemaphoreType.DMA,
    ]
    answers, slots, codes, places, beyond = call(
        answer_kernel,
        (
            shape(128 * LINES, 128),
            shape(64 * 64, 128),
            shape(64, 128, i32),
            shape(128, 128, i32),
            shape(8, 512, i32),
        ),
        "answer",
        scratch=[
            pltpu.VMEM((OWN, 128), f32),
            pltpu.VMEM((OWN, 128), f32),
            pltpu.VMEM((128 * LINES, 128), f32),
        ]
        + indexes[:2]
        + [pltpu.SemaphoreType.DMA((4,)), pltpu.SemaphoreType.DMA],
        in_specs=[VM] * 4,
        flops=4_500_000_000,
    )(came, turned, cos_yaw, sin_yaw)
    arrived = exchange(answers, LINES)
    wide = pltpu.VMEM((LIST, PIX), f32)
    narrow = pltpu.VMEM((LIST, 128), f32)
    returned = call(
        render_kernel,
        shape(128 * LINES, 128),
        "render",
        scratch=[
            pltpu.VMEM((768, 256), bf16),
            pltpu.VMEM((TILES, 256, LIST), bf16),
            pltpu.VMEM((288, 256), f32),
            narrow,
            narrow,
        ]
        + [pltpu.VMEM((16, LIST), f32)] * 2
        + ([wide] * 4 + [narrow, pltpu.VMEM((3 * LIST, 128), f32), pltpu.VMEM((24, PIX), f32)]) * 2,
        in_specs=[VM] * 3,
        flops=5_000_000_000,
    )(arrived, lists, aims)
    back = exchange(returned, LINES)
    return call(
        update_kernel,
        (shape(PARAM, OWN), shape(PARAM, OWN), shape(PARAM, OWN)),
        "update",
        scratch=[pltpu.VMEM((PARAM, OWN), f32)] * 3
        + [
            pltpu.SemaphoreType.DMA((3, 4)),
            pltpu.VMEM((128 * LINES, 128), f32),
            pltpu.VMEM((64 * 64, 128), f32),
            pltpu.VMEM((OWN, 128), f32),
        ]
        + [pltpu.VMEM((OWN + 8, 128), f32)] * 3
        + indexes,
        in_specs=[VM] * 10,
        out_specs=(HB, HB, HB),
        flops=4_500_000_000,
        mib=24,
    )(back, places, beyond, slots, codes, cos_yaw, sin_yaw, params, adam_first, adam_second)


def solution(mesh):
    placed = (
        P(None, AXES),
        P(None, AXES),
        P(None, AXES),
        P(),
        P(AXES),
        P(AXES, None),
        P(AXES, None),
        P(None, AXES, None),
    )
    return jax.shard_map(
        shards,
        mesh=mesh,
        in_specs=placed,
        out_specs=(P(None, AXES), P(None, AXES), P(None, AXES)),
        check_vma=False,
    )
```

```python
from functools import partial

import jax
import jax.numpy as jnp
from jax import lax
from jax.experimental import pallas as pl
from jax.experimental.pallas import tpu as pltpu
from jax.sharding import PartitionSpec as P

AXES = ("img", "blk")
STEP = 1000
TILES_ACROSS = 120
TILES_VIEW = 8160
TILE_EDGE = 16
PARAM = 59
OWN = 4096
SLOTS = 8192
TILES = 16
LIST = 256
PIX = 256
SENT = 9
LINES = 5

focal_px = 2400.0
camera_distance = 10.0
low_pass = 0.3
loss_scale = 16.0
beta_one = 0.9
beta_two = 0.999
adam_eps = 1e-08
log2_e = 1.4426950408889634
band_zero = 0.28209479177387814
band_one = 0.4886025119029199
band_two = (
    1.0925484305920792,
    -1.0925484305920792,
    0.31539156525252005,
    -1.0925484305920792,
    0.5462742152960396,
)
band_three = (
    -0.5900435899266435,
    2.890611442640554,
    -0.4570457994644658,
    0.3731763325901154,
    -0.4570457994644658,
    1.445305721320277,
    -0.5900435899266435,
)
f32 = jnp.float32
bf16 = jnp.bfloat16
i32 = jnp.int32
VM = pl.BlockSpec(memory_space=pltpu.VMEM)
SM = pl.BlockSpec(memory_space=pltpu.SMEM)
HB = pl.BlockSpec(memory_space=pltpu.HBM)


def iota(shape, dim):
    return lax.broadcasted_iota(i32, shape, dim)


def dot(a, b):
    return lax.dot_general(a, b, (((1,), (0,)), ((), ())), preferred_element_type=f32)


def dot_t(a, b):
    return lax.dot_general(a, b, (((1,), (1,)), ((), ())), preferred_element_type=f32)


def pieces(x, count):
    out = []
    for k in range(count):
        part = x.astype(bf16)
        out.append(part)
        if k + 1 < count:
            x = x - part.astype(f32)
    return out


def call(kernel, out_shape, name, scratch=(), in_specs=None, out_specs=None, flops=0, mib=16):
    return partial(
        pl.pallas_call,
        kernel,
        out_shape=out_shape,
        in_specs=in_specs,
        out_specs=out_specs or jax.tree.map(lambda _: VM, out_shape),
        scratch_shapes=list(scratch),
        name=name,
        cost_estimate=pl.CostEstimate(flops=flops, bytes_accessed=4 << 20, transcendentals=0),
        compiler_params=pltpu.CompilerParams(vmem_limit_bytes=mib << 20),
    )()


def harmonics(looking_x, look_y, look_z):
    square_x = looking_x * looking_x
    square_y = look_y * look_y
    square_z = look_z * look_z
    return [
        jnp.full_like(looking_x, band_zero),
        -band_one * look_y,
        band_one * look_z,
        -band_one * looking_x,
        band_two[0] * looking_x * look_y,
        band_two[1] * look_y * look_z,
        band_two[2] * (2.0 * square_z - square_x - square_y),
        band_two[3] * looking_x * look_z,
        band_two[4] * (square_x - square_y),
        band_three[0] * look_y * (3.0 * square_x - square_y),
        band_three[1] * looking_x * look_y * look_z,
        band_three[2] * look_y * (4.0 * square_z - square_x - square_y),
        band_three[3] * look_z * (2.0 * square_z - 3.0 * square_x - 3.0 * square_y),
        band_three[4] * looking_x * (4.0 * square_z - square_x - square_y),
        band_three[5] * look_z * (square_x - square_y),
        band_three[6] * looking_x * (square_x - 3.0 * square_y),
    ]


def project_slots(rows, cos_yaw, sin_yaw, centre_x, centre_y):
    world_x, world_y, world_z = rows[0], rows[1], rows[2]
    view_x = cos_yaw * world_x + sin_yaw * world_z
    view_z = cos_yaw * world_z - sin_yaw * world_x + camera_distance
    inverse_z = 1.0 / view_z
    mean_x = focal_px * view_x * inverse_z - centre_x
    mean_y = focal_px * world_y * inverse_z - centre_y
    scales = [jnp.exp(rows[3 + k]) for k in range(3)]
    norm = jnp.sqrt(
        rows[6] * rows[6] + rows[7] * rows[7] + rows[8] * rows[8] + rows[9] * rows[9]
    )
    inverse_norm = 1.0 / norm
    quat_w, quat_x, quat_y, quat_z = [rows[6 + k] * inverse_norm for k in range(4)]
    rotation = [
        [
            1.0 - 2.0 * (quat_y * quat_y + quat_z * quat_z),
            2.0 * (quat_x * quat_y - quat_w * quat_z),
            2.0 * (quat_x * quat_z + quat_w * quat_y),
        ],
        [
            2.0 * (quat_x * quat_y + quat_w * quat_z),
            1.0 - 2.0 * (quat_x * quat_x + quat_z * quat_z),
            2.0 * (quat_y * quat_z - quat_w * quat_x),
        ],
        [
            2.0 * (quat_x * quat_z - quat_w * quat_y),
            2.0 * (quat_y * quat_z + quat_w * quat_x),
            1.0 - 2.0 * (quat_x * quat_x + quat_y * quat_y),
        ],
    ]
    focal_z = focal_px * inverse_z
    shear_x = focal_z * view_x * inverse_z
    shear_y = focal_z * world_y * inverse_z
    jacob_ax = focal_z * cos_yaw + shear_x * sin_yaw
    jacob_az = focal_z * sin_yaw - shear_x * cos_yaw
    jacob_bx = shear_y * sin_yaw
    jacob_bz = -shear_y * cos_yaw
    row_a = [
        (jacob_ax * rotation[0][k] + jacob_az * rotation[2][k]) * scales[k] for k in range(3)
    ]
    row_b = [
        (jacob_bx * rotation[0][k] + focal_z * rotation[1][k] + jacob_bz * rotation[2][k])
        * scales[k]
        for k in range(3)
    ]
    covar_xx = row_a[0] * row_a[0] + row_a[1] * row_a[1] + row_a[2] * row_a[2] + low_pass
    covar_yy = row_b[0] * row_b[0] + row_b[1] * row_b[1] + row_b[2] * row_b[2] + low_pass
    covar_xy = row_a[0] * row_b[0] + row_a[1] * row_b[1] + row_a[2] * row_b[2]
    inverse_det = 1.0 / (covar_xx * covar_yy - covar_xy * covar_xy)
    conic_a = covar_yy * inverse_det
    conic_b = -covar_xy * inverse_det
    conic_c = covar_xx * inverse_det
    log_opacity = rows[10] - jnp.log(1.0 + jnp.exp(rows[10]))
    slope_x = conic_a * mean_x + conic_b * mean_y
    slope_y = conic_c * mean_y + conic_b * mean_x
    constant = log_opacity - 0.5 * (slope_x * mean_x + slope_y * mean_y)
    inverse_len = 1.0 / jnp.sqrt(view_x * view_x + world_y * world_y + view_z * view_z)
    basis = harmonics(
        (cos_yaw * view_x - sin_yaw * view_z) * inverse_len,
        world_y * inverse_len,
        (sin_yaw * view_x + cos_yaw * view_z) * inverse_len,
    )
    colors = []
    for channel in range(3):
        total = basis[0] * rows[11 + channel]
        for degree in range(1, 16):
            total = total + basis[degree] * rows[11 + 3 * degree + channel]
        colors.append(jnp.maximum(0.5 + total, 0.0))
    return [
        constant,
        slope_x,
        slope_y,
        -0.5 * conic_a,
        -conic_b,
        -0.5 * conic_c,
    ] + colors


def camera_of(codes, cos_ref, sin_ref):
    code = jnp.maximum(codes, 0).astype(f32)
    view = jnp.floor((code + 0.5) * (1.0 / TILES_VIEW))
    number = code - view * float(TILES_VIEW)
    across = jnp.floor((number + 0.5) * (1.0 / TILES_ACROSS))
    column = number - across * float(TILES_ACROSS)
    view = view.astype(i32)
    cos_yaw = jnp.take_along_axis(cos_ref[...], view, axis=1, mode="promise_in_bounds")
    sin_yaw = jnp.take_along_axis(sin_ref[...], view, axis=1, mode="promise_in_bounds")
    centre_x = column * 16.0 + (8.0 - 960.0)
    centre_y = across * 16.0 + (8.0 - 544.0)
    return cos_yaw, sin_yaw, centre_x, centre_y


def slot_parts(slot):
    line = jnp.right_shift(slot, 7)
    high = jnp.bitwise_and(line, 31)
    low = jnp.right_shift(line, 5) * 128 + jnp.bitwise_and(slot, 127)
    return high, low


def hot_rows(low, count=256):
    return (iota((count, low.shape[1]), 0) == low).astype(f32).astype(bf16)


def ask_kernel(plan_any, lists_any, req_any, out_ref, rank_ref, plan_ref, lists_ref, req_ref, sems):
    copies = [
        pltpu.make_async_copy(source, to, sems.at[k])
        for k, (source, to) in enumerate(
            ((lists_any, lists_ref), (plan_any, plan_ref), (req_any, req_ref))
        )
    ]
    for copy in copies:
        copy.start()
    copies[0].wait()
    tiles = jnp.zeros((64, 128), f32)
    for t in range(TILES):
        slot = lists_ref[t : t + 1, :]
        high, low = jnp.right_shift(slot, 7), jnp.bitwise_and(slot, 127)
        left = jnp.where(iota((64, LIST), 0) == high, float(t + 1), 0.0).astype(bf16)
        tiles = tiles + dot_t(left, hot_rows(low, 128))
    named = tiles > 0.0
    a, b = iota((128, 128), 0), iota((128, 128), 1)
    earlier = jnp.logical_and(a < b, jnp.right_shift(a, 6) == jnp.right_shift(b, 6))
    rank = dot(named.astype(f32).astype(bf16), earlier.astype(f32).astype(bf16))
    rank_ref[...] = rank
    gap = jnp.bitwise_and(iota((64, 128), 1), 63) - rank.astype(i32)
    copies[1].wait()
    copies[2].wait()
    held = req_ref[...] + tiles.astype(i32) * 4096 + gap * 131072
    held = jnp.where(named, held, 0)
    for k in range(6):
        ahead = pltpu.roll(held, 128 - (1 << k), 1)
        comes = jnp.bitwise_and(jnp.right_shift(ahead, 17 + k), 1) == 1
        stays = jnp.bitwise_and(jnp.right_shift(held, 17 + k), 1) == 0
        held = jnp.where(comes, ahead, jnp.where(stays, held, 0))
    asked = jnp.bitwise_and(held, 4095)
    tile = jnp.bitwise_and(jnp.right_shift(held, 12), 31)
    codes = jnp.full((64, 128), -1, i32)
    for t in range(TILES):
        codes = jnp.where(tile == t + 1, plan_ref[t], codes)
    first = iota((64, 128), 1) < 64
    out_ref[pl.ds(0, 64, stride=2), :] = jnp.where(first, asked, pltpu.roll(codes, 64, 1))
    out_ref[pl.ds(1, 64, stride=2), :] = jnp.where(first, pltpu.roll(asked, 64, 1), codes)


def relist_kernel(lists_ref, rank_ref, out_ref):
    rank = rank_ref[...]
    table = jnp.concatenate([rank[:32], rank[32:]], axis=1).astype(bf16)

    def tile(t, _):
        slot = lists_ref[pl.ds(t, 1), :]
        high, low = slot_parts(slot)
        found = jnp.where(iota((32, LIST), 0) == high, dot(table, hot_rows(low)), 0.0)
        place = jnp.sum(found, axis=0, keepdims=True).astype(i32)
        out_ref[pl.ds(t, 1), :] = slot - jnp.bitwise_and(slot, 63) + place
        return 0

    lax.fori_loop(0, TILES, tile, 0, unroll=4)


def turn_kernel(params_ref, out_ref):
    for h in range(16):
        block = params_ref[:, h * 256 : (h + 1) * 256]
        out_ref[h * 256 : (h + 1) * 256, :] = jnp.transpose(jnp.concatenate([block, block], axis=0))


FRONT = 32


def list_beyond(came, out_ref):
    lane = iota((128, 128), 1)
    used = jnp.where(jnp.logical_and(lane >= 64, came >= 0), 1.0, 0.0)
    count = jnp.broadcast_to(jnp.sum(used, axis=1, keepdims=True), (128, 128)).astype(i32)
    eights = jnp.right_shift(jnp.maximum(count - FRONT, 0) + 7, 3).astype(f32)
    upto = (lane <= iota((128, 128), 0)).astype(f32).astype(bf16)
    ends = dot(upto, eights.astype(bf16))
    for c in range(4):
        place = (iota((128, 128), 1) + c * 128).astype(f32)
        past = ends <= place
        asker = jnp.sum(jnp.where(past, 1.0, 0.0), axis=0, keepdims=True)
        begun = jnp.sum(jnp.where(past, eights, 0.0), axis=0, keepdims=True)
        slot = FRONT + 8.0 * (place[0:1] - begun)
        row = iota((8, 128), 0)
        lines = jnp.where(row == 0, asker, jnp.where(row == 1, slot, ends[127:128]))
        out_ref[:, c * 128 : (c + 1) * 128] = lines.astype(i32)


def by_groups(count, shift, body):
    size = 1 << shift
    groups = jnp.right_shift(count, shift)
    lax.fori_loop(0, groups, lambda k, _: body(k * size, size), None)
    lax.fori_loop(groups * size, count, lambda k, _: body(k, 1), None)


def answer_kernel(
    came_ref, turned_ref, cos_ref, sin_ref, out_ref, slots_ref, codes_ref, places_ref, beyond_ref,
    over, behind, values, index_s, beyond_s, index_sems, beyond_sem,
):
    index_copies = [
        pltpu.make_async_copy(came_ref.at[part], index_s.at[part], index_sems.at[k])
        for k, part in enumerate(pl.ds(32 * k, 32) for k in range(4))
    ]
    for copy in index_copies:
        copy.start()
    came = came_ref[...]
    list_beyond(came, beyond_ref)
    beyond_copy = pltpu.make_async_copy(beyond_ref, beyond_s, beyond_sem)
    beyond_copy.start()
    codes_ref[...] = jnp.transpose(came.astype(f32))[64:128].astype(i32)
    spare = OWN + jnp.bitwise_and(iota((128, 128), 1), 7)
    places_ref[...] = jnp.where(pltpu.roll(came, 64, 1) < 0, spare, came)

    def fetch(step, _):
        for k in range(2):
            p = 2 * step + k
            for j in range(FRONT):
                over[pl.ds(j * 128 + p, 1), :] = turned_ref[pl.ds(index_s[p, j], 1), :]
        return 0

    behind[...] = jnp.ones_like(behind)
    for k, copy in enumerate(index_copies):
        copy.wait()
        lax.fori_loop(16 * k, 16 * k + 16, fetch, 0)
    beyond_copy.wait()

    def fetch_beyond(first_k, count):
        for k in range(count):
            p, slot = beyond_s[0, first_k + k], beyond_s[1, first_k + k]
            for j in range(8):
                row = turned_ref[pl.ds(index_s[p, slot + j], 1), :]
                behind[pl.ds((slot - FRONT + j) * 128 + p, 1), :] = row

    by_groups(beyond_s[2, 0], 1, fetch_beyond)
    first = iota((128, 128), 1) < 64

    def spread(step, _):
        for k in range(8):
            part = pl.ds(pl.multiple_of((step * 8 + k) * 128, 128), 128)
            over[part, :] = jnp.transpose(jnp.where(first, over[part, :], behind[part, :]))
        return 0

    lax.fori_loop(0, FRONT // 8, spread, 0)

    for r in range(PARAM, 64):
        for g in range(8):
            slots_ref[g * 512 + r * 8 : g * 512 + r * 8 + 8, :] = jnp.zeros((8, 128), f32)

    def work(g, _):
        at = pl.multiple_of(g * 8, 8)
        base = jnp.bitwise_and(g, 3) * 1024 + jnp.right_shift(g, 2) * 64
        rows = [over[pl.ds(base + r, 8, stride=128), :] for r in range(PARAM)]
        for r in range(PARAM):
            slots_ref[pl.ds(pl.multiple_of(g * 512 + r * 8, 8), 8), :] = rows[r]
        camera = camera_of(codes_ref[pl.ds(at, 8), :], cos_ref, sin_ref)
        for q, value in enumerate(project_slots(rows, *camera)):
            values[pl.ds(pl.multiple_of(q * 64 + at, 8), 8), :] = value
        return 0

    values[SENT * 64 :, :] = jnp.zeros((64, 128), f32)
    lax.fori_loop(0, 8, work, 0)
    for line in range(LINES):
        block = values[line * 128 : (line + 1) * 128, :]
        out_ref[pl.ds(line, 128, stride=LINES), :] = jnp.transpose(block)


def monomials(x, y, which):
    out = jnp.zeros(x.shape, f32)
    for k, value in enumerate((jnp.ones_like(x), x, y, x * x, x * y, y * y)):
        out = jnp.where(which == k, value, out)
    return out


def render_kernel(
    came_ref, lists_ref, targets_ref, out_ref,
    table, hots, back, coefs0, coefs1, spread0, spread1, *work_refs,
):
    coefs, spreads = (coefs0, coefs1), (spread0, spread1)
    first = iota((64, 128), 1) < 64
    for q in range(SENT):
        line = q // 2
        even = came_ref[pl.ds(line, 64, stride=10), :]
        odd = came_ref[pl.ds(5 + line, 64, stride=10), :]
        if q % 2 == 0:
            dense = jnp.where(first, even, pltpu.roll(odd, 64, 1))
        else:
            dense = jnp.where(first, pltpu.roll(even, 64, 1), odd)
        square = jnp.concatenate([dense[:32], dense[32:]], axis=1)
        for s, part in enumerate(pieces(square, 3 if q < 6 else 2)):
            table[pl.ds(s * 288 + q * 32, 32), :] = part
    back[...] = jnp.zeros_like(back)
    spread1[...] = jnp.zeros_like(spread1)
    works = (work_refs[:7], work_refs[7:])
    row = iota((32, PIX), 0)
    pix = iota((32, PIX), 1)
    basis = monomials(
        jnp.bitwise_and(pix, 15).astype(f32) - 7.5,
        jnp.right_shift(pix, 4).astype(f32) - 7.5,
        jnp.where(row < 24, jnp.bitwise_and(row, 7), 7),
    ).astype(bf16)
    sub = iota((8, PIX), 0)
    lane = iota((8, 128), 1)
    offset_x = jnp.bitwise_and(lane, 15).astype(f32) - 7.5
    offset_y = jnp.right_shift(lane, 4).astype(f32) - 3.5
    square_y = offset_y * offset_y + 16.0
    eight_y = offset_y * 8.0

    def make_hot(t, _):
        hots[t] = hot_rows(slot_parts(lists_ref[pl.ds(t, 1), :])[1])
        return 0

    lax.fori_loop(0, TILES, make_hot, 0, unroll=2)

    def here_of(t):
        return iota((32, LIST), 0) == slot_parts(lists_ref[pl.ds(t, 1), :])[0]

    def gather(t, to):
        found = dot(table[...], hots[t])
        here = here_of(t)
        values = []
        for q in range(SENT):
            at = q * 32
            value = found[at : at + 32] + (
                found[288 + at : 320 + at] + found[576 + at : 608 + at]
                if q < 6
                else found[288 + at : 320 + at]
            )
            values.append(jnp.sum(jnp.where(here, value, 0.0), axis=0, keepdims=True))
        shape_rows = jnp.zeros((8, LIST), f32)
        color_rows = jnp.zeros((8, LIST), f32)
        for q in range(6):
            shape_rows = jnp.where(sub == q, values[q], shape_rows)
        for q in range(3):
            color_rows = jnp.where(sub == q, values[6 + q], color_rows)
        parts = [p.astype(f32) for p in pieces(shape_rows * log2_e, 3)]
        stack = jnp.concatenate(parts + [color_rows] + [jnp.zeros((96, LIST), f32)], axis=0)
        to[...] = jnp.transpose(stack)

    def scatter(t, source):
        here = here_of(t)
        parts = [p.astype(f32) for p in pieces(source[...], 2)]
        left = []
        for s in range(2):
            for q in range(SENT):
                value = jnp.broadcast_to(parts[s][q : q + 1], (32, LIST))
                left.append(jnp.where(here, value, 0.0).astype(bf16))
        moved = dot_t(jnp.concatenate(left, axis=0), hots[t])
        back[...] += moved[0:288] + moved[288:576]

    def scan8(x, neutral, op, down):
        def shift(y, n):
            if down:
                return jnp.where(sub >= n, pltpu.roll(y, n, 0), neutral)
            return jnp.where(sub < 8 - n, pltpu.roll(y, 8 - n, 0), neutral)

        x = shift(x, 1)
        for n in (1, 2, 4):
            x = op(x, shift(x, n))
        return x

    def rows_of(v):
        return slice(v * 8, v * 8 + 8)

    def twice(x):
        return jnp.concatenate([x, x], axis=1)

    def expose(source, refs):
        refs[0][...] = dot(source[:, 0:32].astype(bf16), basis)

    def forward(v, source, refs, carry):
        ratios, weights, tones = refs[0], refs[1], refs[5]
        product, seen = carry
        alpha = jnp.exp2(ratios[rows_of(v)])
        keep = 1.0 - alpha
        ratios[rows_of(v)] = alpha / keep
        weight = alpha * product
        weights[rows_of(v)] = weight
        out = []
        for c in range(3):
            tone = jnp.broadcast_to(source[rows_of(v), 24 + c : 25 + c], (8, 128))
            tones[c * 256 + v * 8 : c * 256 + v * 8 + 8] = tone
            out.append(seen[c] + weight * twice(tone))
        return product * keep, out

    def compare(t, carry, refs):
        product, seen = carry
        ahead = scan8(product, 1.0, jnp.multiply, True)
        for c in range(3):
            total = jnp.sum(seen[c] * ahead, axis=0, keepdims=True)
            pull = (total - targets_ref[t, c : c + 1, :]) * (1.0 / loss_scale)
            refs[6][c * 8 : c * 8 + 8] = jnp.broadcast_to(pull, (8, PIX)) * ahead

    def pull_back(v, refs, pulls, rest):
        weights, gains, behind, sums, tones = refs[1:6]
        weight = weights[rows_of(v)]
        gain = jnp.zeros((8, PIX), f32)
        line = jnp.zeros((8, 128), f32)
        for c in range(3):
            gain = gain + pulls[c] * twice(tones[c * 256 + v * 8 : c * 256 + v * 8 + 8])
            tint = weight * pulls[c]
            tint = jnp.sum(tint[:, :128] + tint[:, 128:], axis=1, keepdims=True)
            line = jnp.where(lane == 6 + c, tint, line)
        gain = gain * weight
        gains[rows_of(v)] = gain
        behind[rows_of(v)] = rest
        sums[rows_of(v)] = line
        return rest + gain

    def moments(v, refs, after):
        ratios, gains, behind, sums = refs[0], refs[2], refs[3], refs[4]
        slope = gains[rows_of(v)] - (behind[rows_of(v)] + after) * ratios[rows_of(v)]
        upper, lower = slope[:, :128], slope[:, 128:]
        both, apart = upper + lower, lower - upper
        along = both * offset_x
        down = both * offset_y + apart * 4.0
        line = sums[rows_of(v)]
        for k, value in enumerate(
            (both, along, down, along * offset_x, down * offset_x,
             both * square_y + apart * eight_y)
        ):
            line = jnp.where(lane == k, jnp.sum(value, axis=1, keepdims=True), line)
        sums[rows_of(v)] = line

    nothing = jnp.zeros((8, PIX), f32)
    begin = (jnp.ones((8, PIX), f32), [nothing] * 3)
    gather(0, coefs[0])
    gather(1, coefs[1])
    expose(coefs[0], works[0])
    carry = begin
    for v in range(32):
        carry = forward(v, coefs[0], works[0], carry)
    compare(0, carry, works[0])

    def pair(step, _):
        for k in range(2):
            t = 2 * step + k
            coming = jnp.minimum(t + 1, TILES - 1)
            here, there = works[k], works[1 - k]
            expose(coefs[1 - k], there)
            scatter(jnp.maximum(t - 1, 0), spreads[1 - k])
            pulls = [here[6][c * 8 : c * 8 + 8] for c in range(3)]
            carry, rest = begin, nothing
            for v in range(32):
                carry = forward(v, coefs[1 - k], there, carry)
                rest = pull_back(31 - v, here, pulls, rest)
            after = scan8(rest, 0.0, jnp.add, False)
            gather(jnp.minimum(t + 2, TILES - 1), coefs[k])
            for v in range(32):
                moments(v, here, after)
            compare(coming, carry, there)
            spreads[k][...] = jnp.transpose(here[4][...])[0:16]
        return 0

    lax.fori_loop(0, TILES // 2, pair, 0)
    scatter(TILES - 1, spreads[1])

    zero = jnp.zeros((64, 128), f32)

    def dense_of(q):
        if q >= SENT:
            return zero
        square = back[pl.ds(q * 32, 32), :]
        return jnp.concatenate([square[:, :128], square[:, 128:]], axis=0)

    for line in range(LINES):
        a, b = dense_of(2 * line), dense_of(2 * line + 1)
        out_ref[pl.ds(line, 64, stride=10), :] = jnp.where(first, a, pltpu.roll(b, 64, 1))
        out_ref[pl.ds(5 + line, 64, stride=10), :] = jnp.where(first, pltpu.roll(a, 64, 1), b)


def rates(shape):
    row = iota(shape, 0)
    out = jnp.full(shape, 0.000125, f32)
    for end, rate in ((14, 0.0025), (11, 0.05), (10, 0.001), (6, 0.005), (3, 0.0008)):
        out = jnp.where(row < end, rate, out)
    return out


def update_kernel(
    back_ref, places_ref, beyond_ref, slots_ref, codes_ref, cos_ref, sin_ref,
    params_ref, first_ref, second_ref, new_params_any, new_first_any, new_second_any,
    new_params_ref, new_first_ref, new_second_ref, out_sems,
    cots, grads, over, behind, even, odd, index_s, beyond_s, index_sem, beyond_sem,
):
    index_copy = pltpu.make_async_copy(places_ref, index_s, index_sem)
    beyond_copy = pltpu.make_async_copy(beyond_ref, beyond_s, beyond_sem)
    index_copy.start()
    beyond_copy.start()
    for line in range(LINES):
        block = back_ref[pl.ds(line, 128, stride=LINES), :]
        cots[line * 128 : (line + 1) * 128, :] = jnp.transpose(block)
    for r in range(PARAM, 64):
        for g in range(8):
            grads[g * 512 + r * 8 : g * 512 + r * 8 + 8, :] = jnp.zeros((8, 128), f32)

    def work(g, _):
        at = pl.multiple_of(g * 8, 8)
        lines = [pl.ds(pl.multiple_of(g * 512 + r * 8, 8), 8) for r in range(PARAM)]
        camera = camera_of(codes_ref[pl.ds(at, 8), :], cos_ref, sin_ref)
        _, pullback = jax.vjp(
            lambda r: project_slots(r, *camera), [slots_ref[line, :] for line in lines]
        )
        (out,) = pullback(
            [cots[pl.ds(pl.multiple_of(q * 64 + at, 8), 8), :] for q in range(SENT)]
        )
        for r in range(PARAM):
            grads[lines[r], :] = out[r]
        clear = pl.ds(pl.multiple_of(g * 512, 512), 512)
        for sums in (even, odd):
            sums[clear, :] = jnp.zeros((512, 128), f32)
        return 0

    lax.fori_loop(0, 8, work, 0)

    first = iota((128, 128), 1) < 64

    def spread(g, _):
        for k in range(8):
            block = [
                grads[pl.ds((g + half) * 512 + k + m * 64, 8, stride=8), :]
                for half in (0, 4)
                for m in range(8)
            ]
            at = pl.ds(pl.multiple_of((g * 8 + k) * 128, 128), 128)
            turned = jnp.transpose(jnp.concatenate(block, axis=0))
            over[at, :] = jnp.where(first, turned, 0.0)
            behind[at, :] = jnp.where(first, 0.0, turned)
        return 0

    lax.fori_loop(0, FRONT // 8, spread, 0)
    index_copy.wait()
    beyond_copy.wait()

    def add_eight(sums, source, p, slot, line):
        at = [pl.ds(index_s[p, slot + n], 1) for n in range(8)]
        new = [sums[at[n], :] + source[pl.ds((line + n) * 128 + p, 1), :] for n in range(8)]
        for n in range(8):
            sums[at[n], :] = new[n]

    def gather(step, _):
        for j in range(0, FRONT, 8):
            add_eight(even, over, 2 * step, j, j)
            add_eight(odd, over, 2 * step + 1, j, j)
        return 0

    lax.fori_loop(0, 64, gather, 0)

    def gather_beyond(first_k, count):
        for k in range(count):
            p, slot = beyond_s[0, first_k + k], beyond_s[1, first_k + k]
            add_eight((even, odd)[k % 2], behind, p, slot, slot - FRONT)

    by_groups(beyond_s[2, 0], 2, gather_beyond)
    bias_one = 1.0 - beta_one**STEP
    bias_two = 1.0 - beta_two**STEP
    rate = rates((PARAM, 256)) * (1.0 / bias_one)
    pending = []
    for h in range(16):
        cols = slice(h * 256, (h + 1) * 256)
        both = jnp.transpose(even[cols, :] + odd[cols, :])
        gradient = both[:PARAM] + both[64 : 64 + PARAM]
        first_new = beta_one * first_ref[:, cols] + (1.0 - beta_one) * gradient
        second_new = beta_two * second_ref[:, cols] + (1.0 - beta_two) * gradient * gradient
        new_first_ref[:, cols] = first_new
        new_second_ref[:, cols] = second_new
        scaled = second_new * (1.0 / bias_two)
        new_params_ref[:, cols] = params_ref[:, cols] - rate * first_new / (
            scaled * lax.rsqrt(scaled) + adam_eps
        )
        if h % 4 == 3:
            done = pl.ds((h - 3) * 256, 1024)
            for k, (near, far) in enumerate(
                (
                    (new_params_ref, new_params_any),
                    (new_first_ref, new_first_any),
                    (new_second_ref, new_second_any),
                )
            ):
                sem = out_sems.at[k, h // 4]
                pending.append(pltpu.make_async_copy(near.at[:, done], far.at[:, done], sem))
                pending[-1].start()
    for copy in pending:
        copy.wait()


def shape(rows, cols, dtype=f32):
    return jax.ShapeDtypeStruct((rows, cols), dtype)


def exchange(lines, count):
    sent = lines.reshape(128, 1, count * 128)
    came = lax.all_to_all(sent, AXES, split_axis=0, concat_axis=0, tiled=True)
    return came.reshape(128 * count, 128)


def shards(params, adam_first, adam_second, view_yaw, tile_plan, tile_lists, requests, targets):
    cos_yaw = jnp.broadcast_to(jnp.pad(jnp.cos(view_yaw), (0, 96))[None, :], (8, 128))
    sin_yaw = jnp.broadcast_to(jnp.pad(jnp.sin(view_yaw), (0, 96))[None, :], (8, 128))
    woven = jnp.transpose(tile_lists.reshape(TILES, 8, 32), (0, 2, 1)).reshape(TILES, LIST)
    asked, rank = call(
        ask_kernel,
        (shape(128, 128, i32), shape(64, 128)),
        "ask",
        scratch=[
            pltpu.SMEM((TILES,), i32),
            pltpu.VMEM((TILES, LIST), i32),
            pltpu.VMEM((64, 128), i32),
            pltpu.SemaphoreType.DMA((3,)),
        ],
        in_specs=[HB] * 3,
        mib=60,
    )(tile_plan, tile_lists, requests.reshape(64, 128))
    came = exchange(asked, 1)
    turned = call(turn_kernel, shape(OWN, 128), "turn", in_specs=[VM])(
        jnp.pad(params, ((0, 64 - PARAM), (0, 0)))
    )
    lists = call(relist_kernel, shape(TILES, LIST, i32), "relist", in_specs=[VM, VM])(woven, rank)
    aims = jnp.pad(jnp.transpose(targets, (1, 0, 2)), ((0, 0), (0, 5), (0, 0)))
    indexes = [
        pltpu.SMEM((128, 128), i32),
        pltpu.SMEM((8, 512), i32),
        pltpu.SemaphoreType.DMA,
        pltpu.SemaphoreType.DMA,
    ]
    answers, slots, codes, places, beyond = call(
        answer_kernel,
        (
            shape(128 * LINES, 128),
            shape(64 * 64, 128),
            shape(64, 128, i32),
            shape(128, 128, i32),
            shape(8, 512, i32),
        ),
        "answer",
        scratch=[
            pltpu.VMEM((OWN, 128), f32),
            pltpu.VMEM((OWN, 128), f32),
            pltpu.VMEM((128 * LINES, 128), f32),
        ]
        + indexes[:2]
        + [pltpu.SemaphoreType.DMA((4,)), pltpu.SemaphoreType.DMA],
        in_specs=[VM] * 4,
        flops=4_500_000_000,
    )(came, turned, cos_yaw, sin_yaw)
    arrived = exchange(answers, LINES)
    wide = pltpu.VMEM((LIST, PIX), f32)
    narrow = pltpu.VMEM((LIST, 128), f32)
    returned = call(
        render_kernel,
        shape(128 * LINES, 128),
        "render",
        scratch=[
            pltpu.VMEM((768, 256), bf16),
            pltpu.VMEM((TILES, 256, LIST), bf16),
            pltpu.VMEM((288, 256), f32),
            narrow,
            narrow,
        ]
        + [pltpu.VMEM((16, LIST), f32)] * 2
        + ([wide] * 4 + [narrow, pltpu.VMEM((3 * LIST, 128), f32), pltpu.VMEM((24, PIX), f32)]) * 2,
        in_specs=[VM] * 3,
        flops=5_000_000_000,
    )(arrived, lists, aims)
    back = exchange(returned, LINES)
    return call(
        update_kernel,
        (shape(PARAM, OWN), shape(PARAM, OWN), shape(PARAM, OWN)),
        "update",
        scratch=[pltpu.VMEM((PARAM, OWN), f32)] * 3
        + [
            pltpu.SemaphoreType.DMA((3, 4)),
            pltpu.VMEM((128 * LINES, 128), f32),
            pltpu.VMEM((64 * 64, 128), f32),
            pltpu.VMEM((OWN, 128), f32),
            pltpu.VMEM((OWN, 128), f32),
        ]
        + [pltpu.VMEM((OWN + 8, 128), f32)] * 2
        + indexes,
        in_specs=[VM] * 10,
        out_specs=(HB, HB, HB),
        flops=4_500_000_000,
        mib=24,
    )(back, places, beyond, slots, codes, cos_yaw, sin_yaw, params, adam_first, adam_second)


def solution(mesh):
    placed = (
        P(None, AXES),
        P(None, AXES),
        P(None, AXES),
        P(),
        P(AXES),
        P(AXES, None),
        P(AXES, None),
        P(None, AXES, None),
    )
    return jax.shard_map(
        shards,
        mesh=mesh,
        in_specs=placed,
        out_specs=(P(None, AXES), P(None, AXES), P(None, AXES)),
        check_vma=False,
    )
```

```python
from functools import partial

import jax
import jax.numpy as jnp
from jax import lax
from jax.experimental import pallas as pl
from jax.experimental.pallas import tpu as pltpu
from jax.sharding import PartitionSpec as P

AXES = ("img", "blk")
STEP = 1000
TILES_ACROSS = 120
TILES_VIEW = 8160
TILE_EDGE = 16
PARAM = 59
OWN = 4096
SLOTS = 8192
TILES = 16
LIST = 256
PIX = 256
SENT = 9
LINES = 5

focal_px = 2400.0
camera_distance = 10.0
low_pass = 0.3
loss_scale = 16.0
beta_one = 0.9
beta_two = 0.999
adam_eps = 1e-08
log2_e = 1.4426950408889634
band_zero = 0.28209479177387814
band_one = 0.4886025119029199
band_two = (
    1.0925484305920792,
    -1.0925484305920792,
    0.31539156525252005,
    -1.0925484305920792,
    0.5462742152960396,
)
band_three = (
    -0.5900435899266435,
    2.890611442640554,
    -0.4570457994644658,
    0.3731763325901154,
    -0.4570457994644658,
    1.445305721320277,
    -0.5900435899266435,
)
f32 = jnp.float32
bf16 = jnp.bfloat16
i32 = jnp.int32
VM = pl.BlockSpec(memory_space=pltpu.VMEM)
SM = pl.BlockSpec(memory_space=pltpu.SMEM)
HB = pl.BlockSpec(memory_space=pltpu.HBM)


def iota(shape, dim):
    return lax.broadcasted_iota(i32, shape, dim)


def dot(a, b):
    return lax.dot_general(a, b, (((1,), (0,)), ((), ())), preferred_element_type=f32)


def dot_t(a, b):
    return lax.dot_general(a, b, (((1,), (1,)), ((), ())), preferred_element_type=f32)


def pieces(x, count):
    out = []
    for k in range(count):
        part = x.astype(bf16)
        out.append(part)
        if k + 1 < count:
            x = x - part.astype(f32)
    return out


def call(kernel, out_shape, name, scratch=(), in_specs=None, out_specs=None, flops=0, mib=16):
    return partial(
        pl.pallas_call,
        kernel,
        out_shape=out_shape,
        in_specs=in_specs,
        out_specs=out_specs or jax.tree.map(lambda _: VM, out_shape),
        scratch_shapes=list(scratch),
        name=name,
        cost_estimate=pl.CostEstimate(flops=flops, bytes_accessed=4 << 20, transcendentals=0),
        compiler_params=pltpu.CompilerParams(vmem_limit_bytes=mib << 20),
    )()


def harmonics(looking_x, look_y, look_z):
    square_x = looking_x * looking_x
    square_y = look_y * look_y
    square_z = look_z * look_z
    return [
        jnp.full_like(looking_x, band_zero),
        -band_one * look_y,
        band_one * look_z,
        -band_one * looking_x,
        band_two[0] * looking_x * look_y,
        band_two[1] * look_y * look_z,
        band_two[2] * (2.0 * square_z - square_x - square_y),
        band_two[3] * looking_x * look_z,
        band_two[4] * (square_x - square_y),
        band_three[0] * look_y * (3.0 * square_x - square_y),
        band_three[1] * looking_x * look_y * look_z,
        band_three[2] * look_y * (4.0 * square_z - square_x - square_y),
        band_three[3] * look_z * (2.0 * square_z - 3.0 * square_x - 3.0 * square_y),
        band_three[4] * looking_x * (4.0 * square_z - square_x - square_y),
        band_three[5] * look_z * (square_x - square_y),
        band_three[6] * looking_x * (square_x - 3.0 * square_y),
    ]


def project_slots(rows, cos_yaw, sin_yaw, centre_x, centre_y):
    world_x, world_y, world_z = rows[0], rows[1], rows[2]
    view_x = cos_yaw * world_x + sin_yaw * world_z
    view_z = cos_yaw * world_z - sin_yaw * world_x + camera_distance
    inverse_z = 1.0 / view_z
    mean_x = focal_px * view_x * inverse_z - centre_x
    mean_y = focal_px * world_y * inverse_z - centre_y
    scales = [jnp.exp(rows[3 + k]) for k in range(3)]
    norm = jnp.sqrt(
        rows[6] * rows[6] + rows[7] * rows[7] + rows[8] * rows[8] + rows[9] * rows[9]
    )
    inverse_norm = 1.0 / norm
    quat_w, quat_x, quat_y, quat_z = [rows[6 + k] * inverse_norm for k in range(4)]
    rotation = [
        [
            1.0 - 2.0 * (quat_y * quat_y + quat_z * quat_z),
            2.0 * (quat_x * quat_y - quat_w * quat_z),
            2.0 * (quat_x * quat_z + quat_w * quat_y),
        ],
        [
            2.0 * (quat_x * quat_y + quat_w * quat_z),
            1.0 - 2.0 * (quat_x * quat_x + quat_z * quat_z),
            2.0 * (quat_y * quat_z - quat_w * quat_x),
        ],
        [
            2.0 * (quat_x * quat_z - quat_w * quat_y),
            2.0 * (quat_y * quat_z + quat_w * quat_x),
            1.0 - 2.0 * (quat_x * quat_x + quat_y * quat_y),
        ],
    ]
    focal_z = focal_px * inverse_z
    shear_x = focal_z * view_x * inverse_z
    shear_y = focal_z * world_y * inverse_z
    jacob_ax = focal_z * cos_yaw + shear_x * sin_yaw
    jacob_az = focal_z * sin_yaw - shear_x * cos_yaw
    jacob_bx = shear_y * sin_yaw
    jacob_bz = -shear_y * cos_yaw
    row_a = [
        (jacob_ax * rotation[0][k] + jacob_az * rotation[2][k]) * scales[k] for k in range(3)
    ]
    row_b = [
        (jacob_bx * rotation[0][k] + focal_z * rotation[1][k] + jacob_bz * rotation[2][k])
        * scales[k]
        for k in range(3)
    ]
    covar_xx = row_a[0] * row_a[0] + row_a[1] * row_a[1] + row_a[2] * row_a[2] + low_pass
    covar_yy = row_b[0] * row_b[0] + row_b[1] * row_b[1] + row_b[2] * row_b[2] + low_pass
    covar_xy = row_a[0] * row_b[0] + row_a[1] * row_b[1] + row_a[2] * row_b[2]
    inverse_det = 1.0 / (covar_xx * covar_yy - covar_xy * covar_xy)
    conic_a = covar_yy * inverse_det
    conic_b = -covar_xy * inverse_det
    conic_c = covar_xx * inverse_det
    log_opacity = rows[10] - jnp.log(1.0 + jnp.exp(rows[10]))
    slope_x = conic_a * mean_x + conic_b * mean_y
    slope_y = conic_c * mean_y + conic_b * mean_x
    constant = log_opacity - 0.5 * (slope_x * mean_x + slope_y * mean_y)
    inverse_len = 1.0 / jnp.sqrt(view_x * view_x + world_y * world_y + view_z * view_z)
    basis = harmonics(
        (cos_yaw * view_x - sin_yaw * view_z) * inverse_len,
        world_y * inverse_len,
        (sin_yaw * view_x + cos_yaw * view_z) * inverse_len,
    )
    colors = []
    for channel in range(3):
        total = basis[0] * rows[11 + channel]
        for degree in range(1, 16):
            total = total + basis[degree] * rows[11 + 3 * degree + channel]
        colors.append(jnp.maximum(0.5 + total, 0.0))
    return [
        constant,
        slope_x,
        slope_y,
        -0.5 * conic_a,
        -conic_b,
        -0.5 * conic_c,
    ] + colors


def camera_of(codes, cos_ref, sin_ref):
    code = jnp.maximum(codes, 0).astype(f32)
    view = jnp.floor((code + 0.5) * (1.0 / TILES_VIEW))
    number = code - view * float(TILES_VIEW)
    across = jnp.floor((number + 0.5) * (1.0 / TILES_ACROSS))
    column = number - across * float(TILES_ACROSS)
    view = view.astype(i32)
    cos_yaw = jnp.take_along_axis(cos_ref[...], view, axis=1, mode="promise_in_bounds")
    sin_yaw = jnp.take_along_axis(sin_ref[...], view, axis=1, mode="promise_in_bounds")
    centre_x = column * 16.0 + (8.0 - 960.0)
    centre_y = across * 16.0 + (8.0 - 544.0)
    return cos_yaw, sin_yaw, centre_x, centre_y


def slot_parts(slot):
    line = jnp.right_shift(slot, 7)
    high = jnp.bitwise_and(line, 31)
    low = jnp.right_shift(line, 5) * 128 + jnp.bitwise_and(slot, 127)
    return high, low


def hot_rows(low, count=256):
    return (iota((count, low.shape[1]), 0) == low).astype(f32).astype(bf16)


def ask_kernel(plan_any, lists_any, req_any, out_ref, rank_ref, plan_ref, lists_ref, req_ref, sems):
    copies = [
        pltpu.make_async_copy(source, to, sems.at[k])
        for k, (source, to) in enumerate(
            ((lists_any, lists_ref), (plan_any, plan_ref), (req_any, req_ref))
        )
    ]
    for copy in copies:
        copy.start()
    copies[0].wait()
    tiles = jnp.zeros((64, 128), f32)
    for t in range(TILES):
        slot = lists_ref[t : t + 1, :]
        high, low = jnp.right_shift(slot, 7), jnp.bitwise_and(slot, 127)
        left = jnp.where(iota((64, LIST), 0) == high, float(t + 1), 0.0).astype(bf16)
        tiles = tiles + dot_t(left, hot_rows(low, 128))
    named = tiles > 0.0
    a, b = iota((128, 128), 0), iota((128, 128), 1)
    earlier = jnp.logical_and(a < b, jnp.right_shift(a, 6) == jnp.right_shift(b, 6))
    rank = dot(named.astype(f32).astype(bf16), earlier.astype(f32).astype(bf16))
    rank_ref[...] = rank
    gap = jnp.bitwise_and(iota((64, 128), 1), 63) - rank.astype(i32)
    copies[1].wait()
    copies[2].wait()
    held = req_ref[...] + tiles.astype(i32) * 4096 + gap * 131072
    held = jnp.where(named, held, 0)
    for k in range(6):
        ahead = pltpu.roll(held, 128 - (1 << k), 1)
        comes = jnp.bitwise_and(jnp.right_shift(ahead, 17 + k), 1) == 1
        stays = jnp.bitwise_and(jnp.right_shift(held, 17 + k), 1) == 0
        held = jnp.where(comes, ahead, jnp.where(stays, held, 0))
    asked = jnp.bitwise_and(held, 4095)
    tile = jnp.bitwise_and(jnp.right_shift(held, 12), 31)
    codes = jnp.full((64, 128), -1, i32)
    for t in range(TILES):
        codes = jnp.where(tile == t + 1, plan_ref[t], codes)
    first = iota((64, 128), 1) < 64
    out_ref[pl.ds(0, 64, stride=2), :] = jnp.where(first, asked, pltpu.roll(codes, 64, 1))
    out_ref[pl.ds(1, 64, stride=2), :] = jnp.where(first, pltpu.roll(asked, 64, 1), codes)


def relist_kernel(lists_ref, rank_ref, out_ref):
    rank = rank_ref[...]
    table = jnp.concatenate([rank[:32], rank[32:]], axis=1).astype(bf16)

    def tile(t, _):
        slot = lists_ref[pl.ds(t, 1), :]
        high, low = slot_parts(slot)
        found = jnp.where(iota((32, LIST), 0) == high, dot(table, hot_rows(low)), 0.0)
        place = jnp.sum(found, axis=0, keepdims=True).astype(i32)
        out_ref[pl.ds(t, 1), :] = slot - jnp.bitwise_and(slot, 63) + place
        return 0

    lax.fori_loop(0, TILES, tile, 0, unroll=4)


def turn_kernel(params_ref, out_ref):
    for h in range(16):
        block = params_ref[:, h * 256 : (h + 1) * 256]
        out_ref[h * 256 : (h + 1) * 256, :] = jnp.transpose(jnp.concatenate([block, block], axis=0))


FRONT = 32


def list_beyond(came, out_ref):
    lane = iota((128, 128), 1)
    used = jnp.where(jnp.logical_and(lane >= 64, came >= 0), 1.0, 0.0)
    count = jnp.broadcast_to(jnp.sum(used, axis=1, keepdims=True), (128, 128)).astype(i32)
    eights = jnp.right_shift(jnp.maximum(count - FRONT, 0) + 7, 3).astype(f32)
    upto = (lane <= iota((128, 128), 0)).astype(f32).astype(bf16)
    ends = dot(upto, eights.astype(bf16))
    for c in range(4):
        place = (iota((128, 128), 1) + c * 128).astype(f32)
        past = ends <= place
        asker = jnp.sum(jnp.where(past, 1.0, 0.0), axis=0, keepdims=True)
        begun = jnp.sum(jnp.where(past, eights, 0.0), axis=0, keepdims=True)
        slot = FRONT + 8.0 * (place[0:1] - begun)
        row = iota((8, 128), 0)
        lines = jnp.where(row == 0, asker, jnp.where(row == 1, slot, ends[127:128]))
        out_ref[:, c * 128 : (c + 1) * 128] = lines.astype(i32)


def by_groups(count, shift, body):
    size = 1 << shift
    groups = jnp.right_shift(count, shift)
    lax.fori_loop(0, groups, lambda k, _: body(k * size, size), None)
    lax.fori_loop(groups * size, count, lambda k, _: body(k, 1), None)


def answer_kernel(
    came_ref, turned_ref, cos_ref, sin_ref, out_ref, slots_ref, codes_ref, places_ref, beyond_ref,
    over, behind, values, index_s, beyond_s, index_sems, beyond_sem,
):
    index_copies = [
        pltpu.make_async_copy(came_ref.at[part], index_s.at[part], index_sems.at[k])
        for k, part in enumerate(pl.ds(32 * k, 32) for k in range(4))
    ]
    for copy in index_copies:
        copy.start()
    came = came_ref[...]
    list_beyond(came, beyond_ref)
    beyond_copy = pltpu.make_async_copy(beyond_ref, beyond_s, beyond_sem)
    beyond_copy.start()
    codes_ref[...] = jnp.transpose(came.astype(f32))[64:128].astype(i32)
    spare = OWN + jnp.bitwise_and(iota((128, 128), 1), 7)
    places_ref[...] = jnp.where(pltpu.roll(came, 64, 1) < 0, spare, came)

    def fetch(step, _):
        for k in range(2):
            p = 2 * step + k
            for j in range(FRONT):
                over[pl.ds(j * 128 + p, 1), :] = turned_ref[pl.ds(index_s[p, j], 1), :]
        behind[pl.ds(pl.multiple_of(step * 64, 64), 64), :] = jnp.ones((64, 128), f32)
        return 0

    for k, copy in enumerate(index_copies):
        copy.wait()
        lax.fori_loop(16 * k, 16 * k + 16, fetch, 0)
    beyond_copy.wait()

    def fetch_beyond(first_k, count):
        for k in range(count):
            p, slot = beyond_s[0, first_k + k], beyond_s[1, first_k + k]
            for j in range(8):
                row = turned_ref[pl.ds(index_s[p, slot + j], 1), :]
                behind[pl.ds((slot - FRONT + j) * 128 + p, 1), :] = row

    by_groups(beyond_s[2, 0], 1, fetch_beyond)
    first = iota((128, 128), 1) < 64

    def spread(step, _):
        for k in range(8):
            part = pl.ds(pl.multiple_of((step * 8 + k) * 128, 128), 128)
            over[part, :] = jnp.transpose(jnp.where(first, over[part, :], behind[part, :]))
        return 0

    lax.fori_loop(0, FRONT // 8, spread, 0)

    for r in range(PARAM, 64):
        for g in range(8):
            slots_ref[g * 512 + r * 8 : g * 512 + r * 8 + 8, :] = jnp.zeros((8, 128), f32)

    def work(g, _):
        at = pl.multiple_of(g * 8, 8)
        base = jnp.bitwise_and(g, 3) * 1024 + jnp.right_shift(g, 2) * 64
        rows = [over[pl.ds(base + r, 8, stride=128), :] for r in range(PARAM)]
        for r in range(PARAM):
            slots_ref[pl.ds(pl.multiple_of(g * 512 + r * 8, 8), 8), :] = rows[r]
        camera = camera_of(codes_ref[pl.ds(at, 8), :], cos_ref, sin_ref)
        for q, value in enumerate(project_slots(rows, *camera)):
            values[pl.ds(pl.multiple_of(q * 64 + at, 8), 8), :] = value
        return 0

    values[SENT * 64 :, :] = jnp.zeros((64, 128), f32)
    lax.fori_loop(0, 8, work, 0)
    for line in range(LINES):
        block = values[line * 128 : (line + 1) * 128, :]
        out_ref[pl.ds(line, 128, stride=LINES), :] = jnp.transpose(block)


def monomials(x, y, which):
    out = jnp.zeros(x.shape, f32)
    for k, value in enumerate((jnp.ones_like(x), x, y, x * x, x * y, y * y)):
        out = jnp.where(which == k, value, out)
    return out


def render_kernel(
    came_ref, lists_ref, targets_ref, out_ref,
    table, hots, back, coefs0, coefs1, spread0, spread1, *work_refs,
):
    coefs, spreads = (coefs0, coefs1), (spread0, spread1)
    first = iota((64, 128), 1) < 64
    for q in range(SENT):
        line = q // 2
        even = came_ref[pl.ds(line, 64, stride=10), :]
        odd = came_ref[pl.ds(5 + line, 64, stride=10), :]
        if q % 2 == 0:
            dense = jnp.where(first, even, pltpu.roll(odd, 64, 1))
        else:
            dense = jnp.where(first, pltpu.roll(even, 64, 1), odd)
        square = jnp.concatenate([dense[:32], dense[32:]], axis=1)
        for s, part in enumerate(pieces(square, 3 if q < 3 else 2)):
            table[pl.ds(s * 288 + q * 32, 32), :] = part
    back[...] = jnp.zeros_like(back)
    spread1[...] = jnp.zeros_like(spread1)
    works = (work_refs[:7], work_refs[7:])
    row = iota((32, PIX), 0)
    pix = iota((32, PIX), 1)
    basis = monomials(
        jnp.bitwise_and(pix, 15).astype(f32) - 7.5,
        jnp.right_shift(pix, 4).astype(f32) - 7.5,
        jnp.where(row < 24, jnp.bitwise_and(row, 7), 7),
    ).astype(bf16)
    sub = iota((8, PIX), 0)
    lane = iota((8, 128), 1)
    offset_x = jnp.bitwise_and(lane, 15).astype(f32) - 7.5
    offset_y = jnp.right_shift(lane, 4).astype(f32) - 3.5
    square_y = offset_y * offset_y + 16.0
    eight_y = offset_y * 8.0

    def make_hot(t, _):
        hots[t] = hot_rows(slot_parts(lists_ref[pl.ds(t, 1), :])[1])
        return 0

    lax.fori_loop(0, TILES, make_hot, 0, unroll=2)

    def here_of(t):
        return iota((32, LIST), 0) == slot_parts(lists_ref[pl.ds(t, 1), :])[0]

    def gather(t, to):
        found = dot(table[...], hots[t])
        here = here_of(t)
        values = []
        for q in range(SENT):
            at = q * 32
            value = found[at : at + 32] + (
                found[288 + at : 320 + at] + found[576 + at : 608 + at]
                if q < 3
                else found[288 + at : 320 + at]
            )
            values.append(jnp.sum(jnp.where(here, value, 0.0), axis=0, keepdims=True))
        shape_rows = jnp.zeros((8, LIST), f32)
        color_rows = jnp.zeros((8, LIST), f32)
        for q in range(6):
            shape_rows = jnp.where(sub == q, values[q], shape_rows)
        for q in range(3):
            color_rows = jnp.where(sub == q, values[6 + q], color_rows)
        parts = [p.astype(f32) for p in pieces(shape_rows * log2_e, 3)]
        stack = jnp.concatenate(parts + [color_rows] + [jnp.zeros((96, LIST), f32)], axis=0)
        to[...] = jnp.transpose(stack)

    def scatter(t, source):
        here = here_of(t)
        parts = [p.astype(f32) for p in pieces(source[...], 2)]
        left = []
        for s in range(2):
            for q in range(SENT):
                value = jnp.broadcast_to(parts[s][q : q + 1], (32, LIST))
                left.append(jnp.where(here, value, 0.0).astype(bf16))
        moved = dot_t(jnp.concatenate(left, axis=0), hots[t])
        back[...] += moved[0:288] + moved[288:576]

    def scan8(x, neutral, op, down):
        def shift(y, n):
            if down:
                return jnp.where(sub >= n, pltpu.roll(y, n, 0), neutral)
            return jnp.where(sub < 8 - n, pltpu.roll(y, 8 - n, 0), neutral)

        x = shift(x, 1)
        for n in (1, 2, 4):
            x = op(x, shift(x, n))
        return x

    def rows_of(v):
        return slice(v * 8, v * 8 + 8)

    def twice(x):
        return jnp.concatenate([x, x], axis=1)

    def expose(source, refs):
        refs[0][...] = dot(source[:, 0:32].astype(bf16), basis)

    def forward(v, source, refs, carry):
        ratios, weights, tones = refs[0], refs[1], refs[5]
        product, seen = carry
        alpha = jnp.exp2(ratios[rows_of(v)])
        keep = 1.0 - alpha
        ratios[rows_of(v)] = alpha / keep
        weight = alpha * product
        weights[rows_of(v)] = weight
        out = []
        for c in range(3):
            tone = jnp.broadcast_to(source[rows_of(v), 24 + c : 25 + c], (8, 128))
            tones[c * 256 + v * 8 : c * 256 + v * 8 + 8] = tone
            out.append(seen[c] + weight * twice(tone))
        return product * keep, out

    def compare(t, carry, refs):
        product, seen = carry
        ahead = scan8(product, 1.0, jnp.multiply, True)
        for c in range(3):
            total = jnp.sum(seen[c] * ahead, axis=0, keepdims=True)
            pull = (total - targets_ref[t, c : c + 1, :]) * (1.0 / loss_scale)
            refs[6][c * 8 : c * 8 + 8] = jnp.broadcast_to(pull, (8, PIX)) * ahead

    def pull_back(v, refs, pulls, rest):
        weights, gains, behind, sums, tones = refs[1:6]
        weight = weights[rows_of(v)]
        gain = jnp.zeros((8, PIX), f32)
        line = jnp.zeros((8, 128), f32)
        for c in range(3):
            gain = gain + pulls[c] * twice(tones[c * 256 + v * 8 : c * 256 + v * 8 + 8])
            tint = weight * pulls[c]
            tint = jnp.sum(tint[:, :128] + tint[:, 128:], axis=1, keepdims=True)
            line = jnp.where(lane == 6 + c, tint, line)
        gain = gain * weight
        gains[rows_of(v)] = gain
        behind[rows_of(v)] = rest
        sums[rows_of(v)] = line
        return rest + gain

    def moments(v, refs, after):
        ratios, gains, behind, sums = refs[0], refs[2], refs[3], refs[4]
        slope = gains[rows_of(v)] - (behind[rows_of(v)] + after) * ratios[rows_of(v)]
        upper, lower = slope[:, :128], slope[:, 128:]
        both, apart = upper + lower, lower - upper
        along = both * offset_x
        down = both * offset_y + apart * 4.0
        line = sums[rows_of(v)]
        for k, value in enumerate(
            (both, along, down, along * offset_x, down * offset_x,
             both * square_y + apart * eight_y)
        ):
            line = jnp.where(lane == k, jnp.sum(value, axis=1, keepdims=True), line)
        sums[rows_of(v)] = line

    nothing = jnp.zeros((8, PIX), f32)
    begin = (jnp.ones((8, PIX), f32), [nothing] * 3)
    gather(0, coefs[0])
    gather(1, coefs[1])
    expose(coefs[0], works[0])
    carry = begin
    for v in range(32):
        carry = forward(v, coefs[0], works[0], carry)
    compare(0, carry, works[0])

    def pair(step, _):
        for k in range(2):
            t = 2 * step + k
            coming = jnp.minimum(t + 1, TILES - 1)
            here, there = works[k], works[1 - k]
            expose(coefs[1 - k], there)
            scatter(jnp.maximum(t - 1, 0), spreads[1 - k])
            pulls = [here[6][c * 8 : c * 8 + 8] for c in range(3)]
            carry, rest = begin, nothing
            for v in range(32):
                carry = forward(v, coefs[1 - k], there, carry)
                rest = pull_back(31 - v, here, pulls, rest)
            after = scan8(rest, 0.0, jnp.add, False)
            for v in range(32):
                moments(v, here, after)
            gather(jnp.minimum(t + 2, TILES - 1), coefs[k])
            compare(coming, carry, there)
            spreads[k][...] = jnp.transpose(here[4][...])[0:16]
        return 0

    lax.fori_loop(0, TILES // 2, pair, 0)
    scatter(TILES - 1, spreads[1])

    zero = jnp.zeros((64, 128), f32)

    def dense_of(q):
        if q >= SENT:
            return zero
        square = back[pl.ds(q * 32, 32), :]
        return jnp.concatenate([square[:, :128], square[:, 128:]], axis=0)

    for line in range(LINES):
        a, b = dense_of(2 * line), dense_of(2 * line + 1)
        out_ref[pl.ds(line, 64, stride=10), :] = jnp.where(first, a, pltpu.roll(b, 64, 1))
        out_ref[pl.ds(5 + line, 64, stride=10), :] = jnp.where(first, pltpu.roll(a, 64, 1), b)


def rates(shape):
    row = iota(shape, 0)
    out = jnp.full(shape, 0.000125, f32)
    for end, rate in ((14, 0.0025), (11, 0.05), (10, 0.001), (6, 0.005), (3, 0.0008)):
        out = jnp.where(row < end, rate, out)
    return out


def update_kernel(
    back_ref, places_ref, beyond_ref, slots_ref, codes_ref, cos_ref, sin_ref,
    params_ref, first_ref, second_ref, new_params_any, new_first_any, new_second_any,
    new_params_ref, new_first_ref, new_second_ref, out_sems,
    cots, grads, over, behind, even, odd, index_s, beyond_s, index_sem, beyond_sem,
):
    index_copy = pltpu.make_async_copy(places_ref, index_s, index_sem)
    beyond_copy = pltpu.make_async_copy(beyond_ref, beyond_s, beyond_sem)
    index_copy.start()
    beyond_copy.start()
    for line in range(LINES):
        block = back_ref[pl.ds(line, 128, stride=LINES), :]
        cots[line * 128 : (line + 1) * 128, :] = jnp.transpose(block)
    for r in range(PARAM, 64):
        for g in range(8):
            grads[g * 512 + r * 8 : g * 512 + r * 8 + 8, :] = jnp.zeros((8, 128), f32)

    def work(g, _):
        at = pl.multiple_of(g * 8, 8)
        lines = [pl.ds(pl.multiple_of(g * 512 + r * 8, 8), 8) for r in range(PARAM)]
        camera = camera_of(codes_ref[pl.ds(at, 8), :], cos_ref, sin_ref)
        _, pullback = jax.vjp(
            lambda r: project_slots(r, *camera), [slots_ref[line, :] for line in lines]
        )
        (out,) = pullback(
            [cots[pl.ds(pl.multiple_of(q * 64 + at, 8), 8), :] for q in range(SENT)]
        )
        for r in range(PARAM):
            grads[lines[r], :] = out[r]
        return 0

    lax.fori_loop(0, 8, work, 0)

    first = iota((128, 128), 1) < 64

    def spread(g, _):
        for k in range(8):
            block = [
                grads[pl.ds((g + half) * 512 + k + m * 64, 8, stride=8), :]
                for half in (0, 4)
                for m in range(8)
            ]
            at = pl.ds(pl.multiple_of((g * 8 + k) * 128, 128), 128)
            turned = jnp.transpose(jnp.concatenate(block, axis=0))
            over[at, :] = jnp.where(first, turned, 0.0)
            behind[at, :] = jnp.where(first, 0.0, turned)
            for sums in (even, odd):
                sums[at, :] = jnp.zeros((128, 128), f32)
        return 0

    lax.fori_loop(0, FRONT // 8, spread, 0)
    index_copy.wait()
    beyond_copy.wait()

    def add_eight(sums, source, p, slot, line):
        at = [pl.ds(index_s[p, slot + n], 1) for n in range(8)]
        new = [sums[at[n], :] + source[pl.ds((line + n) * 128 + p, 1), :] for n in range(8)]
        for n in range(8):
            sums[at[n], :] = new[n]

    def gather(step, _):
        for j in range(0, FRONT, 8):
            add_eight(even, over, 2 * step, j, j)
            add_eight(odd, over, 2 * step + 1, j, j)
        return 0

    lax.fori_loop(0, 64, gather, 0)

    def gather_beyond(first_k, count):
        for k in range(count):
            p, slot = beyond_s[0, first_k + k], beyond_s[1, first_k + k]
            add_eight((even, odd)[k % 2], behind, p, slot, slot - FRONT)

    by_groups(beyond_s[2, 0], 2, gather_beyond)
    bias_one = 1.0 - beta_one**STEP
    bias_two = 1.0 - beta_two**STEP
    rate = rates((PARAM, 256)) * (1.0 / bias_one)
    pending = []
    for h in range(16):
        cols = slice(h * 256, (h + 1) * 256)
        both = jnp.transpose(even[cols, :] + odd[cols, :])
        gradient = both[:PARAM] + both[64 : 64 + PARAM]
        first_new = beta_one * first_ref[:, cols] + (1.0 - beta_one) * gradient
        second_new = beta_two * second_ref[:, cols] + (1.0 - beta_two) * gradient * gradient
        new_first_ref[:, cols] = first_new
        new_second_ref[:, cols] = second_new
        scaled = second_new * (1.0 / bias_two)
        new_params_ref[:, cols] = params_ref[:, cols] - rate * first_new / (
            scaled * lax.rsqrt(scaled) + adam_eps
        )
        if h % 4 == 3:
            done = pl.ds((h - 3) * 256, 1024)
            for k, (near, far) in enumerate(
                (
                    (new_params_ref, new_params_any),
                    (new_first_ref, new_first_any),
                    (new_second_ref, new_second_any),
                )
            ):
                sem = out_sems.at[k, h // 4]
                pending.append(pltpu.make_async_copy(near.at[:, done], far.at[:, done], sem))
                pending[-1].start()
    for copy in pending:
        copy.wait()


def shape(rows, cols, dtype=f32):
    return jax.ShapeDtypeStruct((rows, cols), dtype)


def exchange(lines, count):
    sent = lines.reshape(128, 1, count * 128)
    came = lax.all_to_all(sent, AXES, split_axis=0, concat_axis=0, tiled=True)
    return came.reshape(128 * count, 128)


def shards(params, adam_first, adam_second, view_yaw, tile_plan, tile_lists, requests, targets):
    cos_yaw = jnp.broadcast_to(jnp.pad(jnp.cos(view_yaw), (0, 96))[None, :], (8, 128))
    sin_yaw = jnp.broadcast_to(jnp.pad(jnp.sin(view_yaw), (0, 96))[None, :], (8, 128))
    woven = jnp.transpose(tile_lists.reshape(TILES, 8, 32), (0, 2, 1)).reshape(TILES, LIST)
    asked, rank = call(
        ask_kernel,
        (shape(128, 128, i32), shape(64, 128)),
        "ask",
        scratch=[
            pltpu.SMEM((TILES,), i32),
            pltpu.VMEM((TILES, LIST), i32),
            pltpu.VMEM((64, 128), i32),
            pltpu.SemaphoreType.DMA((3,)),
        ],
        in_specs=[HB] * 3,
        mib=60,
    )(tile_plan, tile_lists, requests.reshape(64, 128))
    came = exchange(asked, 1)
    turned = call(turn_kernel, shape(OWN, 128), "turn", in_specs=[VM])(
        jnp.pad(params, ((0, 64 - PARAM), (0, 0)))
    )
    lists = call(relist_kernel, shape(TILES, LIST, i32), "relist", in_specs=[VM, VM])(woven, rank)
    aims = jnp.pad(jnp.transpose(targets, (1, 0, 2)), ((0, 0), (0, 5), (0, 0)))
    indexes = [
        pltpu.SMEM((128, 128), i32),
        pltpu.SMEM((8, 512), i32),
        pltpu.SemaphoreType.DMA,
        pltpu.SemaphoreType.DMA,
    ]
    answers, slots, codes, places, beyond = call(
        answer_kernel,
        (
            shape(128 * LINES, 128),
            shape(64 * 64, 128),
            shape(64, 128, i32),
            shape(128, 128, i32),
            shape(8, 512, i32),
        ),
        "answer",
        scratch=[
            pltpu.VMEM((OWN, 128), f32),
            pltpu.VMEM((OWN, 128), f32),
            pltpu.VMEM((128 * LINES, 128), f32),
        ]
        + indexes[:2]
        + [pltpu.SemaphoreType.DMA((4,)), pltpu.SemaphoreType.DMA],
        in_specs=[VM] * 4,
        flops=4_500_000_000,
    )(came, turned, cos_yaw, sin_yaw)
    arrived = exchange(answers, LINES)
    wide = pltpu.VMEM((LIST, PIX), f32)
    narrow = pltpu.VMEM((LIST, 128), f32)
    returned = call(
        render_kernel,
        shape(128 * LINES, 128),
        "render",
        scratch=[
            pltpu.VMEM((672, 256), bf16),
            pltpu.VMEM((TILES, 256, LIST), bf16),
            pltpu.VMEM((288, 256), f32),
            narrow,
            narrow,
        ]
        + [pltpu.VMEM((16, LIST), f32)] * 2
        + ([wide] * 4 + [narrow, pltpu.VMEM((3 * LIST, 128), f32), pltpu.VMEM((24, PIX), f32)]) * 2,
        in_specs=[VM] * 3,
        flops=5_000_000_000,
    )(arrived, lists, aims)
    back = exchange(returned, LINES)
    return call(
        update_kernel,
        (shape(PARAM, OWN), shape(PARAM, OWN), shape(PARAM, OWN)),
        "update",
        scratch=[pltpu.VMEM((PARAM, OWN), f32)] * 3
        + [
            pltpu.SemaphoreType.DMA((3, 4)),
            pltpu.VMEM((128 * LINES, 128), f32),
            pltpu.VMEM((64 * 64, 128), f32),
            pltpu.VMEM((OWN, 128), f32),
            pltpu.VMEM((OWN, 128), f32),
        ]
        + [pltpu.VMEM((OWN + 8, 128), f32)] * 2
        + indexes,
        in_specs=[VM] * 10,
        out_specs=(HB, HB, HB),
        flops=4_500_000_000,
        mib=24,
    )(back, places, beyond, slots, codes, cos_yaw, sin_yaw, params, adam_first, adam_second)


def solution(mesh):
    placed = (
        P(None, AXES),
        P(None, AXES),
        P(None, AXES),
        P(),
        P(AXES),
        P(AXES, None),
        P(AXES, None),
        P(None, AXES, None),
    )
    return jax.shard_map(
        shards,
        mesh=mesh,
        in_specs=placed,
        out_specs=(P(None, AXES), P(None, AXES), P(None, AXES)),
        check_vma=False,
    )
```

```python
from functools import partial

import jax
import jax.numpy as jnp
from jax import lax
from jax.experimental import pallas as pl
from jax.experimental.pallas import tpu as pltpu
from jax.sharding import PartitionSpec as P

AXES = ("img", "blk")
STEP = 1000
TILES_ACROSS = 120
TILES_VIEW = 8160
TILE_EDGE = 16
PARAM = 59
OWN = 4096
SLOTS = 8192
TILES = 16
LIST = 256
PIX = 256
SENT = 9
LINES = 5

focal_px = 2400.0
camera_distance = 10.0
low_pass = 0.3
loss_scale = 16.0
beta_one = 0.9
beta_two = 0.999
adam_eps = 1e-08
log2_e = 1.4426950408889634
band_zero = 0.28209479177387814
band_one = 0.4886025119029199
band_two = (
    1.0925484305920792,
    -1.0925484305920792,
    0.31539156525252005,
    -1.0925484305920792,
    0.5462742152960396,
)
band_three = (
    -0.5900435899266435,
    2.890611442640554,
    -0.4570457994644658,
    0.3731763325901154,
    -0.4570457994644658,
    1.445305721320277,
    -0.5900435899266435,
)
f32 = jnp.float32
bf16 = jnp.bfloat16
i32 = jnp.int32
VM = pl.BlockSpec(memory_space=pltpu.VMEM)
SM = pl.BlockSpec(memory_space=pltpu.SMEM)
HB = pl.BlockSpec(memory_space=pltpu.HBM)


def iota(shape, dim):
    return lax.broadcasted_iota(i32, shape, dim)


def dot(a, b):
    return lax.dot_general(a, b, (((1,), (0,)), ((), ())), preferred_element_type=f32)


def dot_t(a, b):
    return lax.dot_general(a, b, (((1,), (1,)), ((), ())), preferred_element_type=f32)


def pieces(x, count):
    out = []
    for k in range(count):
        part = x.astype(bf16)
        out.append(part)
        if k + 1 < count:
            x = x - part.astype(f32)
    return out


def call(kernel, out_shape, name, scratch=(), in_specs=None, out_specs=None, flops=0, mib=16):
    return partial(
        pl.pallas_call,
        kernel,
        out_shape=out_shape,
        in_specs=in_specs,
        out_specs=out_specs or jax.tree.map(lambda _: VM, out_shape),
        scratch_shapes=list(scratch),
        name=name,
        cost_estimate=pl.CostEstimate(flops=flops, bytes_accessed=4 << 20, transcendentals=0),
        compiler_params=pltpu.CompilerParams(vmem_limit_bytes=mib << 20),
    )()


def harmonics(looking_x, look_y, look_z):
    square_x = looking_x * looking_x
    square_y = look_y * look_y
    square_z = look_z * look_z
    return [
        jnp.full_like(looking_x, band_zero),
        -band_one * look_y,
        band_one * look_z,
        -band_one * looking_x,
        band_two[0] * looking_x * look_y,
        band_two[1] * look_y * look_z,
        band_two[2] * (2.0 * square_z - square_x - square_y),
        band_two[3] * looking_x * look_z,
        band_two[4] * (square_x - square_y),
        band_three[0] * look_y * (3.0 * square_x - square_y),
        band_three[1] * looking_x * look_y * look_z,
        band_three[2] * look_y * (4.0 * square_z - square_x - square_y),
        band_three[3] * look_z * (2.0 * square_z - 3.0 * square_x - 3.0 * square_y),
        band_three[4] * looking_x * (4.0 * square_z - square_x - square_y),
        band_three[5] * look_z * (square_x - square_y),
        band_three[6] * looking_x * (square_x - 3.0 * square_y),
    ]


def project_slots(rows, cos_yaw, sin_yaw, centre_x, centre_y):
    world_x, world_y, world_z = rows[0], rows[1], rows[2]
    view_x = cos_yaw * world_x + sin_yaw * world_z
    view_z = cos_yaw * world_z - sin_yaw * world_x + camera_distance
    inverse_z = 1.0 / view_z
    mean_x = focal_px * view_x * inverse_z - centre_x
    mean_y = focal_px * world_y * inverse_z - centre_y
    scales = [jnp.exp(rows[3 + k]) for k in range(3)]
    norm = jnp.sqrt(
        rows[6] * rows[6] + rows[7] * rows[7] + rows[8] * rows[8] + rows[9] * rows[9]
    )
    inverse_norm = 1.0 / norm
    quat_w, quat_x, quat_y, quat_z = [rows[6 + k] * inverse_norm for k in range(4)]
    rotation = [
        [
            1.0 - 2.0 * (quat_y * quat_y + quat_z * quat_z),
            2.0 * (quat_x * quat_y - quat_w * quat_z),
            2.0 * (quat_x * quat_z + quat_w * quat_y),
        ],
        [
            2.0 * (quat_x * quat_y + quat_w * quat_z),
            1.0 - 2.0 * (quat_x * quat_x + quat_z * quat_z),
            2.0 * (quat_y * quat_z - quat_w * quat_x),
        ],
        [
            2.0 * (quat_x * quat_z - quat_w * quat_y),
            2.0 * (quat_y * quat_z + quat_w * quat_x),
            1.0 - 2.0 * (quat_x * quat_x + quat_y * quat_y),
        ],
    ]
    focal_z = focal_px * inverse_z
    shear_x = focal_z * view_x * inverse_z
    shear_y = focal_z * world_y * inverse_z
    jacob_ax = focal_z * cos_yaw + shear_x * sin_yaw
    jacob_az = focal_z * sin_yaw - shear_x * cos_yaw
    jacob_bx = shear_y * sin_yaw
    jacob_bz = -shear_y * cos_yaw
    row_a = [
        (jacob_ax * rotation[0][k] + jacob_az * rotation[2][k]) * scales[k] for k in range(3)
    ]
    row_b = [
        (jacob_bx * rotation[0][k] + focal_z * rotation[1][k] + jacob_bz * rotation[2][k])
        * scales[k]
        for k in range(3)
    ]
    covar_xx = row_a[0] * row_a[0] + row_a[1] * row_a[1] + row_a[2] * row_a[2] + low_pass
    covar_yy = row_b[0] * row_b[0] + row_b[1] * row_b[1] + row_b[2] * row_b[2] + low_pass
    covar_xy = row_a[0] * row_b[0] + row_a[1] * row_b[1] + row_a[2] * row_b[2]
    inverse_det = 1.0 / (covar_xx * covar_yy - covar_xy * covar_xy)
    conic_a = covar_yy * inverse_det
    conic_b = -covar_xy * inverse_det
    conic_c = covar_xx * inverse_det
    log_opacity = rows[10] - jnp.log(1.0 + jnp.exp(rows[10]))
    slope_x = conic_a * mean_x + conic_b * mean_y
    slope_y = conic_c * mean_y + conic_b * mean_x
    constant = log_opacity - 0.5 * (slope_x * mean_x + slope_y * mean_y)
    inverse_len = 1.0 / jnp.sqrt(view_x * view_x + world_y * world_y + view_z * view_z)
    basis = harmonics(
        (cos_yaw * view_x - sin_yaw * view_z) * inverse_len,
        world_y * inverse_len,
        (sin_yaw * view_x + cos_yaw * view_z) * inverse_len,
    )
    colors = []
    for channel in range(3):
        total = basis[0] * rows[11 + channel]
        for degree in range(1, 16):
            total = total + basis[degree] * rows[11 + 3 * degree + channel]
        colors.append(jnp.maximum(0.5 + total, 0.0))
    return [
        constant,
        slope_x,
        slope_y,
        -0.5 * conic_a,
        -conic_b,
        -0.5 * conic_c,
    ] + colors


def camera_of(codes, cos_ref, sin_ref):
    code = jnp.maximum(codes, 0).astype(f32)
    view = jnp.floor((code + 0.5) * (1.0 / TILES_VIEW))
    number = code - view * float(TILES_VIEW)
    across = jnp.floor((number + 0.5) * (1.0 / TILES_ACROSS))
    column = number - across * float(TILES_ACROSS)
    view = view.astype(i32)
    cos_yaw = jnp.take_along_axis(cos_ref[...], view, axis=1, mode="promise_in_bounds")
    sin_yaw = jnp.take_along_axis(sin_ref[...], view, axis=1, mode="promise_in_bounds")
    centre_x = column * 16.0 + (8.0 - 960.0)
    centre_y = across * 16.0 + (8.0 - 544.0)
    return cos_yaw, sin_yaw, centre_x, centre_y


def slot_parts(slot):
    line = jnp.right_shift(slot, 7)
    high = jnp.bitwise_and(line, 31)
    low = jnp.right_shift(line, 5) * 128 + jnp.bitwise_and(slot, 127)
    return high, low


def hot_rows(low, count=256):
    return (iota((count, low.shape[1]), 0) == low).astype(f32).astype(bf16)


def ask_kernel(plan_any, lists_any, req_any, out_ref, rank_ref, plan_ref, lists_ref, req_ref, sems):
    copies = [
        pltpu.make_async_copy(source, to, sems.at[k])
        for k, (source, to) in enumerate(
            ((lists_any, lists_ref), (plan_any, plan_ref), (req_any, req_ref))
        )
    ]
    for copy in copies:
        copy.start()
    copies[0].wait()
    tiles = jnp.zeros((64, 128), f32)
    for t in range(TILES):
        slot = lists_ref[t : t + 1, :]
        high, low = jnp.right_shift(slot, 7), jnp.bitwise_and(slot, 127)
        left = jnp.where(iota((64, LIST), 0) == high, float(t + 1), 0.0).astype(bf16)
        tiles = tiles + dot_t(left, hot_rows(low, 128))
    named = tiles > 0.0
    a, b = iota((128, 128), 0), iota((128, 128), 1)
    earlier = jnp.logical_and(a < b, jnp.right_shift(a, 6) == jnp.right_shift(b, 6))
    rank = dot(named.astype(f32).astype(bf16), earlier.astype(f32).astype(bf16))
    rank_ref[...] = rank
    gap = jnp.bitwise_and(iota((64, 128), 1), 63) - rank.astype(i32)
    copies[1].wait()
    copies[2].wait()
    held = req_ref[...] + tiles.astype(i32) * 4096 + gap * 131072
    held = jnp.where(named, held, 0)
    for k in range(6):
        ahead = pltpu.roll(held, 128 - (1 << k), 1)
        comes = jnp.bitwise_and(jnp.right_shift(ahead, 17 + k), 1) == 1
        stays = jnp.bitwise_and(jnp.right_shift(held, 17 + k), 1) == 0
        held = jnp.where(comes, ahead, jnp.where(stays, held, 0))
    asked = jnp.bitwise_and(held, 4095)
    tile = jnp.bitwise_and(jnp.right_shift(held, 12), 31)
    codes = jnp.full((64, 128), -1, i32)
    for t in range(TILES):
        codes = jnp.where(tile == t + 1, plan_ref[t], codes)
    first = iota((64, 128), 1) < 64
    out_ref[pl.ds(0, 64, stride=2), :] = jnp.where(first, asked, pltpu.roll(codes, 64, 1))
    out_ref[pl.ds(1, 64, stride=2), :] = jnp.where(first, pltpu.roll(asked, 64, 1), codes)


def relist_kernel(lists_ref, rank_ref, out_ref):
    rank = rank_ref[...]
    table = jnp.concatenate([rank[:32], rank[32:]], axis=1).astype(bf16)

    def tile(t, _):
        slot = lists_ref[pl.ds(t, 1), :]
        high, low = slot_parts(slot)
        found = jnp.where(iota((32, LIST), 0) == high, dot(table, hot_rows(low)), 0.0)
        place = jnp.sum(found, axis=0, keepdims=True).astype(i32)
        out_ref[pl.ds(t, 1), :] = slot - jnp.bitwise_and(slot, 63) + place
        return 0

    lax.fori_loop(0, TILES, tile, 0, unroll=4)


def turn_kernel(params_ref, out_ref):
    for h in range(16):
        block = params_ref[:, h * 256 : (h + 1) * 256]
        out_ref[h * 256 : (h + 1) * 256, :] = jnp.transpose(jnp.concatenate([block, block], axis=0))


FRONT = 32


def list_beyond(came, out_ref):
    lane = iota((128, 128), 1)
    used = jnp.where(jnp.logical_and(lane >= 64, came >= 0), 1.0, 0.0)
    count = jnp.broadcast_to(jnp.sum(used, axis=1, keepdims=True), (128, 128)).astype(i32)
    eights = jnp.right_shift(jnp.maximum(count - FRONT, 0) + 7, 3).astype(f32)
    upto = (lane <= iota((128, 128), 0)).astype(f32).astype(bf16)
    ends = dot(upto, eights.astype(bf16))
    for c in range(4):
        place = (iota((128, 128), 1) + c * 128).astype(f32)
        past = ends <= place
        asker = jnp.sum(jnp.where(past, 1.0, 0.0), axis=0, keepdims=True)
        begun = jnp.sum(jnp.where(past, eights, 0.0), axis=0, keepdims=True)
        slot = FRONT + 8.0 * (place[0:1] - begun)
        row = iota((8, 128), 0)
        lines = jnp.where(row == 0, asker, jnp.where(row == 1, slot, ends[127:128]))
        out_ref[:, c * 128 : (c + 1) * 128] = lines.astype(i32)


def by_groups(count, shift, body):
    size = 1 << shift
    groups = jnp.right_shift(count, shift)
    lax.fori_loop(0, groups, lambda k, _: body(k * size, size), None)
    lax.fori_loop(groups * size, count, lambda k, _: body(k, 1), None)


def answer_kernel(
    came_ref, turned_ref, cos_ref, sin_ref, out_ref, slots_ref, codes_ref, places_ref, beyond_ref,
    over, behind, values, index_s, beyond_s, index_sems, beyond_sem,
):
    index_copies = [
        pltpu.make_async_copy(came_ref.at[part], index_s.at[part], index_sems.at[k])
        for k, part in enumerate(pl.ds(32 * k, 32) for k in range(4))
    ]
    for copy in index_copies:
        copy.start()
    came = came_ref[...]
    list_beyond(came, beyond_ref)
    beyond_copy = pltpu.make_async_copy(beyond_ref, beyond_s, beyond_sem)
    beyond_copy.start()
    codes_ref[...] = jnp.transpose(came.astype(f32))[64:128].astype(i32)
    spare = OWN + jnp.bitwise_and(iota((128, 128), 1), 7)
    places_ref[...] = jnp.where(pltpu.roll(came, 64, 1) < 0, spare, came)

    def fetch(step, _):
        for k in range(2):
            p = 2 * step + k
            for j in range(FRONT):
                over[pl.ds(j * 128 + p, 1), :] = turned_ref[pl.ds(index_s[p, j], 1), :]
        behind[pl.ds(pl.multiple_of(step * 64, 64), 64), :] = jnp.ones((64, 128), f32)
        return 0

    for k, copy in enumerate(index_copies):
        copy.wait()
        lax.fori_loop(16 * k, 16 * k + 16, fetch, 0)
    beyond_copy.wait()

    def fetch_beyond(first_k, count):
        for k in range(count):
            p, slot = beyond_s[0, first_k + k], beyond_s[1, first_k + k]
            for j in range(8):
                row = turned_ref[pl.ds(index_s[p, slot + j], 1), :]
                behind[pl.ds((slot - FRONT + j) * 128 + p, 1), :] = row

    by_groups(beyond_s[2, 0], 1, fetch_beyond)
    first = iota((128, 128), 1) < 64

    def spread(step, _):
        for k in range(8):
            part = pl.ds(pl.multiple_of((step * 8 + k) * 128, 128), 128)
            over[part, :] = jnp.transpose(jnp.where(first, over[part, :], behind[part, :]))
        return 0

    lax.fori_loop(0, FRONT // 8, spread, 0)

    for r in range(PARAM, 64):
        for g in range(8):
            slots_ref[g * 512 + r * 8 : g * 512 + r * 8 + 8, :] = jnp.zeros((8, 128), f32)

    def work(g, _):
        at = pl.multiple_of(g * 8, 8)
        base = jnp.bitwise_and(g, 3) * 1024 + jnp.right_shift(g, 2) * 64
        rows = [over[pl.ds(base + r, 8, stride=128), :] for r in range(PARAM)]
        for r in range(PARAM):
            slots_ref[pl.ds(pl.multiple_of(g * 512 + r * 8, 8), 8), :] = rows[r]
        camera = camera_of(codes_ref[pl.ds(at, 8), :], cos_ref, sin_ref)
        for q, value in enumerate(project_slots(rows, *camera)):
            values[pl.ds(pl.multiple_of(q * 64 + at, 8), 8), :] = value
        return 0

    values[SENT * 64 :, :] = jnp.zeros((64, 128), f32)
    lax.fori_loop(0, 8, work, 0)
    for line in range(LINES):
        block = values[line * 128 : (line + 1) * 128, :]
        out_ref[pl.ds(line, 128, stride=LINES), :] = jnp.transpose(block)


def monomials(x, y, which):
    out = jnp.zeros(x.shape, f32)
    for k, value in enumerate((jnp.ones_like(x), x, y, x * x, x * y, y * y)):
        out = jnp.where(which == k, value, out)
    return out


def render_kernel(
    came_ref, lists_ref, targets_ref, out_ref,
    table, hots, back, coefs0, coefs1, spread0, spread1, *work_refs,
):
    coefs, spreads = (coefs0, coefs1), (spread0, spread1)
    first = iota((64, 128), 1) < 64
    for q in range(SENT):
        line = q // 2
        even = came_ref[pl.ds(line, 64, stride=10), :]
        odd = came_ref[pl.ds(5 + line, 64, stride=10), :]
        if q % 2 == 0:
            dense = jnp.where(first, even, pltpu.roll(odd, 64, 1))
        else:
            dense = jnp.where(first, pltpu.roll(even, 64, 1), odd)
        square = jnp.concatenate([dense[:32], dense[32:]], axis=1)
        for s, part in enumerate(pieces(square, 3 if q < 6 else 2)):
            table[pl.ds(s * 288 + q * 32, 32), :] = part
    back[...] = jnp.zeros_like(back)
    spread1[...] = jnp.zeros_like(spread1)
    works = (work_refs[:7], work_refs[7:])
    row = iota((32, PIX), 0)
    pix = iota((32, PIX), 1)
    basis = monomials(
        jnp.bitwise_and(pix, 15).astype(f32) - 7.5,
        jnp.right_shift(pix, 4).astype(f32) - 7.5,
        jnp.where(row < 24, jnp.bitwise_and(row, 7), 7),
    ).astype(bf16)
    sub = iota((8, PIX), 0)
    lane = iota((8, 128), 1)
    offset_x = jnp.bitwise_and(lane, 15).astype(f32) - 7.5
    offset_y = jnp.right_shift(lane, 4).astype(f32) - 3.5
    square_y = offset_y * offset_y + 16.0
    eight_y = offset_y * 8.0

    def make_hot(t, _):
        hots[t] = hot_rows(slot_parts(lists_ref[pl.ds(t, 1), :])[1])
        return 0

    lax.fori_loop(0, TILES, make_hot, 0, unroll=2)

    def here_of(t):
        return iota((32, LIST), 0) == slot_parts(lists_ref[pl.ds(t, 1), :])[0]

    def gather(t, to):
        found = dot(table[...], hots[t])
        here = here_of(t)
        values = []
        for q in range(SENT):
            at = q * 32
            value = found[at : at + 32] + (
                found[288 + at : 320 + at] + found[576 + at : 608 + at]
                if q < 6
                else found[288 + at : 320 + at]
            )
            values.append(jnp.sum(jnp.where(here, value, 0.0), axis=0, keepdims=True))
        shape_rows = jnp.zeros((8, LIST), f32)
        color_rows = jnp.zeros((8, LIST), f32)
        for q in range(6):
            shape_rows = jnp.where(sub == q, values[q], shape_rows)
        for q in range(3):
            color_rows = jnp.where(sub == q, values[6 + q], color_rows)
        parts = [p.astype(f32) for p in pieces(shape_rows * log2_e, 3)]
        stack = jnp.concatenate(parts + [color_rows] + [jnp.zeros((96, LIST), f32)], axis=0)
        to[...] = jnp.transpose(stack)

    def scatter(t, source):
        here = here_of(t)
        parts = [p.astype(f32) for p in pieces(source[...], 2)]
        left = []
        for s in range(2):
            for q in range(SENT):
                value = jnp.broadcast_to(parts[s][q : q + 1], (32, LIST))
                left.append(jnp.where(here, value, 0.0).astype(bf16))
        moved = dot_t(jnp.concatenate(left, axis=0), hots[t])
        back[...] += moved[0:288] + moved[288:576]

    def scan8(x, neutral, op, down):
        def shift(y, n):
            if down:
                return jnp.where(sub >= n, pltpu.roll(y, n, 0), neutral)
            return jnp.where(sub < 8 - n, pltpu.roll(y, 8 - n, 0), neutral)

        x = shift(x, 1)
        for n in (1, 2, 4):
            x = op(x, shift(x, n))
        return x

    def rows_of(v):
        return slice(v * 8, v * 8 + 8)

    def twice(x):
        return jnp.concatenate([x, x], axis=1)

    def expose(source, refs):
        refs[0][...] = dot(source[:, 0:32].astype(bf16), basis)

    def forward(v, source, refs, carry):
        ratios, weights, tones = refs[0], refs[1], refs[5]
        product, seen = carry
        alpha = jnp.exp2(ratios[rows_of(v)])
        keep = 1.0 - alpha
        ratios[rows_of(v)] = alpha / keep
        weight = alpha * product
        weights[rows_of(v)] = weight
        out = []
        for c in range(3):
            tone = jnp.broadcast_to(source[rows_of(v), 24 + c : 25 + c], (8, 128))
            tones[c * 256 + v * 8 : c * 256 + v * 8 + 8] = tone
            out.append(seen[c] + weight * twice(tone))
        return product * keep, out

    def compare(t, carry, refs):
        product, seen = carry
        ahead = scan8(product, 1.0, jnp.multiply, True)
        for c in range(3):
            total = jnp.sum(seen[c] * ahead, axis=0, keepdims=True)
            pull = (total - targets_ref[t, c : c + 1, :]) * (1.0 / loss_scale)
            refs[6][c * 8 : c * 8 + 8] = jnp.broadcast_to(pull, (8, PIX)) * ahead

    def pull_back(v, refs, pulls, rest):
        weights, gains, behind, sums, tones = refs[1:6]
        weight = weights[rows_of(v)]
        gain = jnp.zeros((8, PIX), f32)
        line = jnp.zeros((8, 128), f32)
        for c in range(3):
            gain = gain + pulls[c] * twice(tones[c * 256 + v * 8 : c * 256 + v * 8 + 8])
            tint = weight * pulls[c]
            tint = jnp.sum(tint[:, :128] + tint[:, 128:], axis=1, keepdims=True)
            line = jnp.where(lane == 6 + c, tint, line)
        gain = gain * weight
        gains[rows_of(v)] = gain
        behind[rows_of(v)] = rest
        sums[rows_of(v)] = line
        return rest + gain

    def moments(v, refs, after):
        ratios, gains, behind, sums = refs[0], refs[2], refs[3], refs[4]
        slope = gains[rows_of(v)] - (behind[rows_of(v)] + after) * ratios[rows_of(v)]
        upper, lower = slope[:, :128], slope[:, 128:]
        both, apart = upper + lower, lower - upper
        along = both * offset_x
        down = both * offset_y + apart * 4.0
        line = sums[rows_of(v)]
        for k, value in enumerate(
            (both, along, down, along * offset_x, down * offset_x,
             both * square_y + apart * eight_y)
        ):
            line = jnp.where(lane == k, jnp.sum(value, axis=1, keepdims=True), line)
        sums[rows_of(v)] = line

    nothing = jnp.zeros((8, PIX), f32)
    begin = (jnp.ones((8, PIX), f32), [nothing] * 3)
    gather(0, coefs[0])
    gather(1, coefs[1])
    expose(coefs[0], works[0])
    carry = begin
    for v in range(32):
        carry = forward(v, coefs[0], works[0], carry)
    compare(0, carry, works[0])

    def pair(step, _):
        for k in range(2):
            t = 2 * step + k
            coming = jnp.minimum(t + 1, TILES - 1)
            here, there = works[k], works[1 - k]
            expose(coefs[1 - k], there)
            scatter(jnp.maximum(t - 1, 0), spreads[1 - k])
            pulls = [here[6][c * 8 : c * 8 + 8] for c in range(3)]
            carry, rest = begin, nothing
            for v in range(32):
                carry = forward(v, coefs[1 - k], there, carry)
                rest = pull_back(31 - v, here, pulls, rest)
            after = scan8(rest, 0.0, jnp.add, False)
            for v in range(32):
                moments(v, here, after)
            gather(jnp.minimum(t + 2, TILES - 1), coefs[k])
            compare(coming, carry, there)
            spreads[k][...] = jnp.transpose(here[4][...])[0:16]
        return 0

    lax.fori_loop(0, TILES // 2, pair, 0)
    scatter(TILES - 1, spreads[1])

    zero = jnp.zeros((64, 128), f32)

    def dense_of(q):
        if q >= SENT:
            return zero
        square = back[pl.ds(q * 32, 32), :]
        return jnp.concatenate([square[:, :128], square[:, 128:]], axis=0)

    for line in range(LINES):
        a, b = dense_of(2 * line), dense_of(2 * line + 1)
        out_ref[pl.ds(line, 64, stride=10), :] = jnp.where(first, a, pltpu.roll(b, 64, 1))
        out_ref[pl.ds(5 + line, 64, stride=10), :] = jnp.where(first, pltpu.roll(a, 64, 1), b)


def rates(shape):
    row = iota(shape, 0)
    out = jnp.full(shape, 0.000125, f32)
    for end, rate in ((14, 0.0025), (11, 0.05), (10, 0.001), (6, 0.005), (3, 0.0008)):
        out = jnp.where(row < end, rate, out)
    return out


def update_kernel(
    back_ref, places_ref, beyond_ref, slots_ref, codes_ref, cos_ref, sin_ref,
    params_ref, first_ref, second_ref, new_params_any, new_first_any, new_second_any,
    new_params_ref, new_first_ref, new_second_ref, out_sems,
    cots, grads, over, behind, even, odd, index_s, beyond_s, index_sem, beyond_sem,
):
    index_copy = pltpu.make_async_copy(places_ref, index_s, index_sem)
    beyond_copy = pltpu.make_async_copy(beyond_ref, beyond_s, beyond_sem)
    index_copy.start()
    beyond_copy.start()
    for line in range(LINES):
        block = back_ref[pl.ds(line, 128, stride=LINES), :]
        cots[line * 128 : (line + 1) * 128, :] = jnp.transpose(block)
    for r in range(PARAM, 64):
        for g in range(8):
            grads[g * 512 + r * 8 : g * 512 + r * 8 + 8, :] = jnp.zeros((8, 128), f32)

    def work(g, _):
        at = pl.multiple_of(g * 8, 8)
        lines = [pl.ds(pl.multiple_of(g * 512 + r * 8, 8), 8) for r in range(PARAM)]
        camera = camera_of(codes_ref[pl.ds(at, 8), :], cos_ref, sin_ref)
        _, pullback = jax.vjp(
            lambda r: project_slots(r, *camera), [slots_ref[line, :] for line in lines]
        )
        (out,) = pullback(
            [cots[pl.ds(pl.multiple_of(q * 64 + at, 8), 8), :] for q in range(SENT)]
        )
        for r in range(PARAM):
            grads[lines[r], :] = out[r]
        return 0

    lax.fori_loop(0, 8, work, 0)

    first = iota((128, 128), 1) < 64

    def spread(g, _):
        for k in range(8):
            block = [
                grads[pl.ds((g + half) * 512 + k + m * 64, 8, stride=8), :]
                for half in (0, 4)
                for m in range(8)
            ]
            at = pl.ds(pl.multiple_of((g * 8 + k) * 128, 128), 128)
            turned = jnp.transpose(jnp.concatenate(block, axis=0))
            over[at, :] = jnp.where(first, turned, 0.0)
            behind[at, :] = jnp.where(first, 0.0, turned)
            for sums in (even, odd):
                sums[at, :] = jnp.zeros((128, 128), f32)
        return 0

    lax.fori_loop(0, FRONT // 8, spread, 0)
    index_copy.wait()
    beyond_copy.wait()

    def add_eight(sums, source, p, slot, line):
        at = [pl.ds(index_s[p, slot + n], 1) for n in range(8)]
        new = [sums[at[n], :] + source[pl.ds((line + n) * 128 + p, 1), :] for n in range(8)]
        for n in range(8):
            sums[at[n], :] = new[n]

    def gather(step, _):
        for j in range(0, FRONT, 8):
            for k in range(4):
                add_eight((even, odd)[k % 2], over, 4 * step + k, j, j)
        return 0

    lax.fori_loop(0, 32, gather, 0)

    def gather_beyond(first_k, count):
        for k in range(count):
            p, slot = beyond_s[0, first_k + k], beyond_s[1, first_k + k]
            add_eight((even, odd)[k % 2], behind, p, slot, slot - FRONT)

    by_groups(beyond_s[2, 0], 2, gather_beyond)
    bias_one = 1.0 - beta_one**STEP
    bias_two = 1.0 - beta_two**STEP
    rate = rates((PARAM, 256)) * (1.0 / bias_one)
    pending = []
    for h in range(16):
        cols = slice(h * 256, (h + 1) * 256)
        both = jnp.transpose(even[cols, :] + odd[cols, :])
        gradient = both[:PARAM] + both[64 : 64 + PARAM]
        first_new = beta_one * first_ref[:, cols] + (1.0 - beta_one) * gradient
        second_new = beta_two * second_ref[:, cols] + (1.0 - beta_two) * gradient * gradient
        new_first_ref[:, cols] = first_new
        new_second_ref[:, cols] = second_new
        scaled = second_new * (1.0 / bias_two)
        new_params_ref[:, cols] = params_ref[:, cols] - rate * first_new / (
            scaled * lax.rsqrt(scaled) + adam_eps
        )
        if h % 4 == 3:
            done = pl.ds((h - 3) * 256, 1024)
            for k, (near, far) in enumerate(
                (
                    (new_params_ref, new_params_any),
                    (new_first_ref, new_first_any),
                    (new_second_ref, new_second_any),
                )
            ):
                sem = out_sems.at[k, h // 4]
                pending.append(pltpu.make_async_copy(near.at[:, done], far.at[:, done], sem))
                pending[-1].start()
    for copy in pending:
        copy.wait()


def shape(rows, cols, dtype=f32):
    return jax.ShapeDtypeStruct((rows, cols), dtype)


def exchange(lines, count):
    sent = lines.reshape(128, 1, count * 128)
    came = lax.all_to_all(sent, AXES, split_axis=0, concat_axis=0, tiled=True)
    return came.reshape(128 * count, 128)


def shards(params, adam_first, adam_second, view_yaw, tile_plan, tile_lists, requests, targets):
    cos_yaw = jnp.broadcast_to(jnp.pad(jnp.cos(view_yaw), (0, 96))[None, :], (8, 128))
    sin_yaw = jnp.broadcast_to(jnp.pad(jnp.sin(view_yaw), (0, 96))[None, :], (8, 128))
    woven = jnp.transpose(tile_lists.reshape(TILES, 8, 32), (0, 2, 1)).reshape(TILES, LIST)
    asked, rank = call(
        ask_kernel,
        (shape(128, 128, i32), shape(64, 128)),
        "ask",
        scratch=[
            pltpu.SMEM((TILES,), i32),
            pltpu.VMEM((TILES, LIST), i32),
            pltpu.VMEM((64, 128), i32),
            pltpu.SemaphoreType.DMA((3,)),
        ],
        in_specs=[HB] * 3,
        mib=60,
    )(tile_plan, tile_lists, requests.reshape(64, 128))
    came = exchange(asked, 1)
    turned = call(turn_kernel, shape(OWN, 128), "turn", in_specs=[VM])(
        jnp.pad(params, ((0, 64 - PARAM), (0, 0)))
    )
    lists = call(relist_kernel, shape(TILES, LIST, i32), "relist", in_specs=[VM, VM])(woven, rank)
    aims = jnp.pad(jnp.transpose(targets, (1, 0, 2)), ((0, 0), (0, 5), (0, 0)))
    indexes = [
        pltpu.SMEM((128, 128), i32),
        pltpu.SMEM((8, 512), i32),
        pltpu.SemaphoreType.DMA,
        pltpu.SemaphoreType.DMA,
    ]
    answers, slots, codes, places, beyond = call(
        answer_kernel,
        (
            shape(128 * LINES, 128),
            shape(64 * 64, 128),
            shape(64, 128, i32),
            shape(128, 128, i32),
            shape(8, 512, i32),
        ),
        "answer",
        scratch=[
            pltpu.VMEM((OWN, 128), f32),
            pltpu.VMEM((OWN, 128), f32),
            pltpu.VMEM((128 * LINES, 128), f32),
        ]
        + indexes[:2]
        + [pltpu.SemaphoreType.DMA((4,)), pltpu.SemaphoreType.DMA],
        in_specs=[VM] * 4,
        flops=4_500_000_000,
    )(came, turned, cos_yaw, sin_yaw)
    arrived = exchange(answers, LINES)
    wide = pltpu.VMEM((LIST, PIX), f32)
    narrow = pltpu.VMEM((LIST, 128), f32)
    returned = call(
        render_kernel,
        shape(128 * LINES, 128),
        "render",
        scratch=[
            pltpu.VMEM((768, 256), bf16),
            pltpu.VMEM((TILES, 256, LIST), bf16),
            pltpu.VMEM((288, 256), f32),
            narrow,
            narrow,
        ]
        + [pltpu.VMEM((16, LIST), f32)] * 2
        + ([wide] * 4 + [narrow, pltpu.VMEM((3 * LIST, 128), f32), pltpu.VMEM((24, PIX), f32)]) * 2,
        in_specs=[VM] * 3,
        flops=5_000_000_000,
    )(arrived, lists, aims)
    back = exchange(returned, LINES)
    return call(
        update_kernel,
        (shape(PARAM, OWN), shape(PARAM, OWN), shape(PARAM, OWN)),
        "update",
        scratch=[pltpu.VMEM((PARAM, OWN), f32)] * 3
        + [
            pltpu.SemaphoreType.DMA((3, 4)),
            pltpu.VMEM((128 * LINES, 128), f32),
            pltpu.VMEM((64 * 64, 128), f32),
            pltpu.VMEM((OWN, 128), f32),
            pltpu.VMEM((OWN, 128), f32),
        ]
        + [pltpu.VMEM((OWN + 8, 128), f32)] * 2
        + indexes,
        in_specs=[VM] * 10,
        out_specs=(HB, HB, HB),
        flops=4_500_000_000,
        mib=24,
    )(back, places, beyond, slots, codes, cos_yaw, sin_yaw, params, adam_first, adam_second)


def solution(mesh):
    placed = (
        P(None, AXES),
        P(None, AXES),
        P(None, AXES),
        P(),
        P(AXES),
        P(AXES, None),
        P(AXES, None),
        P(None, AXES, None),
    )
    return jax.shard_map(
        shards,
        mesh=mesh,
        in_specs=placed,
        out_specs=(P(None, AXES), P(None, AXES), P(None, AXES)),
        check_vma=False,
    )
```
